256 devices in a mesh: gx: 8 (over y, core), gy: 16 (over z_lo, x), ka: 2 (over z_hi).
Axes of the slice: x: 4, y: 4, z: 8 (z_hi: 2, z_lo: 4; z = z_hi * 4 + z_lo), core: 2. Of those that a mesh axis runs over, the one named last changes fastest.
Arguments:
- mask_param: float32 [24576, 2048], P('gy', 'gx'), may hold values from -6 to 6
- target: int32 [24576, 2048], P('gy', 'gx'), may hold values 0 or 1
- kernels: float32 [12, 2, 4096], P('ka'), may hold values from -4 to 4
- weights: float32 [12], P('ka'), may hold values from 0.05 to 0.3
Outputs:
- mask_gradient: float32 [24576, 2048], P('gy', 'gx')
- resist_image: float32 [24576, 2048], P('gy', 'gx')
The draws below stay inside these ranges and needn't reach their ends.
All inputs are finite; a program needn't handle non-finite values. No bound on the sum of `target` on one device may be relied on, other than what follows from the above.
Results may differ from the reference program's by a relative error of at most 0.0003.
Values sent between devices are 32-bit elements; how exact they have to be, the bound alone decides.
No kernel may reach another device: no remote copies, remote signals or barrier semaphores. Data moves between devices by JAX's collectives and lax.ppermute only.
A program may use at most 128 MiB of HBM per device.

```python
import math
import jax
import jax.numpy as jnp
from jax import lax

WIN = 512
HALO = 128
FB = 64
KERN = 12
TILE = 256
NY = 24576
NX = 2048


def set_ends(result, own_key, smallest, top_value):
    place = [jax.random.randint(jax.random.fold_in(own_key, axis), (), 0, length) for axis, length in enumerate(result.shape)]
    longest = result.shape.index(max(result.shape))
    next_to = place[:longest] + [(place[longest] + 1) % result.shape[longest]] + place[longest + 1:]
    return result.at[tuple(place)].set(smallest).at[tuple(next_to)].set(top_value)


def steps_of(own_key, dims, shards, low, top_value):
    factor_of, own = 1.0, jax.random.fold_in(own_key, 6)
    for axis_at, blocks in shards:
        heights = jnp.exp(jax.random.uniform(jax.random.fold_in(own, axis_at), (blocks,), jnp.float32, low / len(shards), top_value / len(shards)))
        factor_of = factor_of * jnp.repeat(heights, dims[axis_at] // blocks).reshape([-1 if axis == axis_at else 1 for axis in range(len(dims))])
    return factor_of


def bell_draw(rng, dims, spread, bound, cuts=(), kind=jnp.bfloat16):
    factor_of = steps_of(rng, dims, cuts, -0.22, 0.18) if cuts else 1.0
    array = jax.random.normal(rng, dims, jnp.float32) * spread * factor_of
    return jnp.minimum(jnp.maximum(array, -bound), bound).astype(kind)


def setup_inputs(seed: int = 0) -> dict:
    splits = jax.random.split(jax.random.key(seed), 5)
    return {
        "mask_param": bell_draw(splits[0], (NY, NX), 1.5, 6.0, ((0, 16), (1, 8)), jnp.float32),
        "target": set_ends((jax.random.randint(splits[1], (NY, NX), 0, 2) < 1).astype(jnp.int32), jax.random.fold_in(splits[1], 1), 0, 1),
        "kernels": bell_draw(splits[2], (KERN, 2, FB * FB), 0.7, 4.0, ((0, 2),), jnp.float32),
        "weights": jnp.clip(jnp.exp(math.log(0.3) - 1.7917595 * jax.random.uniform(splits[3], (KERN,), jnp.float32) ** steps_of(splits[3], (KERN,), ((0, 2),), -0.2, 0.2)), 0.05, 0.3),
    }


steepness = 4.0
threshold = 1.0
highest = lax.Precision.HIGHEST

def contract(form, left, right):
    return jnp.einsum(form, left, right, precision=highest)

def phase_tables(points, offset, band_size, period):
    frequencies = jnp.arange(band_size, dtype=jnp.int32) - band_size // 2
    places = jnp.arange(points, dtype=jnp.int32) + offset
    windings = jnp.mod(frequencies[:, None] * places[None, :], period)
    angles = windings.astype(jnp.float32) * (2.0 * math.pi / period)
    return (jnp.cos(angles), jnp.sin(angles))

def tile_penalty(window, target_tile, kern_real, kern_imag, weights, tables):
    cos_win, sin_win, cos_tile, sin_tile = tables
    factor = 1.0 / (WIN * FB)
    rows_real = contract('fx,xy->fy', cos_win, window)
    rows_imag = -contract('fx,xy->fy', sin_win, window)
    spec_real = factor * (contract('fy,gy->fg', rows_real, cos_win) + contract('fy,gy->fg', rows_imag, sin_win))
    spec_imag = factor * (contract('fy,gy->fg', rows_imag, cos_win) - contract('fy,gy->fg', rows_real, sin_win))
    prod_real = kern_real * spec_real - kern_imag * spec_imag
    prod_imag = kern_real * spec_imag + kern_imag * spec_real
    half_real = contract('kfg,gq->kfq', prod_real, cos_tile) - contract('kfg,gq->kfq', prod_imag, sin_tile)
    half_imag = contract('kfg,gq->kfq', prod_real, sin_tile) + contract('kfg,gq->kfq', prod_imag, cos_tile)
    field_real = contract('fp,kfq->kpq', cos_tile, half_real) - contract('fp,kfq->kpq', sin_tile, half_imag)
    field_imag = contract('fp,kfq->kpq', sin_tile, half_real) + contract('fp,kfq->kpq', cos_tile, half_imag)
    intensity = contract('k,kpq->pq', weights, field_real * field_real + field_imag * field_imag)
    resist = jax.nn.sigmoid(steepness * (intensity - threshold))
    misfit = resist - target_tile
    return (jnp.sum(misfit * misfit), resist)

def reference(mask_param, target, kernels, weights):
    transmit = jnp.tanh(mask_param)
    padded = jnp.pad(transmit, HALO)
    target_float = target.astype(jnp.float32)
    kern_real = kernels[:, 0].reshape(KERN, FB, FB)
    kern_imag = kernels[:, 1].reshape(KERN, FB, FB)
    cos_win, sin_win = phase_tables(WIN, 0, FB, WIN)
    cos_tile, sin_tile = phase_tables(TILE, HALO, FB, WIN)
    tables = (cos_win, sin_win, cos_tile, sin_tile)
    tile_rows = NY // TILE
    tile_cols = NX // TILE

    def visit_tile(accumulated, number):
        row_start = number // tile_cols * TILE
        col_start = number % tile_cols * TILE
        window = lax.dynamic_slice(padded, (row_start, col_start), (WIN, WIN))
        target_tile = lax.dynamic_slice(target_float, (row_start, col_start), (TILE, TILE))

        def penalty_of(block_in):
            return tile_penalty(block_in, target_tile, kern_real, kern_imag, weights, tables)
        penalty, backward, resist = jax.vjp(penalty_of, window, has_aux=True)
        window_grad, = backward(jnp.ones_like(penalty))
        current = lax.dynamic_slice(accumulated, (row_start, col_start), (WIN, WIN))
        accumulated = lax.dynamic_update_slice(accumulated, current + window_grad, (row_start, col_start))
        return (accumulated, resist)
    numbers = jnp.arange(tile_rows * tile_cols, dtype=jnp.int32)
    accumulated, resists = lax.scan(visit_tile, jnp.zeros(padded.shape, jnp.float32), numbers)
    gradient = accumulated[HALO:HALO + NY, HALO:HALO + NX] * (1.0 - transmit * transmit)
    resist_image = resists.reshape(tile_rows, tile_cols, TILE, TILE).transpose(0, 2, 1, 3).reshape(NY, NX)
    return (gradient, resist_image)
```

```python
import math

import jax
import jax.numpy as jnp
import ml_dtypes
import numpy as np
from jax import lax
from jax.experimental import pallas as pl
from jax.experimental.pallas import tpu as pltpu
from jax.sharding import PartitionSpec as P

WIN = 512
HALO = 128
FB = 64
TILE = 256
COARSE = 128
HALF = COARSE // 2
VMEM_LIMIT = 48 * 1024 * 1024

bf16 = ml_dtypes.bfloat16


def halves(table):
    high = table.astype(np.float32).astype(bf16)
    low = (table - high.astype(np.float64)).astype(np.float32).astype(bf16)
    return high, low


def as_left(table):
    high, low = halves(table)
    return np.concatenate([high, low, high], axis=1)


def as_right(table):
    high, low = halves(table)
    return np.concatenate([high, high, low], axis=0)


def angles(points):
    frequencies = np.arange(FB) - FB // 2
    windings = np.mod(frequencies[:, None] * np.asarray(points)[None, :], WIN)
    return windings * (2.0 * math.pi / WIN)


ORDER = np.concatenate([np.arange(0, FB, 2), np.arange(1, FB, 2)])


def blocks(table):
    return [table[:, i : i + 128] for i in range(0, table.shape[1], 128)]


def make_tables():
    factor = 1.0 / (WIN * FB)
    pixels = np.arange(HALO)
    columns, rows, outs, pixs = [], [], [], []
    for points in (pixels + 3 * HALO, pixels):
        cos, sin = np.cos(angles(points)), np.sin(angles(points))
        columns.append(as_right(np.concatenate([cos.T, -sin.T], axis=1)))
        pixs.append(as_right(np.concatenate([cos, -sin], axis=0)))
        cos, sin = cos[ORDER], sin[ORDER]
        rows += blocks(as_left(factor * np.concatenate([cos, sin], axis=0)))
        outs += blocks(as_left(factor * np.concatenate([cos.T, sin.T], axis=1)))
    plus = 4 * np.arange(HALF) + 2
    samples = np.concatenate([plus, -plus])
    cos, sin = np.cos(angles(samples)), np.sin(angles(samples))
    spread = as_right(
        np.concatenate(
            [np.concatenate([cos, sin], axis=1), np.concatenate([-sin, cos], axis=1)], axis=0
        )
    )
    gather = np.concatenate(
        [np.concatenate([cos.T, -sin.T], axis=1), np.concatenate([sin.T, cos.T], axis=1)], axis=0
    )
    gather = np.concatenate(halves(gather), axis=1)
    cos, sin = np.cos(angles(plus))[ORDER], np.sin(angles(plus))[ORDER]
    lift = as_left(np.concatenate([cos.T, sin.T], axis=0))
    lift = np.concatenate([lift, np.zeros((COARSE, 64), bf16)], axis=1)
    high, low = halves(np.concatenate([cos, sin], axis=1))
    fold = np.concatenate(
        [np.concatenate([high, high], axis=1), np.concatenate([low, 0 * low], axis=1)], axis=0
    )
    offset = (np.arange(TILE) + HALO)[:, None] - samples[None, :]
    orders = np.arange(1, COARSE // 2)
    turns = np.mod(offset[..., None] * orders, WIN) * (2.0 * math.pi / WIN)
    interp = (1.0 + 2.0 * np.cos(turns).sum(-1)) / COARSE
    high, low = halves(interp)
    fine_left = np.concatenate(
        [np.concatenate([high, high], axis=1), np.concatenate([low, 0 * low], axis=1)], axis=0
    )
    coarse_left = np.concatenate(halves(interp.T), axis=0)
    coarse_right = np.concatenate(halves(interp), axis=1)
    return {
        "analysis": np.concatenate(columns + rows, axis=0),
        "synthesis": np.concatenate(pixs + outs, axis=0),
        "imaging": np.concatenate(
            [spread, gather, lift, fold, as_right(interp.T), fine_left, coarse_left, coarse_right],
            axis=0,
        ),
    }


TABLES = make_tables()
SPREAD, GATHER, LIFT, FOLD, FINE_RIGHT, FINE_LEFT, COARSE_LEFT, COARSE_RIGHT = (
    slice(a, b)
    for a, b in (
        (0, 384), (384, 640), (640, 768), (768, 896), (896, 1280), (1280, 1792), (1792, 2048),
        (2048, 2304),
    )
)


def split(value):
    high = value.astype(jnp.bfloat16)
    low = (value - high.astype(jnp.float32)).astype(jnp.bfloat16)
    return high, low


def dot(left, right):
    return jnp.dot(left, right, preferred_element_type=jnp.float32)


def times_table(value, table):
    high, low = split(value)
    return dot(jnp.concatenate([high, low, high], axis=1), table)


def table_times(table, value):
    high, low = split(value)
    return dot(table, jnp.concatenate([high, high, low], axis=0))


def stacked_times(table, value):
    high, low = split(value)
    found = dot(table, jnp.concatenate([high, low], axis=0))
    size = found.shape[0] // 2
    return found[:size] + found[size:]


def times_paired(value, table):
    high, low = split(value)
    width = table.shape[1] // 2
    first = dot(high, table)
    return first[:, :width] + (first[:, width:] + dot(low, table[:, :width]))


def col_table(packed, index):
    return packed[index * 384 : (index + 1) * 384, :]


def row_table(packed, index):
    start = 768 + index * 384
    return jnp.concatenate(
        [packed[start + i : start + i + 128, :] for i in (0, 128, 256)], axis=1
    )


def parity(shape):
    index = lax.broadcasted_iota(jnp.int32, shape, 1)
    return (1 - 2 * (index % 2)).astype(jnp.float32)


def row_parity(shape):
    index = lax.broadcasted_iota(jnp.int32, shape, 0)
    return jnp.where(index < FB // 2, 1.0, -1.0)


def low_lanes(shape):
    return lax.broadcasted_iota(jnp.int32, shape, 1) < FB


def swapped(value):
    return pltpu.roll(value, FB, 1)


def preparation_kernel(roots, own, other, straight, crossed, real, imag):
    count = own.shape[0]
    lanes = low_lanes((FB // 2, 2 * FB))
    for group, source in enumerate((own, other)):
        for index in range(count):
            for row in range(FB // 2):
                place = slice(row * 2 * FB, (row + 1) * 2 * FB)
                real[row : row + 1, :] = source[index, 0:1, place]
                imag[row : row + 1, :] = source[index, 1:2, place]
            root = roots[group, index]
            re, im = root * real[...], root * imag[...]
            re_turned, im_turned = swapped(re), swapped(im)
            at = group * count + index
            straight[at, : FB // 2] = jnp.where(lanes, re, re_turned)
            straight[at, FB // 2 :] = jnp.where(lanes, re_turned, re)
            crossed[at, : FB // 2] = jnp.where(lanes, -im, im_turned)
            crossed[at, FB // 2 :] = jnp.where(lanes, -im_turned, im)


def analysis_kernel(mask, above, below, tables, left, right, slope, total):
    step = pl.program_id(0)
    count = left.shape[0]
    sign = jnp.where(low_lanes((FB, 2 * FB)), 1.0, -1.0)
    flip = row_parity((FB, 4 * FB))

    def spectra(transmit):
        high, low = split(transmit)
        rows = []
        for side in (0, 1):
            lanes = slice(side * HALO, (side + 1) * HALO)
            three = jnp.concatenate([high[:, lanes], low[:, lanes], high[:, lanes]], axis=1)
            rows.append(dot(three, col_table(tables, side)))
        rows = jnp.concatenate(rows, axis=1)
        found = []
        for part in (0, 1):
            both = table_times(row_table(tables, part), rows[part * HALO : (part + 1) * HALO])
            sine = both[FB:]
            turned = [sign * swapped(sine[:, : 2 * FB]), sign * swapped(sine[:, 2 * FB :])]
            found.append(both[:FB] + jnp.concatenate(turned, axis=1))
        return found

    @pl.when(step == 0)
    def _():
        outer = jnp.concatenate([below[...], above[...]], axis=0)
        upper, lower = spectra(jnp.tanh(outer))
        total[...] = jnp.zeros_like(total)
        total[1] = lower
        total[count] = upper

    transmit = jnp.tanh(mask[...])
    slope[...] = 1.0 - transmit * transmit
    upper, lower = spectra(transmit)
    total[step] += upper
    total[step + 1] += flip * (upper + lower)
    total[step + 2] += lower

    @pl.when(step == count - 1)
    def _():
        left[...] = total[1 : count + 1, :, : 2 * FB]
        right[...] = total[1 : count + 1, :, 2 * FB :]


def imaging_kernel(
    left, right, from_left, from_right, straight, crossed, target, wide,
    resist_ref, grad, fields, intensity, weight, adjoint, sides,
):
    count = straight.shape[0] // 2
    flip = parity((FB, 2 * FB))
    spectrum = flip * (left[0] + right[0]) + from_left[0] + from_right[0]
    turned = swapped(spectrum)

    def forward(group, carry):
        first = group * count
        products = [
            straight[first + i] * spectrum + crossed[first + i] * turned for i in range(count)
        ]
        rows = times_table(jnp.concatenate(products, axis=0), wide[SPREAD, :])
        total = jnp.zeros((COARSE, COARSE), jnp.float32)
        for i in range(count):
            both = table_times(wide[LIFT, :192], rows[i * FB : (i + 1) * FB])
            cosine, sine = both[:HALF], both[HALF:]
            sine_re, sine_im = sine[:, :COARSE], sine[:, COARSE:]
            cosine_re, cosine_im = cosine[:, :COARSE], cosine[:, COARSE:]
            real = jnp.concatenate([cosine_re - sine_im, cosine_re + sine_im], axis=0)
            imag = jnp.concatenate([cosine_im + sine_re, cosine_im - sine_re], axis=0)
            fields[first + i, :, :COARSE] = real
            fields[first + i, :, COARSE:] = imag
            total = total + (real * real + imag * imag)
        intensity[group] = total
        return carry

    lax.fori_loop(0, 2, forward, 0)

    half_fine = times_table(intensity[0] + intensity[1], wide[FINE_RIGHT, :])
    fine = stacked_times(wide[FINE_LEFT, :], half_fine)
    resist = jax.nn.sigmoid(4.0 * (fine - 1.0))
    resist_ref[...] = resist
    misfit = resist - target[...].astype(jnp.float32)
    push = 16.0 * misfit * resist * (1.0 - resist)
    high, low = split(push)
    from_high = dot(wide[COARSE_LEFT, :], high)
    half_coarse = from_high[:COARSE] + (
        from_high[COARSE:] + dot(wide[COARSE_LEFT, :][:COARSE], low)
    )
    weight[...] = times_paired(half_coarse, wide[COARSE_RIGHT, :])

    sign = jnp.where(low_lanes((HALF, 2 * FB)), 1.0, -1.0)

    def backward(group, carry):
        first = group * count
        scale = jnp.concatenate([weight[...], weight[...]], axis=1)
        scaled = jnp.concatenate([fields[first + i] * scale for i in range(count)], axis=0)
        sides[...] = times_paired(scaled, wide[GATHER, :])
        total = jnp.zeros((FB, 2 * FB), jnp.float32)
        for i in range(0, count, 2):
            pair = []
            for j in (i, i + 1):
                plus = sides[j * COARSE : j * COARSE + HALF, :]
                minus = sides[j * COARSE + HALF : (j + 1) * COARSE, :]
                pair.append(
                    jnp.concatenate([plus + minus, sign * swapped(plus - minus)], axis=0)
                )
            found = stacked_times(wide[FOLD, :], jnp.concatenate(pair, axis=1))
            for j in (0, 1):
                part = found[:, j * 2 * FB : (j + 1) * 2 * FB]
                total = total + (
                    straight[first + i + j] * part - crossed[first + i + j] * swapped(part)
                )
        adjoint[group] = total
        return carry

    lax.fori_loop(0, 2, backward, 0)
    grad[0] = adjoint[0] + adjoint[1]


def synthesis_kernel(own, from_left, from_right, above, below, slope, tables, result, mixed):
    step = pl.program_id(0)
    count = own.shape[0]
    flip_col = parity((FB, 2 * FB))
    flip_row = row_parity((FB, 4 * FB))
    sign = jnp.where(low_lanes((FB, 2 * FB)), -1.0, 1.0)

    @pl.when(step == 0)
    def _():
        mixed[0] = above[...]
        mixed[count + 1] = below[...]
        for index in range(count):
            base = flip_col * own[index]
            mixed[index + 1, :, : 2 * FB] = base + from_left[index]
            mixed[index + 1, :, 2 * FB :] = base + from_right[index]

    base = flip_row * mixed[step + 1]
    rows = []
    for near, part in ((step, 0), (step + 2, 1)):
        block = base + mixed[near]
        turned = [sign * swapped(block[:, : 2 * FB]), sign * swapped(block[:, 2 * FB :])]
        stacked = jnp.concatenate([block, jnp.concatenate(turned, axis=1)], axis=0)
        rows.append(table_times(row_table(tables, part), stacked))
    high, low = split(jnp.concatenate(rows, axis=0))
    sides = []
    for side in (0, 1):
        lanes = slice(side * 2 * FB, (side + 1) * 2 * FB)
        three = jnp.concatenate([high[:, lanes], low[:, lanes], high[:, lanes]], axis=1)
        sides.append(dot(three, col_table(tables, side)))
    result[...] = jnp.concatenate(sides, axis=1) * slope[...]


def whole(array):
    zeros = (0,) * len(array.shape)
    return pl.BlockSpec(array.shape, lambda step: zeros)


def tile_rows():
    return pl.BlockSpec((TILE, TILE), lambda step: (step, 0))


def spectra_of_tile():
    return pl.BlockSpec((1, FB, 2 * FB), lambda step: (step, 0, 0))


def params():
    return pltpu.CompilerParams(
        dimension_semantics=("arbitrary",), vmem_limit_bytes=VMEM_LIMIT
    )


def preparation(roots, own, other):
    shape = jax.ShapeDtypeStruct((2 * own.shape[0], FB, 2 * FB), jnp.float32)
    part = pltpu.VMEM((FB // 2, 2 * FB), jnp.float32)
    return pl.pallas_call(
        preparation_kernel,
        out_shape=(shape, shape),
        in_specs=[pl.BlockSpec(memory_space=pltpu.SMEM)]
        + [pl.BlockSpec(memory_space=pltpu.VMEM)] * 2,
        out_specs=[pl.BlockSpec(memory_space=pltpu.VMEM)] * 2,
        scratch_shapes=[part, part],
        compiler_params=pltpu.CompilerParams(vmem_limit_bytes=VMEM_LIMIT),
        cost_estimate=pl.CostEstimate(flops=400000, bytes_accessed=1600000, transcendentals=0),
        name="preparation",
    )(roots, own, other)


def analysis(mask, above, below):
    tiles = mask.shape[0] // TILE
    tables = jnp.asarray(TABLES["analysis"])
    spectra = jax.ShapeDtypeStruct((tiles, FB, 2 * FB), jnp.float32)
    return pl.pallas_call(
        analysis_kernel,
        grid=(tiles,),
        out_shape=(spectra, spectra, jax.ShapeDtypeStruct(mask.shape, jnp.float32)),
        in_specs=[tile_rows(), whole(above), whole(below), whole(tables)],
        out_specs=[whole(spectra), whole(spectra), tile_rows()],
        scratch_shapes=[pltpu.VMEM((tiles + 2, FB, 4 * FB), jnp.float32)],
        compiler_params=params(),
        name="analysis",
    )(mask, above, below, tables)


def imaging(left, right, from_left, from_right, straight, crossed, target):
    tiles = left.shape[0]
    kernels = straight.shape[0]
    tables = jnp.asarray(TABLES["imaging"])
    return pl.pallas_call(
        imaging_kernel,
        grid=(tiles,),
        out_shape=(
            jax.ShapeDtypeStruct(target.shape, jnp.float32),
            jax.ShapeDtypeStruct(left.shape, jnp.float32),
        ),
        in_specs=[spectra_of_tile()] * 4
        + [whole(straight), whole(crossed), tile_rows(), whole(tables)],
        out_specs=[tile_rows(), spectra_of_tile()],
        scratch_shapes=[
            pltpu.VMEM((kernels, COARSE, 2 * COARSE), jnp.float32),
            pltpu.VMEM((2, COARSE, COARSE), jnp.float32),
            pltpu.VMEM((COARSE, COARSE), jnp.float32),
            pltpu.VMEM((2, FB, 2 * FB), jnp.float32),
            pltpu.VMEM((kernels // 2 * COARSE, 2 * FB), jnp.float32),
        ],
        compiler_params=params(),
        name="imaging",
    )(left, right, from_left, from_right, straight, crossed, target, tables)


def synthesis(own, from_left, from_right, above, below, slope):
    tiles = own.shape[0]
    tables = jnp.asarray(TABLES["synthesis"])
    return pl.pallas_call(
        synthesis_kernel,
        grid=(tiles,),
        out_shape=jax.ShapeDtypeStruct(slope.shape, jnp.float32),
        in_specs=[whole(own)] * 3 + [whole(above), whole(below), tile_rows(), whole(tables)],
        out_specs=tile_rows(),
        scratch_shapes=[pltpu.VMEM((tiles + 2, FB, 4 * FB), jnp.float32)],
        compiler_params=params(),
        name="synthesis",
    )(own, from_left, from_right, above, below, slope, tables)


def shifted(value, axis, steps):
    count = lax.axis_size(axis)
    pairs = [(i, i + steps) for i in range(count) if 0 <= i + steps < count]
    return lax.ppermute(value, axis, pairs)


def local(mask_param, target, kernels, weights):
    above = shifted(mask_param[-HALO:], "gy", 1)
    below = shifted(mask_param[:HALO], "gy", -1)
    rows = lax.axis_size("gy")
    inner = rows // 4
    pairs = []
    for place in range(rows):
        mirror = (3 - place // inner) * inner + place % inner
        pairs += [(2 * place, 2 * mirror + 1), (2 * place + 1, 2 * mirror)]
    other = lax.ppermute(kernels, ("gy", "ka"), pairs)
    roots = jnp.sqrt(lax.all_gather(weights, "ka"))
    roots = jnp.where(lax.axis_index("ka") == 0, roots, roots[::-1])
    left, right, slope = analysis(mask_param, above, below)
    from_right = shifted(left, "gx", -1)
    from_left = shifted(right, "gx", 1)
    straight, crossed = preparation(roots, kernels, other)
    resist, grad = imaging(left, right, from_left, from_right, straight, crossed, target)
    grad_left = shifted(grad, "gx", 1)
    grad_right = shifted(grad, "gx", -1)

    flip = jnp.asarray(np.where(np.arange(2 * FB) % 2 == 0, 1.0, -1.0).astype(np.float32))

    def edge(index):
        base = flip * grad[index]
        return jnp.concatenate([base + grad_left[index], base + grad_right[index]], axis=-1)

    from_above = shifted(edge(-1), "gy", 1)
    from_below = shifted(edge(0), "gy", -1)
    gradient = synthesis(grad, grad_left, grad_right, from_above, from_below, slope)
    return (gradient, resist)


def solution(mesh):
    placed = (P("gy", "gx"), P("gy", "gx"), P("ka", None, None), P("ka"))
    return jax.shard_map(
        local, mesh=mesh, in_specs=placed, out_specs=(P("gy", "gx"), P("gy", "gx")), check_vma=False
    )
```

```python
import math

import jax
import jax.numpy as jnp
import ml_dtypes
import numpy as np
from jax import lax
from jax.experimental import pallas as pl
from jax.experimental.pallas import tpu as pltpu
from jax.sharding import PartitionSpec as P

WIN = 512
HALO = 128
FB = 64
TILE = 256
COARSE = 128
HALF = COARSE // 2
VMEM_LIMIT = 32 * 1024 * 1024

bf16 = ml_dtypes.bfloat16


def halves(table):
    high = table.astype(np.float32).astype(bf16)
    low = (table - high.astype(np.float64)).astype(np.float32).astype(bf16)
    return high, low


def as_left(table):
    high, low = halves(table)
    return np.concatenate([high, low, high], axis=1)


def as_right(table):
    high, low = halves(table)
    return np.concatenate([high, high, low], axis=0)


def angles(points):
    frequencies = np.arange(FB) - FB // 2
    windings = np.mod(frequencies[:, None] * np.asarray(points)[None, :], WIN)
    return windings * (2.0 * math.pi / WIN)


ORDER = np.concatenate([np.arange(0, FB, 2), np.arange(1, FB, 2)])


def blocks(table):
    return [table[:, i : i + 128] for i in range(0, table.shape[1], 128)]


def make_tables():
    factor = 1.0 / (WIN * FB)
    pixels = np.arange(HALO)
    columns, rows, outs, pixs = [], [], [], []
    for points in (pixels + 3 * HALO, pixels):
        cos, sin = np.cos(angles(points)), np.sin(angles(points))
        columns.append(as_right(np.concatenate([cos.T, -sin.T], axis=1)))
        pixs.append(as_right(np.concatenate([cos, -sin], axis=0)))
        cos, sin = cos[ORDER], sin[ORDER]
        rows += blocks(as_left(factor * np.concatenate([cos, sin], axis=0)))
        outs += blocks(as_left(factor * np.concatenate([cos.T, sin.T], axis=1)))
    plus = 4 * np.arange(HALF) + 2
    samples = np.concatenate([plus, -plus])
    cos, sin = np.cos(angles(samples)), np.sin(angles(samples))
    spread = as_right(
        np.concatenate(
            [np.concatenate([cos, sin], axis=1), np.concatenate([-sin, cos], axis=1)], axis=0
        )
    )
    gather = np.concatenate(
        [np.concatenate([cos.T, -sin.T], axis=1), np.concatenate([sin.T, cos.T], axis=1)], axis=0
    )
    gather = np.concatenate(halves(gather), axis=1)
    cos, sin = np.cos(angles(plus))[ORDER], np.sin(angles(plus))[ORDER]
    lift = as_left(np.concatenate([cos.T, sin.T], axis=0))
    lift = np.concatenate([lift, np.zeros((COARSE, 64), bf16)], axis=1)
    high, low = halves(np.concatenate([cos, sin], axis=1))
    fold = np.concatenate(
        [np.concatenate([high, high], axis=1), np.concatenate([low, 0 * low], axis=1)], axis=0
    )
    offset = (np.arange(TILE) + HALO)[:, None] - samples[None, :]
    orders = np.arange(1, COARSE // 2)
    turns = np.mod(offset[..., None] * orders, WIN) * (2.0 * math.pi / WIN)
    interp = (1.0 + 2.0 * np.cos(turns).sum(-1)) / COARSE
    high, low = halves(interp)
    fine_left = np.concatenate(
        [np.concatenate([high, high], axis=1), np.concatenate([low, 0 * low], axis=1)], axis=0
    )
    coarse_left = np.concatenate(halves(interp.T), axis=0)
    coarse_right = np.concatenate(halves(interp), axis=1)
    return {
        "analysis": np.concatenate(columns + rows, axis=0),
        "synthesis": np.concatenate(pixs + outs, axis=0),
        "imaging": np.concatenate(
            sum(
                map(
                    blocks,
                    (
                        spread, gather, lift, fold, as_right(interp.T), fine_left, coarse_left,
                        coarse_right,
                    ),
                ),
                [],
            ),
            axis=0,
        ),
    }


TABLES = make_tables()
SPREAD, GATHER, LIFT, FOLD, FINE_RIGHT, FINE_LEFT, COARSE_LEFT, COARSE_RIGHT = (
    (2 * a, b - a)
    for a, b in (
        (0, 384), (384, 640), (640, 768), (768, 896), (896, 1280), (1280, 1792), (1792, 2048),
        (2048, 2304),
    )
)


def split(value):
    high = value.astype(jnp.bfloat16)
    low = (value - high.astype(jnp.float32)).astype(jnp.bfloat16)
    return high, low


def dot(left, right):
    return jnp.dot(left, right, preferred_element_type=jnp.float32)


def times_table(value, table):
    high, low = split(value)
    return dot(jnp.concatenate([high, low, high], axis=1), table)


def table_times(table, value):
    high, low = split(value)
    return dot(table, jnp.concatenate([high, high, low], axis=0))


def stacked_times(table, value):
    high, low = split(value)
    found = dot(table, jnp.concatenate([high, low], axis=0))
    size = found.shape[0] // 2
    return found[:size] + found[size:]


def times_paired(value, table):
    high, low = split(value)
    width = table.shape[1] // 2
    first = dot(high, table)
    return first[:, :width] + (first[:, width:] + dot(low, table[:, :width]))


def col_table(packed, index):
    return packed[index * 384 : (index + 1) * 384, :]


def row_table(packed, index):
    start = 768 + index * 384
    return jnp.concatenate(
        [packed[start + i : start + i + 128, :] for i in (0, 128, 256)], axis=1
    )


def wide_table(packed, place):
    start, size = place
    return jnp.concatenate(
        [packed[start : start + size, :], packed[start + size : start + 2 * size, :]], axis=1
    )


def parity(shape):
    index = lax.broadcasted_iota(jnp.int32, shape, 1)
    return (1 - 2 * (index % 2)).astype(jnp.float32)


def row_parity(shape):
    index = lax.broadcasted_iota(jnp.int32, shape, 0)
    return jnp.where(index < FB // 2, 1.0, -1.0)


def low_lanes(shape):
    return lax.broadcasted_iota(jnp.int32, shape, 1) < FB


def swapped(value):
    return pltpu.roll(value, FB, 1)


def prelude_kernel(first, last, kernels, weights, first_out, last_out, packed, real, imag):
    first_out[...] = first[...]
    last_out[...] = last[...]
    lanes = low_lanes((FB // 2, 2 * FB))
    for index in range(kernels.shape[0]):
        for row in range(FB // 2):
            place = slice(row * 2 * FB, (row + 1) * 2 * FB)
            real[row : row + 1, :] = kernels[index, 0:1, place]
            imag[row : row + 1, :] = kernels[index, 1:2, place]
        root = jnp.sqrt(jnp.full((FB // 2, 2 * FB), weights[index], jnp.float32))
        re, im = root * real[...], root * imag[...]
        packed[index, : FB // 2] = jnp.where(lanes, re, swapped(im))
        packed[index, FB // 2 :] = jnp.where(lanes, swapped(re), im)


def preparation_kernel(own, other, straight, crossed):
    count = own.shape[0]
    lanes = low_lanes((FB, 2 * FB))
    for group, source in enumerate((own, other)):
        for index in range(count):
            spectrum = source[index]
            turned = swapped(spectrum)
            straight[group * count + index] = jnp.where(lanes, spectrum, turned)
            crossed[group * count + index] = jnp.where(lanes, -turned, spectrum)


def analysis_kernel(mask, above, below, tables, left, right, slope, total):
    step = pl.program_id(0)
    count = left.shape[0]
    sign = jnp.where(low_lanes((FB, 2 * FB)), 1.0, -1.0)
    flip = row_parity((FB, 4 * FB))

    def spectra(transmit):
        high, low = split(transmit)
        rows = []
        for side in (0, 1):
            lanes = slice(side * HALO, (side + 1) * HALO)
            three = jnp.concatenate([high[:, lanes], low[:, lanes], high[:, lanes]], axis=1)
            rows.append(dot(three, col_table(tables, side)))
        rows = jnp.concatenate(rows, axis=1)
        found = []
        for part in (0, 1):
            both = table_times(row_table(tables, part), rows[part * HALO : (part + 1) * HALO])
            sine = both[FB:]
            turned = [sign * swapped(sine[:, : 2 * FB]), sign * swapped(sine[:, 2 * FB :])]
            found.append(both[:FB] + jnp.concatenate(turned, axis=1))
        return found

    @pl.when(step == 0)
    def _():
        outer = jnp.concatenate([below[...], above[...]], axis=0)
        upper, lower = spectra(jnp.tanh(outer))
        total[...] = jnp.zeros_like(total)
        total[1] = lower
        total[count] = upper

    transmit = jnp.tanh(mask[...])
    slope[...] = 1.0 - transmit * transmit
    upper, lower = spectra(transmit)
    total[step] += upper
    total[step + 1] += flip * (upper + lower)
    total[step + 2] += lower

    @pl.when(step == count - 1)
    def _():
        left[...] = total[1 : count + 1, :, : 2 * FB]
        right[...] = total[1 : count + 1, :, 2 * FB :]


def imaging_kernel(
    left, right, from_left, from_right, straight, crossed, target, wide,
    resist_ref, grad, fields, intensity, weight, adjoint, sides,
):
    count = straight.shape[0] // 2
    flip = parity((FB, 2 * FB))
    spectrum = flip * (left[0] + right[0]) + from_left[0] + from_right[0]
    turned = swapped(spectrum)

    for group in range(2):
        first = group * count
        products = [
            straight[first + i] * spectrum + crossed[first + i] * turned for i in range(count)
        ]
        rows = times_table(jnp.concatenate(products, axis=0), wide_table(wide, SPREAD))
        total = jnp.zeros((COARSE, COARSE), jnp.float32)
        for i in range(count):
            both = table_times(wide_table(wide, LIFT)[:, :192], rows[i * FB : (i + 1) * FB])
            cosine, sine = both[:HALF], both[HALF:]
            sine_re, sine_im = sine[:, :COARSE], sine[:, COARSE:]
            cosine_re, cosine_im = cosine[:, :COARSE], cosine[:, COARSE:]
            real = jnp.concatenate([cosine_re - sine_im, cosine_re + sine_im], axis=0)
            imag = jnp.concatenate([cosine_im + sine_re, cosine_im - sine_re], axis=0)
            fields[first + i, :, :COARSE] = real
            fields[first + i, :, COARSE:] = imag
            total = total + (real * real + imag * imag)
        intensity[group] = total

    half_fine = times_table(intensity[0] + intensity[1], wide_table(wide, FINE_RIGHT))
    fine = stacked_times(wide_table(wide, FINE_LEFT), half_fine)
    resist = jax.nn.sigmoid(4.0 * (fine - 1.0))
    resist_ref[...] = resist
    misfit = resist - target[...].astype(jnp.float32)
    push = 16.0 * misfit * resist * (1.0 - resist)
    high, low = split(push)
    from_high = dot(wide_table(wide, COARSE_LEFT), high)
    half_coarse = from_high[:COARSE] + (
        from_high[COARSE:] + dot(wide_table(wide, COARSE_LEFT)[:COARSE], low)
    )
    weight[...] = times_paired(half_coarse, wide_table(wide, COARSE_RIGHT))

    sign = jnp.where(low_lanes((HALF, 2 * FB)), 1.0, -1.0)

    for group in range(2):
        first = group * count
        scale = jnp.concatenate([weight[...], weight[...]], axis=1)
        scaled = jnp.concatenate([fields[first + i] * scale for i in range(count)], axis=0)
        sides[group] = times_paired(scaled, wide_table(wide, GATHER))
        total = jnp.zeros((FB, 2 * FB), jnp.float32)
        for i in range(0, count, 2):
            pair = []
            for j in (i, i + 1):
                plus = sides[group, j * COARSE : j * COARSE + HALF, :]
                minus = sides[group, j * COARSE + HALF : (j + 1) * COARSE, :]
                pair.append(
                    jnp.concatenate([plus + minus, sign * swapped(plus - minus)], axis=0)
                )
            found = stacked_times(wide_table(wide, FOLD), jnp.concatenate(pair, axis=1))
            for j in (0, 1):
                part = found[:, j * 2 * FB : (j + 1) * 2 * FB]
                total = total + (
                    straight[first + i + j] * part - crossed[first + i + j] * swapped(part)
                )
        adjoint[group] = total

    grad[0] = adjoint[0] + adjoint[1]


def synthesis_block(upper, middle, lower, slope, tables):
    sign = jnp.where(low_lanes((FB, 2 * FB)), -1.0, 1.0)
    base = row_parity((FB, 4 * FB)) * middle
    rows = []
    for part, near in enumerate((upper, lower)):
        block = base + near
        turned = [sign * swapped(block[:, : 2 * FB]), sign * swapped(block[:, 2 * FB :])]
        stacked = jnp.concatenate([block, jnp.concatenate(turned, axis=1)], axis=0)
        rows.append(table_times(row_table(tables, part), stacked))
    high, low = split(jnp.concatenate(rows, axis=0))
    sides = []
    for side in (0, 1):
        lanes = slice(side * 2 * FB, (side + 1) * 2 * FB)
        three = jnp.concatenate([high[:, lanes], low[:, lanes], high[:, lanes]], axis=1)
        sides.append(dot(three, col_table(tables, side)))
    return jnp.concatenate(sides, axis=1) * slope


def mixed_row(own, from_left, from_right, index):
    base = parity((FB, 2 * FB)) * own[index]
    return jnp.concatenate([base + from_left[index], base + from_right[index]], axis=1)


def inner_kernel(own, from_left, from_right, slope, tables, result, mixed):
    step = pl.program_id(0)

    @pl.when(step == 0)
    def _():
        for index in range(own.shape[0]):
            mixed[index] = mixed_row(own, from_left, from_right, index)

    result[...] = synthesis_block(
        mixed[step], mixed[step + 1], mixed[step + 2], slope[...], tables
    )


def outer_kernel(own, from_left, from_right, above, below, slope, tables, partial, result):
    del partial
    last = own.shape[0] - 1
    rows = [mixed_row(own, from_left, from_right, i) for i in (0, 1, last - 1, last)]

    @pl.when(pl.program_id(0) == 0)
    def _():
        result[...] = synthesis_block(above[...], rows[0], rows[1], slope[...], tables)

    @pl.when(pl.program_id(0) == 1)
    def _():
        result[...] = synthesis_block(rows[2], rows[3], below[...], slope[...], tables)


def whole(array):
    zeros = (0,) * len(array.shape)
    return pl.BlockSpec(array.shape, lambda step: zeros)


def tile_rows():
    return pl.BlockSpec((TILE, TILE), lambda step: (step, 0))


def spectra_of_tile():
    return pl.BlockSpec((1, FB, 2 * FB), lambda step: (step, 0, 0))


def params():
    return pltpu.CompilerParams(
        dimension_semantics=("arbitrary",), vmem_limit_bytes=VMEM_LIMIT
    )


def prelude(mask, kernels, weights):
    count = kernels.shape[0]
    last = mask.shape[0] // HALO - 1
    edge = jax.ShapeDtypeStruct((HALO, TILE), jnp.float32)
    part = pltpu.VMEM((FB // 2, 2 * FB), jnp.float32)
    packed = jax.ShapeDtypeStruct((count, FB, 2 * FB), jnp.float32)
    return pl.pallas_call(
        prelude_kernel,
        grid=(1,),
        out_shape=(edge, edge, packed),
        in_specs=[
            pl.BlockSpec((HALO, TILE), lambda step: (0, 0)),
            pl.BlockSpec((HALO, TILE), lambda step: (last, 0)),
            whole(kernels),
            pl.BlockSpec(memory_space=pltpu.SMEM),
        ],
        out_specs=[whole(edge), whole(edge), whole(packed)],
        scratch_shapes=[part, part],
        compiler_params=params(),
        name="prelude",
    )(mask, mask, kernels, weights)


def preparation(own, other):
    shape = jax.ShapeDtypeStruct((2 * own.shape[0], FB, 2 * FB), jnp.float32)
    return pl.pallas_call(
        preparation_kernel,
        out_shape=(shape, shape),
        in_specs=[pl.BlockSpec(memory_space=pltpu.VMEM)] * 2,
        out_specs=[pl.BlockSpec(memory_space=pltpu.VMEM)] * 2,
        compiler_params=pltpu.CompilerParams(vmem_limit_bytes=VMEM_LIMIT),
        cost_estimate=pl.CostEstimate(flops=400000, bytes_accessed=1600000, transcendentals=0),
        name="preparation",
    )(own, other)


def analysis(mask, above, below):
    tiles = mask.shape[0] // TILE
    tables = jnp.asarray(TABLES["analysis"])
    spectra = jax.ShapeDtypeStruct((tiles, FB, 2 * FB), jnp.float32)
    return pl.pallas_call(
        analysis_kernel,
        grid=(tiles,),
        out_shape=(spectra, spectra, jax.ShapeDtypeStruct(mask.shape, jnp.float32)),
        in_specs=[tile_rows(), whole(above), whole(below), whole(tables)],
        out_specs=[whole(spectra), whole(spectra), tile_rows()],
        scratch_shapes=[pltpu.VMEM((tiles + 2, FB, 4 * FB), jnp.float32)],
        compiler_params=params(),
        name="analysis",
    )(mask, above, below, tables)


def imaging(left, right, from_left, from_right, straight, crossed, target):
    tiles = left.shape[0]
    kernels = straight.shape[0]
    tables = jnp.asarray(TABLES["imaging"])
    return pl.pallas_call(
        imaging_kernel,
        grid=(tiles,),
        out_shape=(
            jax.ShapeDtypeStruct(target.shape, jnp.float32),
            jax.ShapeDtypeStruct(left.shape, jnp.float32),
        ),
        in_specs=[spectra_of_tile()] * 4
        + [whole(straight), whole(crossed), tile_rows(), whole(tables)],
        out_specs=[tile_rows(), spectra_of_tile()],
        scratch_shapes=[
            pltpu.VMEM((kernels, COARSE, 2 * COARSE), jnp.float32),
            pltpu.VMEM((2, COARSE, COARSE), jnp.float32),
            pltpu.VMEM((COARSE, COARSE), jnp.float32),
            pltpu.VMEM((2, FB, 2 * FB), jnp.float32),
            pltpu.VMEM((2, kernels // 2 * COARSE, 2 * FB), jnp.float32),
        ],
        compiler_params=params(),
        name="imaging",
    )(left, right, from_left, from_right, straight, crossed, target, tables)


def inner_synthesis(own, from_left, from_right, slope):
    tiles = own.shape[0]
    tables = jnp.asarray(TABLES["synthesis"])
    place = pl.BlockSpec((TILE, TILE), lambda step: (step + 1, 0))
    return pl.pallas_call(
        inner_kernel,
        grid=(tiles - 2,),
        out_shape=jax.ShapeDtypeStruct(slope.shape, jnp.float32),
        in_specs=[whole(own)] * 3 + [place, whole(tables)],
        out_specs=place,
        scratch_shapes=[pltpu.VMEM((tiles, FB, 4 * FB), jnp.float32)],
        compiler_params=params(),
        cost_estimate=pl.CostEstimate(
            flops=1500000000, bytes_accessed=2500000, transcendentals=0
        ),
        name="inner_synthesis",
    )(own, from_left, from_right, slope, tables)


def outer_synthesis(own, from_left, from_right, above, below, slope, partial):
    tiles = own.shape[0]
    tables = jnp.asarray(TABLES["synthesis"])
    place = pl.BlockSpec((TILE, TILE), lambda step: (step * (tiles - 1), 0))
    return pl.pallas_call(
        outer_kernel,
        grid=(2,),
        out_shape=jax.ShapeDtypeStruct(slope.shape, jnp.float32),
        in_specs=[whole(own)] * 3
        + [whole(above), whole(below), place, whole(tables), pl.BlockSpec(memory_space=pl.ANY)],
        out_specs=place,
        input_output_aliases={7: 0},
        compiler_params=params(),
        name="outer_synthesis",
    )(own, from_left, from_right, above, below, slope, tables, partial)


def shifted(value, axis, steps):
    count = lax.axis_size(axis)
    pairs = [(i, i + steps) for i in range(count) if 0 <= i + steps < count]
    return lax.ppermute(value, axis, pairs)


def local(mask_param, target, kernels, weights):
    first, last, own = prelude(mask_param, kernels, weights)
    above = shifted(last, "gy", 1)
    below = shifted(first, "gy", -1)
    rows = lax.axis_size("gy")
    inner = rows // 4
    pairs = []
    for place in range(rows):
        mirror = (3 - place // inner) * inner + place % inner
        pairs += [(2 * place, 2 * mirror + 1), (2 * place + 1, 2 * mirror)]
    other = lax.ppermute(own, ("gy", "ka"), pairs)
    left, right, slope = analysis(mask_param, above, below)
    from_right = shifted(left, "gx", -1)
    from_left = shifted(right, "gx", 1)
    straight, crossed = preparation(own, other)
    resist, grad = imaging(left, right, from_left, from_right, straight, crossed, target)
    grad_left = shifted(grad, "gx", 1)
    grad_right = shifted(grad, "gx", -1)

    flip = jnp.asarray(np.where(np.arange(2 * FB) % 2 == 0, 1.0, -1.0).astype(np.float32))

    def edge(index):
        base = flip * grad[index]
        return jnp.concatenate([base + grad_left[index], base + grad_right[index]], axis=-1)

    from_above = shifted(edge(-1), "gy", 1)
    from_below = shifted(edge(0), "gy", -1)
    partial = inner_synthesis(grad, grad_left, grad_right, slope)
    gradient = outer_synthesis(
        grad, grad_left, grad_right, from_above, from_below, slope, partial
    )
    return (gradient, resist)


def solution(mesh):
    placed = (P("gy", "gx"), P("gy", "gx"), P("ka", None, None), P("ka"))
    return jax.shard_map(
        local, mesh=mesh, in_specs=placed, out_specs=(P("gy", "gx"), P("gy", "gx")), check_vma=False
    )
```

```python
import math

import jax
import jax.numpy as jnp
import ml_dtypes
import numpy as np
from jax import lax
from jax.experimental import pallas as pl
from jax.experimental.pallas import tpu as pltpu
from jax.sharding import PartitionSpec as P

WIN = 512
HALO = 128
FB = 64
TILE = 256
COARSE = 128
HALF = COARSE // 2
VMEM_LIMIT = 32 * 1024 * 1024
PAIR = 2
PRELUDE_LIMIT = 63 * 1024 * 1024

bf16 = ml_dtypes.bfloat16


def halves(table):
    high = table.astype(np.float32).astype(bf16)
    low = (table - high.astype(np.float64)).astype(np.float32).astype(bf16)
    return high, low


def as_left(table):
    high, low = halves(table)
    return np.concatenate([high, low, high], axis=1)


def as_right(table):
    high, low = halves(table)
    return np.concatenate([high, high, low], axis=0)


def angles(points):
    frequencies = np.arange(FB) - FB // 2
    windings = np.mod(frequencies[:, None] * np.asarray(points)[None, :], WIN)
    return windings * (2.0 * math.pi / WIN)


ORDER = np.concatenate([np.arange(0, FB, 2), np.arange(1, FB, 2)])


def blocks(table):
    return [table[:, i : i + 128] for i in range(0, table.shape[1], 128)]


def make_tables():
    factor = 1.0 / (WIN * FB)
    pixels = np.arange(HALO)
    columns, rows, outs, pixs = [], [], [], []
    for points in (pixels + 3 * HALO, pixels):
        cos, sin = np.cos(angles(points)), np.sin(angles(points))
        columns.append(as_right(np.concatenate([cos.T, -sin.T], axis=1)))
        pixs.append(as_right(np.concatenate([cos, -sin], axis=0)))
        cos, sin = cos[ORDER], sin[ORDER]
        rows += blocks(as_left(factor * np.concatenate([cos, sin], axis=0)))
        outs += blocks(as_left(factor * np.concatenate([cos.T, sin.T], axis=1)))
    plus = 4 * np.arange(HALF) + 2
    samples = np.concatenate([plus, -plus])
    cos, sin = np.cos(angles(samples)), np.sin(angles(samples))
    spread = as_right(
        np.concatenate(
            [np.concatenate([cos, sin], axis=1), np.concatenate([-sin, cos], axis=1)], axis=0
        )
    )
    gather = np.concatenate(
        [np.concatenate([cos.T, -sin.T], axis=1), np.concatenate([sin.T, cos.T], axis=1)], axis=0
    )
    gather = np.concatenate(halves(gather), axis=1)
    cos, sin = np.cos(angles(plus))[ORDER], np.sin(angles(plus))[ORDER]
    lift = as_left(np.concatenate([cos.T, sin.T], axis=0))
    lift = np.concatenate([lift, np.zeros((COARSE, 64), bf16)], axis=1)
    high, low = halves(np.concatenate([cos, sin], axis=1))
    fold = np.concatenate(
        [np.concatenate([high, high], axis=1), np.concatenate([low, 0 * low], axis=1)], axis=0
    )
    offset = (np.arange(TILE) + HALO)[:, None] - samples[None, :]
    orders = np.arange(1, COARSE // 2)
    turns = np.mod(offset[..., None] * orders, WIN) * (2.0 * math.pi / WIN)
    interp = (1.0 + 2.0 * np.cos(turns).sum(-1)) / COARSE
    high, low = halves(interp)
    fine_left = np.concatenate(
        [np.concatenate([high, high], axis=1), np.concatenate([low, 0 * low], axis=1)], axis=0
    )
    coarse_left = np.concatenate(halves(interp.T), axis=0)
    coarse_right = np.concatenate(halves(interp), axis=1)
    return {
        "analysis": np.concatenate(columns + rows, axis=0),
        "synthesis": np.concatenate(pixs + outs, axis=0),
        "imaging": np.concatenate(
            sum(
                map(
                    blocks,
                    (
                        spread, gather, lift, fold, as_right(interp.T), fine_left, coarse_left,
                        coarse_right,
                    ),
                ),
                [],
            ),
            axis=0,
        ),
    }


TABLES = make_tables()
SPREAD, GATHER, LIFT, FOLD, FINE_RIGHT, FINE_LEFT, COARSE_LEFT, COARSE_RIGHT = (
    (2 * a, b - a)
    for a, b in (
        (0, 384), (384, 640), (640, 768), (768, 896), (896, 1280), (1280, 1792), (1792, 2048),
        (2048, 2304),
    )
)


def split(value):
    high = value.astype(jnp.bfloat16)
    low = (value - high.astype(jnp.float32)).astype(jnp.bfloat16)
    return high, low


def dot(left, right):
    return jnp.dot(left, right, preferred_element_type=jnp.float32)


def times_table(value, table):
    high, low = split(value)
    return dot(jnp.concatenate([high, low, high], axis=1), table)


def table_times(table, value):
    high, low = split(value)
    return dot(table, jnp.concatenate([high, high, low], axis=0))


def stacked_times(table, value):
    high, low = split(value)
    found = dot(table, jnp.concatenate([high, low], axis=0))
    size = found.shape[0] // 2
    return found[:size] + found[size:]


def times_paired(value, table):
    high, low = split(value)
    width = table.shape[1] // 2
    first = dot(high, table)
    return first[:, :width] + (first[:, width:] + dot(low, table[:, :width]))


def col_table(packed, index):
    return packed[index * 384 : (index + 1) * 384, :]


def row_table(packed, index):
    start = 768 + index * 384
    return jnp.concatenate(
        [packed[start + i : start + i + 128, :] for i in (0, 128, 256)], axis=1
    )


def wide_table(packed, place):
    start, size = place
    return jnp.concatenate(
        [packed[start : start + size, :], packed[start + size : start + 2 * size, :]], axis=1
    )


def parity(shape):
    index = lax.broadcasted_iota(jnp.int32, shape, 1)
    return (1 - 2 * (index % 2)).astype(jnp.float32)


def row_parity(shape):
    index = lax.broadcasted_iota(jnp.int32, shape, 0)
    return jnp.where(index < FB // 2, 1.0, -1.0)


def low_lanes(shape):
    return lax.broadcasted_iota(jnp.int32, shape, 1) < FB


def swapped(value):
    return pltpu.roll(value, FB, 1)


def prelude_kernel(odd, first, last, kernels, weights, even_out, odd_out, packed, real, imag):
    odd_row = odd[0] == 1
    even_out[...] = jnp.where(odd_row, first[...], last[...])
    odd_out[...] = jnp.where(odd_row, last[...], first[...])
    lanes = low_lanes((FB // 2, 2 * FB))
    for index in range(kernels.shape[0]):
        for row in range(FB // 2):
            place = slice(row * 2 * FB, (row + 1) * 2 * FB)
            real[row : row + 1, :] = kernels[index, 0:1, place]
            imag[row : row + 1, :] = kernels[index, 1:2, place]
        root = jnp.sqrt(jnp.full((FB // 2, 2 * FB), weights[index], jnp.float32))
        re, im = root * real[...], root * imag[...]
        packed[index, : FB // 2] = jnp.where(lanes, re, swapped(im))
        packed[index, FB // 2 :] = jnp.where(lanes, swapped(re), im)


def preparation_kernel(own, other, straight, crossed):
    count = own.shape[0]
    lanes = low_lanes((FB, 2 * FB))
    for group, source in enumerate((own, other)):
        for index in range(count):
            spectrum = source[index]
            turned = swapped(spectrum)
            straight[group * count + index] = jnp.where(lanes, spectrum, turned)
            crossed[group * count + index] = jnp.where(lanes, -turned, spectrum)


def analysis_kernel(
    odd, mask, halo_even, halo_odd, tables, share, to_even, to_odd, slope, total
):
    step = pl.program_id(0)
    count = share.shape[0]
    sign = jnp.where(low_lanes((FB, 2 * FB)), 1.0, -1.0)
    flip = row_parity((FB, 4 * FB))

    def spectra(transmit):
        high, low = split(transmit)
        rows = []
        for side in (0, 1):
            lanes = slice(side * HALO, (side + 1) * HALO)
            three = jnp.concatenate([high[:, lanes], low[:, lanes], high[:, lanes]], axis=1)
            rows.append(dot(three, col_table(tables, side)))
        rows = jnp.concatenate(rows, axis=1)
        found = []
        for part in (0, 1):
            both = table_times(row_table(tables, part), rows[part * HALO : (part + 1) * HALO])
            sine = both[FB:]
            turned = [sign * swapped(sine[:, : 2 * FB]), sign * swapped(sine[:, 2 * FB :])]
            found.append(both[:FB] + jnp.concatenate(turned, axis=1))
        return found

    @pl.when(step == 0)
    def _():
        odd_row = odd[0] == 1
        below = jnp.where(odd_row, halo_odd[...], halo_even[...])
        above = jnp.where(odd_row, halo_even[...], halo_odd[...])
        outer = jnp.concatenate([below, above], axis=0)
        upper, lower = spectra(jnp.tanh(outer))
        total[...] = jnp.zeros_like(total)
        total[1] = lower
        total[count] = upper

    transmit = jnp.tanh(mask[...])
    slope[...] = 1.0 - transmit * transmit
    upper, lower = spectra(transmit)
    total[step] += upper
    total[step + 1] += flip * (upper + lower)
    total[step + 2] += lower

    @pl.when(step == count - 1)
    def _():
        odd_col = odd[1] == 1
        for index in range(count):
            left, right = total[index + 1, :, : 2 * FB], total[index + 1, :, 2 * FB :]
            share[index] = parity((FB, 2 * FB)) * (left + right)
            to_even[index] = jnp.where(odd_col, left, right)
            to_odd[index] = jnp.where(odd_col, right, left)


def imaging_kernel(
    share, from_even, from_odd, straight, crossed, target, wide,
    resist_ref, grad, fields, sides,
):
    count = straight.shape[0] // 2
    sign = jnp.where(low_lanes((HALF, 2 * FB)), 1.0, -1.0)
    tiles = range(PAIR)
    weights = []
    intensities = [[] for tile in tiles]

    for tile in tiles:
        spectrum = share[tile] + from_even[tile] + from_odd[tile]
        turned = swapped(spectrum)
        for group in range(2):
            first = group * count
            products = [
                straight[first + i] * spectrum + crossed[first + i] * turned
                for i in range(count)
            ]
            rows = times_table(jnp.concatenate(products, axis=0), wide_table(wide, SPREAD))
            total = jnp.zeros((COARSE, COARSE), jnp.float32)
            for i in range(count):
                both = table_times(
                    wide_table(wide, LIFT)[:, :192], rows[i * FB : (i + 1) * FB]
                )
                cosine, sine = both[:HALF], both[HALF:]
                sine_re, sine_im = sine[:, :COARSE], sine[:, COARSE:]
                cosine_re, cosine_im = cosine[:, :COARSE], cosine[:, COARSE:]
                real = jnp.concatenate([cosine_re - sine_im, cosine_re + sine_im], axis=0)
                imag = jnp.concatenate([cosine_im + sine_re, cosine_im - sine_re], axis=0)
                fields[tile, first + i, :, :COARSE] = real
                fields[tile, first + i, :, COARSE:] = imag
                total = total + (real * real + imag * imag)
            intensities[tile].append(total)

    for tile in tiles:
        intensity = intensities[tile][0] + intensities[tile][1]
        half_fine = times_table(intensity, wide_table(wide, FINE_RIGHT))
        fine = stacked_times(wide_table(wide, FINE_LEFT), half_fine)
        resist = jax.nn.sigmoid(4.0 * (fine - 1.0))
        place = slice(tile * TILE, (tile + 1) * TILE)
        resist_ref[place, :] = resist
        misfit = resist - target[place, :].astype(jnp.float32)
        push = 16.0 * misfit * resist * (1.0 - resist)
        high, low = split(push)
        from_high = dot(wide_table(wide, COARSE_LEFT), high)
        half_coarse = from_high[:COARSE] + (
            from_high[COARSE:] + dot(wide_table(wide, COARSE_LEFT)[:COARSE], low)
        )
        weights.append(times_paired(half_coarse, wide_table(wide, COARSE_RIGHT)))

    for tile in tiles:
        scale = jnp.concatenate([weights[tile], weights[tile]], axis=1)
        adjoint = []
        for group in range(2):
            first = group * count
            scaled = jnp.concatenate(
                [fields[tile, first + i] * scale for i in range(count)], axis=0
            )
            sides[tile, group] = times_paired(scaled, wide_table(wide, GATHER))
            total = jnp.zeros((FB, 2 * FB), jnp.float32)
            for i in range(0, count, 2):
                pair = []
                for j in (i, i + 1):
                    plus = sides[tile, group, j * COARSE : j * COARSE + HALF, :]
                    minus = sides[tile, group, j * COARSE + HALF : (j + 1) * COARSE, :]
                    pair.append(
                        jnp.concatenate([plus + minus, sign * swapped(plus - minus)], axis=0)
                    )
                found = stacked_times(
                    wide_table(wide, FOLD), jnp.concatenate(pair, axis=1)
                )
                for j in (0, 1):
                    part = found[:, j * 2 * FB : (j + 1) * 2 * FB]
                    total = total + (
                        straight[first + i + j] * part - crossed[first + i + j] * swapped(part)
                    )
            adjoint.append(total)
        grad[tile] = adjoint[0] + adjoint[1]


def sides_of(odd, even_in, odd_in, index):
    odd_col = odd[1] == 1
    return (
        jnp.where(odd_col, even_in[index], odd_in[index]),
        jnp.where(odd_col, odd_in[index], even_in[index]),
    )


def synthesis_block(upper, middle, lower, slope, tables):
    sign = jnp.where(low_lanes((FB, 2 * FB)), -1.0, 1.0)
    base = row_parity((FB, 4 * FB)) * middle
    rows = []
    for part, near in enumerate((upper, lower)):
        block = base + near
        turned = [sign * swapped(block[:, : 2 * FB]), sign * swapped(block[:, 2 * FB :])]
        stacked = jnp.concatenate([block, jnp.concatenate(turned, axis=1)], axis=0)
        rows.append(table_times(row_table(tables, part), stacked))
    high, low = split(jnp.concatenate(rows, axis=0))
    sides = []
    for side in (0, 1):
        lanes = slice(side * 2 * FB, (side + 1) * 2 * FB)
        three = jnp.concatenate([high[:, lanes], low[:, lanes], high[:, lanes]], axis=1)
        sides.append(dot(three, col_table(tables, side)))
    return jnp.concatenate(sides, axis=1) * slope


def mixed_row(odd, own, even_in, odd_in, index):
    base = parity((FB, 2 * FB)) * own[index]
    from_left, from_right = sides_of(odd, even_in, odd_in, index)
    return jnp.concatenate([base + from_left, base + from_right], axis=1)


def edges_kernel(odd, own, even_in, odd_in, side_even, side_odd):
    first = mixed_row(odd, own, even_in, odd_in, 0)
    last = mixed_row(odd, own, even_in, odd_in, own.shape[0] - 1)
    odd_row = odd[0] == 1
    side_even[...] = jnp.where(odd_row, first, last)
    side_odd[...] = jnp.where(odd_row, last, first)


def inner_kernel(odd, own, even_in, odd_in, slope, tables, result, mixed):
    step = pl.program_id(0)

    @pl.when(step == 0)
    def _():
        for index in range(own.shape[0]):
            mixed[index] = mixed_row(odd, own, even_in, odd_in, index)

    result[...] = synthesis_block(
        mixed[step], mixed[step + 1], mixed[step + 2], slope[...], tables
    )


def outer_kernel(
    odd, own, even_in, odd_in, near_even, near_odd, slope, tables, partial, result
):
    del partial
    last = own.shape[0] - 1
    rows = [mixed_row(odd, own, even_in, odd_in, i) for i in (0, 1, last - 1, last)]
    odd_row = odd[0] == 1

    @pl.when(pl.program_id(0) == 0)
    def _():
        above = jnp.where(odd_row, near_even[...], near_odd[...])
        result[...] = synthesis_block(above, rows[0], rows[1], slope[...], tables)

    @pl.when(pl.program_id(0) == 1)
    def _():
        below = jnp.where(odd_row, near_odd[...], near_even[...])
        result[...] = synthesis_block(rows[2], rows[3], below, slope[...], tables)


def whole(array):
    zeros = (0,) * len(array.shape)
    return pl.BlockSpec(array.shape, lambda step: zeros)


def tile_rows():
    return pl.BlockSpec((TILE, TILE), lambda step: (step, 0))


def params(limit=VMEM_LIMIT):
    return pltpu.CompilerParams(dimension_semantics=("arbitrary",), vmem_limit_bytes=limit)


def prelude(odd, mask, kernels, weights):
    count = kernels.shape[0]
    last = mask.shape[0] // HALO - 1
    edge = jax.ShapeDtypeStruct((HALO, TILE), jnp.float32)
    part = pltpu.VMEM((FB // 2, 2 * FB), jnp.float32)
    packed = jax.ShapeDtypeStruct((count, FB, 2 * FB), jnp.float32)
    return pl.pallas_call(
        prelude_kernel,
        grid=(1,),
        out_shape=(edge, edge, packed),
        in_specs=[
            pl.BlockSpec(memory_space=pltpu.SMEM),
            pl.BlockSpec((HALO, TILE), lambda step: (0, 0)),
            pl.BlockSpec((HALO, TILE), lambda step: (last, 0)),
            whole(kernels),
            pl.BlockSpec(memory_space=pltpu.SMEM),
        ],
        out_specs=[whole(edge), whole(edge), whole(packed)],
        scratch_shapes=[part, part],
        compiler_params=params(PRELUDE_LIMIT),
        name="prelude",
    )(odd, mask, mask, kernels, weights)


def preparation(own, other):
    shape = jax.ShapeDtypeStruct((2 * own.shape[0], FB, 2 * FB), jnp.float32)
    return pl.pallas_call(
        preparation_kernel,
        out_shape=(shape, shape),
        in_specs=[pl.BlockSpec(memory_space=pltpu.VMEM)] * 2,
        out_specs=[pl.BlockSpec(memory_space=pltpu.VMEM)] * 2,
        compiler_params=pltpu.CompilerParams(vmem_limit_bytes=VMEM_LIMIT),
        cost_estimate=pl.CostEstimate(flops=400000, bytes_accessed=1600000, transcendentals=0),
        name="preparation",
    )(own, other)


def analysis(odd, mask, halo_even, halo_odd):
    tiles = mask.shape[0] // TILE
    tables = jnp.asarray(TABLES["analysis"])
    spectra = jax.ShapeDtypeStruct((tiles, FB, 2 * FB), jnp.float32)
    return pl.pallas_call(
        analysis_kernel,
        grid=(tiles,),
        out_shape=(spectra, spectra, spectra, jax.ShapeDtypeStruct(mask.shape, jnp.float32)),
        in_specs=[
            pl.BlockSpec(memory_space=pltpu.SMEM),
            tile_rows(),
            whole(halo_even),
            whole(halo_odd),
            whole(tables),
        ],
        out_specs=[whole(spectra)] * 3 + [tile_rows()],
        scratch_shapes=[pltpu.VMEM((tiles + 2, FB, 4 * FB), jnp.float32)],
        compiler_params=params(),
        name="analysis",
    )(odd, mask, halo_even, halo_odd, tables)


def imaging(share, from_even, from_odd, straight, crossed, target):
    tiles = share.shape[0]
    kernels = straight.shape[0]
    tables = jnp.asarray(TABLES["imaging"])
    spectra = pl.BlockSpec((PAIR, FB, 2 * FB), lambda step: (step, 0, 0))
    pixels = pl.BlockSpec((PAIR * TILE, TILE), lambda step: (step, 0))
    return pl.pallas_call(
        imaging_kernel,
        grid=(tiles // PAIR,),
        out_shape=(
            jax.ShapeDtypeStruct(target.shape, jnp.float32),
            jax.ShapeDtypeStruct(share.shape, jnp.float32),
        ),
        in_specs=[spectra] * 3 + [whole(straight), whole(crossed), pixels, whole(tables)],
        out_specs=[pixels, spectra],
        scratch_shapes=[
            pltpu.VMEM((PAIR, kernels, COARSE, 2 * COARSE), jnp.float32),
            pltpu.VMEM((PAIR, 2, kernels // 2 * COARSE, 2 * FB), jnp.float32),
        ],
        compiler_params=params(),
        name="imaging",
    )(share, from_even, from_odd, straight, crossed, target, tables)


def edges(odd, grad, grad_even, grad_odd):
    side = jax.ShapeDtypeStruct((FB, 4 * FB), jnp.float32)
    vmem = pl.BlockSpec(memory_space=pltpu.VMEM)
    return pl.pallas_call(
        edges_kernel,
        out_shape=(side, side),
        in_specs=[pl.BlockSpec(memory_space=pltpu.SMEM)] + [vmem] * 3,
        out_specs=[vmem] * 2,
        compiler_params=pltpu.CompilerParams(vmem_limit_bytes=VMEM_LIMIT),
        name="edges",
    )(odd, grad, grad_even, grad_odd)


def inner_synthesis(odd, own, even_in, odd_in, slope):
    tiles = own.shape[0]
    tables = jnp.asarray(TABLES["synthesis"])
    place = pl.BlockSpec((TILE, TILE), lambda step: (step + 1, 0))
    return pl.pallas_call(
        inner_kernel,
        grid=(tiles - 2,),
        out_shape=jax.ShapeDtypeStruct(slope.shape, jnp.float32),
        in_specs=[pl.BlockSpec(memory_space=pltpu.SMEM)]
        + [whole(own)] * 3
        + [place, whole(tables)],
        out_specs=place,
        scratch_shapes=[pltpu.VMEM((tiles, FB, 4 * FB), jnp.float32)],
        compiler_params=params(),
        cost_estimate=pl.CostEstimate(
            flops=1500000000, bytes_accessed=2500000, transcendentals=0
        ),
        name="inner_synthesis",
    )(odd, own, even_in, odd_in, slope, tables)


def outer_synthesis(odd, own, even_in, odd_in, near_even, near_odd, slope, partial):
    tiles = own.shape[0]
    tables = jnp.asarray(TABLES["synthesis"])
    place = pl.BlockSpec((TILE, TILE), lambda step: (step * (tiles - 1), 0))
    return pl.pallas_call(
        outer_kernel,
        grid=(2,),
        out_shape=jax.ShapeDtypeStruct(slope.shape, jnp.float32),
        in_specs=[pl.BlockSpec(memory_space=pltpu.SMEM)]
        + [whole(own)] * 3
        + [whole(near_even), whole(near_odd), place, whole(tables)]
        + [pl.BlockSpec(memory_space=pl.ANY)],
        out_specs=place,
        input_output_aliases={8: 0},
        compiler_params=params(),
        name="outer_synthesis",
    )(odd, own, even_in, odd_in, near_even, near_odd, slope, tables, partial)


def swap_pairs(count, first):
    pairs = []
    for place in range(first, count - 1, 2):
        pairs += [(place, place + 1), (place + 1, place)]
    return pairs


def local(mask_param, target, kernels, weights):
    rows, cols = lax.axis_size("gy"), lax.axis_size("gx")
    odd_row, odd_col = lax.axis_index("gy") % 2, lax.axis_index("gx") % 2
    odd = jnp.stack([odd_row, odd_col]).astype(jnp.int32)

    def swap(value, axis, first):
        return lax.ppermute(value, axis, swap_pairs(lax.axis_size(axis), first))

    edge_even, edge_odd, own = prelude(odd, mask_param, kernels, weights)
    halo_odd = swap(edge_odd, "gy", 1)
    halo_even = swap(edge_even, "gy", 0)
    inner = rows // 4
    pairs = []
    for place in range(rows):
        mirror = (3 - place // inner) * inner + place % inner
        pairs += [(2 * place, 2 * mirror + 1), (2 * place + 1, 2 * mirror)]
    other = lax.ppermute(own, ("gy", "ka"), pairs)
    share, to_even, to_odd, slope = analysis(odd, mask_param, halo_even, halo_odd)
    from_odd = swap(to_odd, "gx", 1)
    from_even = swap(to_even, "gx", 0)
    straight, crossed = preparation(own, other)
    resist, grad = imaging(share, from_even, from_odd, straight, crossed, target)
    grad_odd = swap(grad, "gx", 1)
    grad_even = swap(grad, "gx", 0)
    side_even, side_odd = edges(odd, grad, grad_even, grad_odd)
    near_odd = swap(side_odd, "gy", 1)
    near_even = swap(side_even, "gy", 0)
    partial = inner_synthesis(odd, grad, grad_even, grad_odd, slope)
    gradient = outer_synthesis(
        odd, grad, grad_even, grad_odd, near_even, near_odd, slope, partial
    )
    return (gradient, resist)


def solution(mesh):
    placed = (P("gy", "gx"), P("gy", "gx"), P("ka", None, None), P("ka"))
    return jax.shard_map(
        local, mesh=mesh, in_specs=placed, out_specs=(P("gy", "gx"), P("gy", "gx")), check_vma=False
    )
```

```python
import math

import jax
import jax.numpy as jnp
import ml_dtypes
import numpy as np
from jax import lax
from jax.experimental import pallas as pl
from jax.experimental.pallas import tpu as pltpu
from jax.sharding import PartitionSpec as P

WIN = 512
HALO = 128
FB = 64
TILE = 256
COARSE = 128
HALF = COARSE // 2
VMEM_LIMIT = 32 * 1024 * 1024
PAIR = 2
TILES_AT_ONCE = 3
FIRST_LIMIT = 63 * 1024 * 1024

bf16 = ml_dtypes.bfloat16


def halves(table):
    high = table.astype(np.float32).astype(bf16)
    low = (table - high.astype(np.float64)).astype(np.float32).astype(bf16)
    return high, low


def as_left(table):
    high, low = halves(table)
    return np.concatenate([high, low, high], axis=1)


def as_right(table):
    high, low = halves(table)
    return np.concatenate([high, high, low], axis=0)


def angles(points):
    frequencies = np.arange(FB) - FB // 2
    windings = np.mod(frequencies[:, None] * np.asarray(points)[None, :], WIN)
    return windings * (2.0 * math.pi / WIN)


ORDER = np.concatenate([np.arange(0, FB, 2), np.arange(1, FB, 2)])


def blocks(table):
    return [table[:, i : i + 128] for i in range(0, table.shape[1], 128)]


def make_tables():
    factor = 1.0 / (WIN * FB)
    pixels = np.arange(HALO)
    columns, rows, outs, pixs = [], [], [], []
    for points in (pixels + 3 * HALO, pixels):
        cos, sin = np.cos(angles(points)), np.sin(angles(points))
        columns.append(as_right(np.concatenate([cos.T, -sin.T], axis=1)))
        pixs.append(as_right(np.concatenate([cos, -sin], axis=0)))
        cos, sin = cos[ORDER], sin[ORDER]
        rows += blocks(as_left(factor * np.concatenate([cos, sin], axis=0)))
        outs += blocks(as_left(factor * np.concatenate([cos.T, sin.T], axis=1)))
    plus = 4 * np.arange(HALF) + 2
    samples = np.concatenate([plus, -plus])
    cos, sin = np.cos(angles(samples)), np.sin(angles(samples))
    spread = as_right(
        np.concatenate(
            [np.concatenate([cos, sin], axis=1), np.concatenate([-sin, cos], axis=1)], axis=0
        )
    )
    gather = np.concatenate(
        [np.concatenate([cos.T, -sin.T], axis=1), np.concatenate([sin.T, cos.T], axis=1)], axis=0
    )
    gather = np.concatenate(halves(gather), axis=1)
    cos, sin = np.cos(angles(plus))[ORDER], np.sin(angles(plus))[ORDER]
    lift = as_left(np.concatenate([cos.T, sin.T], axis=0))
    lift = np.concatenate([lift, np.zeros((COARSE, 64), bf16)], axis=1)
    high, low = halves(np.concatenate([cos, sin], axis=1))
    fold = np.concatenate(
        [np.concatenate([high, high], axis=1), np.concatenate([low, 0 * low], axis=1)], axis=0
    )
    offset = (np.arange(TILE) + HALO)[:, None] - samples[None, :]
    orders = np.arange(1, COARSE // 2)
    turns = np.mod(offset[..., None] * orders, WIN) * (2.0 * math.pi / WIN)
    interp = (1.0 + 2.0 * np.cos(turns).sum(-1)) / COARSE
    high, low = halves(interp)
    fine_left = np.concatenate(
        [np.concatenate([high, high], axis=1), np.concatenate([low, 0 * low], axis=1)], axis=0
    )
    coarse_left = np.concatenate(halves(interp.T), axis=0)
    coarse_right = np.concatenate(halves(interp), axis=1)
    return {
        "analysis": np.concatenate(columns + rows, axis=0),
        "synthesis": np.concatenate(pixs + outs, axis=0),
        "imaging": np.concatenate(
            sum(
                map(
                    blocks,
                    (
                        spread, gather, lift, fold, as_right(interp.T), fine_left, coarse_left,
                        coarse_right,
                    ),
                ),
                [],
            ),
            axis=0,
        ),
    }


TABLES = make_tables()
SPREAD, GATHER, LIFT, FOLD, FINE_RIGHT, FINE_LEFT, COARSE_LEFT, COARSE_RIGHT = (
    (2 * a, b - a)
    for a, b in (
        (0, 384), (384, 640), (640, 768), (768, 896), (896, 1280), (1280, 1792), (1792, 2048),
        (2048, 2304),
    )
)


def split(value):
    high = value.astype(jnp.bfloat16)
    low = (value - high.astype(jnp.float32)).astype(jnp.bfloat16)
    return high, low


def dot(left, right):
    return jnp.dot(left, right, preferred_element_type=jnp.float32)


def times_table(value, table):
    high, low = split(value)
    return dot(jnp.concatenate([high, low, high], axis=1), table)


def table_times(table, value):
    high, low = split(value)
    return dot(table, jnp.concatenate([high, high, low], axis=0))


def stacked_times(table, value):
    high, low = split(value)
    found = dot(table, jnp.concatenate([high, low], axis=0))
    size = found.shape[0] // 2
    return found[:size] + found[size:]


def times_paired(value, table):
    high, low = split(value)
    width = table.shape[1] // 2
    first = dot(high, table)
    return first[:, :width] + (first[:, width:] + dot(low, table[:, :width]))


def col_table(packed, index):
    return packed[index * 384 : (index + 1) * 384, :]


def row_table(packed, index):
    start = 768 + index * 384
    return jnp.concatenate(
        [packed[start + i : start + i + 128, :] for i in (0, 128, 256)], axis=1
    )


def wide_table(packed, place):
    start, size = place
    return jnp.concatenate(
        [packed[start : start + size, :], packed[start + size : start + 2 * size, :]], axis=1
    )


def parity(shape):
    index = lax.broadcasted_iota(jnp.int32, shape, 1)
    return (1 - 2 * (index % 2)).astype(jnp.float32)


def is_odd(axis):
    return lax.axis_index(axis) % 2 == 1


def row_parity(shape):
    index = lax.broadcasted_iota(jnp.int32, shape, 0)
    return jnp.where(index < FB // 2, 1.0, -1.0)


def low_lanes(shape):
    return lax.broadcasted_iota(jnp.int32, shape, 1) < FB


def swapped(value):
    return pltpu.roll(value, FB, 1)


def preparation_kernel(own, other, tables, straight, crossed, loaded, semaphore):
    copy = pltpu.make_async_copy(tables, loaded, semaphore)
    copy.start()
    count = own.shape[0]
    lanes = low_lanes((FB, 2 * FB))
    for group, source in enumerate((own, other)):
        for index in range(count):
            spectrum = source[index]
            turned = swapped(spectrum)
            straight[group * count + index] = jnp.where(lanes, spectrum, turned)
            crossed[group * count + index] = jnp.where(lanes, -turned, spectrum)
    copy.wait()


def pack_kernels(kernels, weights, packed, real, imag):
    lanes = low_lanes((FB // 2, 2 * FB))
    for index in range(kernels.shape[0]):
        for row in range(FB // 2):
            place = slice(row * 2 * FB, (row + 1) * 2 * FB)
            real[row : row + 1, :] = kernels[index, 0:1, place]
            imag[row : row + 1, :] = kernels[index, 1:2, place]
        root = jnp.sqrt(jnp.full((FB // 2, 2 * FB), weights[index], jnp.float32))
        re, im = root * real[...], root * imag[...]
        packed[index, : FB // 2] = jnp.where(lanes, re, swapped(im))
        packed[index, FB // 2 :] = jnp.where(lanes, swapped(re), im)


def block_spectra(transmit, tables):
    sign = jnp.where(low_lanes((FB, 2 * FB)), 1.0, -1.0)
    high, low = split(transmit)
    rows = []
    for side in (0, 1):
        lanes = slice(side * HALO, (side + 1) * HALO)
        three = jnp.concatenate([high[:, lanes], low[:, lanes], high[:, lanes]], axis=1)
        rows.append(dot(three, col_table(tables, side)))
    rows = jnp.concatenate(rows, axis=1)
    found = []
    for block in range(transmit.shape[0] // HALO):
        both = table_times(
            row_table(tables, block % 2), rows[block * HALO : (block + 1) * HALO]
        )
        sine = both[FB:]
        turned = [sign * swapped(sine[:, : 2 * FB]), sign * swapped(sine[:, 2 * FB :])]
        found.append(both[:FB] + jnp.concatenate(turned, axis=1))
    return found


def analysis_kernel(
    mask, kernels, weights, tables, total, packed, edge_even, edge_odd, slope, real, imag, sums
):
    step = pl.program_id(0)
    count = total.shape[0]

    @pl.when(step == 0)
    def _():
        sums[...] = jnp.zeros_like(sums)
        pack_kernels(kernels, weights, packed, real, imag)

    transmit = jnp.tanh(mask[...])
    slope[...] = 1.0 - transmit * transmit
    found = block_spectra(transmit, tables)
    flip = row_parity((FB, 4 * FB))
    first = step * PAIR
    for tile in range(PAIR):
        upper, lower = found[2 * tile], found[2 * tile + 1]
        sums[first + tile] += upper
        sums[first + tile + 1] += flip * (upper + lower)
        sums[first + tile + 2] += lower

    @pl.when(step == pl.num_programs(0) - 1)
    def _():
        total[...] = sums[1 : count + 1]
        up, down = sums[0], sums[count + 1]
        odd_row = is_odd("gy")
        edge_even[...] = jnp.where(odd_row, up, down)
        edge_odd[...] = jnp.where(odd_row, down, up)


def merge_kernel(total, near_even, near_odd, share, to_even, to_odd):
    count = share.shape[0]
    odd_row, odd_col = is_odd("gy"), is_odd("gx")
    above = jnp.where(odd_row, near_even[...], near_odd[...])
    below = jnp.where(odd_row, near_odd[...], near_even[...])
    for index in range(count):
        both = total[index]
        if index == 0:
            both = both + above
        if index == count - 1:
            both = both + below
        left, right = both[:, : 2 * FB], both[:, 2 * FB :]
        share[index] = parity((FB, 2 * FB)) * (left + right)
        to_even[index] = jnp.where(odd_col, left, right)
        to_odd[index] = jnp.where(odd_col, right, left)


def imaging_kernel(
    share, from_even, from_odd, straight, crossed, target, wide,
    resist_ref, grad, fields, sides,
):
    count = straight.shape[0] // 2
    sign = jnp.where(low_lanes((HALF, 2 * FB)), 1.0, -1.0)
    tiles = range(share.shape[0])
    weights = []
    intensities = [[] for tile in tiles]

    for tile in tiles:
        spectrum = share[tile] + from_even[tile] + from_odd[tile]
        turned = swapped(spectrum)
        for group in range(2):
            first = group * count
            products = [
                straight[first + i] * spectrum + crossed[first + i] * turned
                for i in range(count)
            ]
            rows = times_table(jnp.concatenate(products, axis=0), wide_table(wide, SPREAD))
            total = jnp.zeros((COARSE, COARSE), jnp.float32)
            for i in range(count):
                both = table_times(
                    wide_table(wide, LIFT)[:, :192], rows[i * FB : (i + 1) * FB]
                )
                cosine, sine = both[:HALF], both[HALF:]
                sine_re, sine_im = sine[:, :COARSE], sine[:, COARSE:]
                cosine_re, cosine_im = cosine[:, :COARSE], cosine[:, COARSE:]
                real = jnp.concatenate([cosine_re - sine_im, cosine_re + sine_im], axis=0)
                imag = jnp.concatenate([cosine_im + sine_re, cosine_im - sine_re], axis=0)
                fields[tile, first + i, :, :COARSE] = real
                fields[tile, first + i, :, COARSE:] = imag
                total = total + (real * real + imag * imag)
            intensities[tile].append(total)

    for tile in tiles:
        intensity = intensities[tile][0] + intensities[tile][1]
        half_fine = times_table(intensity, wide_table(wide, FINE_RIGHT))
        fine = stacked_times(wide_table(wide, FINE_LEFT), half_fine)
        resist = jax.nn.sigmoid(4.0 * (fine - 1.0))
        place = slice(tile * TILE, (tile + 1) * TILE)
        resist_ref[place, :] = resist
        misfit = resist - target[place, :].astype(jnp.float32)
        push = 16.0 * misfit * resist * (1.0 - resist)
        high, low = split(push)
        from_high = dot(wide_table(wide, COARSE_LEFT), high)
        half_coarse = from_high[:COARSE] + (
            from_high[COARSE:] + dot(wide_table(wide, COARSE_LEFT)[:COARSE], low)
        )
        weights.append(times_paired(half_coarse, wide_table(wide, COARSE_RIGHT)))

    for tile in tiles:
        scale = jnp.concatenate([weights[tile], weights[tile]], axis=1)
        adjoint = []
        for group in range(2):
            first = group * count
            scaled = jnp.concatenate(
                [fields[tile, first + i] * scale for i in range(count)], axis=0
            )
            sides[tile, group] = times_paired(scaled, wide_table(wide, GATHER))
            total = jnp.zeros((FB, 2 * FB), jnp.float32)
            for i in range(0, count, 2):
                pair = []
                for j in (i, i + 1):
                    plus = sides[tile, group, j * COARSE : j * COARSE + HALF, :]
                    minus = sides[tile, group, j * COARSE + HALF : (j + 1) * COARSE, :]
                    pair.append(
                        jnp.concatenate([plus + minus, sign * swapped(plus - minus)], axis=0)
                    )
                found = stacked_times(
                    wide_table(wide, FOLD), jnp.concatenate(pair, axis=1)
                )
                for j in (0, 1):
                    part = found[:, j * 2 * FB : (j + 1) * 2 * FB]
                    total = total + (
                        straight[first + i + j] * part - crossed[first + i + j] * swapped(part)
                    )
            adjoint.append(total)
        grad[tile] = adjoint[0] + adjoint[1]


def sides_of(even_in, odd_in, index):
    odd_col = is_odd("gx")
    return (
        jnp.where(odd_col, even_in[index], odd_in[index]),
        jnp.where(odd_col, odd_in[index], even_in[index]),
    )


def synthesis_rows(rows, slope, tables):
    sign = jnp.where(low_lanes((FB, 2 * FB)), -1.0, 1.0)
    flip = row_parity((FB, 4 * FB))
    outer = []
    for index in range(1, len(rows) - 1):
        base = flip * rows[index]
        for part, near in enumerate((rows[index - 1], rows[index + 1])):
            block = base + near
            turned = [sign * swapped(block[:, : 2 * FB]), sign * swapped(block[:, 2 * FB :])]
            stacked = jnp.concatenate([block, jnp.concatenate(turned, axis=1)], axis=0)
            outer.append(table_times(row_table(tables, part), stacked))
    high, low = split(jnp.concatenate(outer, axis=0))
    sides = []
    for side in (0, 1):
        lanes = slice(side * 2 * FB, (side + 1) * 2 * FB)
        three = jnp.concatenate([high[:, lanes], low[:, lanes], high[:, lanes]], axis=1)
        sides.append(dot(three, col_table(tables, side)))
    return jnp.concatenate(sides, axis=1) * slope


def mixed_row(own, even_in, odd_in, index):
    base = parity((FB, 2 * FB)) * own[index]
    from_left, from_right = sides_of(even_in, odd_in, index)
    return jnp.concatenate([base + from_left, base + from_right], axis=1)


def edges_kernel(own, even_in, odd_in, side_even, side_odd):
    first = mixed_row(own, even_in, odd_in, 0)
    last = mixed_row(own, even_in, odd_in, own.shape[0] - 1)
    odd_row = is_odd("gy")
    side_even[...] = jnp.where(odd_row, first, last)
    side_odd[...] = jnp.where(odd_row, last, first)


def inner_kernel(own, even_in, odd_in, slope, tables, result):
    rows = [mixed_row(own, even_in, odd_in, i) for i in range(PAIR - 1, 2 * PAIR + 1)]
    result[...] = synthesis_rows(rows, slope[...], tables)


def outer_kernel(own, even_in, odd_in, near_even, near_odd, slope, tables, partial, result):
    del partial
    count = own.shape[0]
    odd_row = is_odd("gy")

    @pl.when(pl.program_id(0) == 0)
    def _():
        rows = [jnp.where(odd_row, near_even[...], near_odd[...])]
        rows += [mixed_row(own, even_in, odd_in, i) for i in range(PAIR + 1)]
        result[...] = synthesis_rows(rows, slope[...], tables)

    @pl.when(pl.program_id(0) == 1)
    def _():
        rows = [mixed_row(own, even_in, odd_in, i) for i in range(count - PAIR - 1, count)]
        rows += [jnp.where(odd_row, near_odd[...], near_even[...])]
        result[...] = synthesis_rows(rows, slope[...], tables)


def whole(array):
    zeros = (0,) * len(array.shape)
    return pl.BlockSpec(array.shape, lambda step: zeros)


def tile_pair():
    return pl.BlockSpec((PAIR * TILE, TILE), lambda step: (step, 0))


def params(limit=VMEM_LIMIT):
    return pltpu.CompilerParams(dimension_semantics=("arbitrary",), vmem_limit_bytes=limit)


def analysis(mask, kernels, weights):
    tiles = mask.shape[0] // TILE
    tables = jnp.asarray(TABLES["analysis"])
    part = pltpu.VMEM((FB // 2, 2 * FB), jnp.float32)
    total = jax.ShapeDtypeStruct((tiles, FB, 4 * FB), jnp.float32)
    packed = jax.ShapeDtypeStruct((kernels.shape[0], FB, 2 * FB), jnp.float32)
    edge = jax.ShapeDtypeStruct((FB, 4 * FB), jnp.float32)
    return pl.pallas_call(
        analysis_kernel,
        grid=(tiles // PAIR,),
        out_shape=(total, packed, edge, edge, jax.ShapeDtypeStruct(mask.shape, jnp.float32)),
        in_specs=[
            tile_pair(),
            whole(kernels),
            pl.BlockSpec(memory_space=pltpu.SMEM),
            whole(tables),
        ],
        out_specs=[whole(total), whole(packed), whole(edge), whole(edge), tile_pair()],
        scratch_shapes=[part, part, pltpu.VMEM((tiles + 2, FB, 4 * FB), jnp.float32)],
        compiler_params=params(FIRST_LIMIT),
        name="analysis",
    )(mask, kernels, weights, tables)


def simple_call(kernel, out_shape, *operands, name):
    vmem = pl.BlockSpec(memory_space=pltpu.VMEM)
    return pl.pallas_call(
        kernel,
        out_shape=out_shape,
        in_specs=[vmem] * len(operands),
        out_specs=[vmem] * len(out_shape),
        compiler_params=pltpu.CompilerParams(vmem_limit_bytes=VMEM_LIMIT),
        name=name,
    )(*operands)


def merge(total, near_even, near_odd):
    spectra = jax.ShapeDtypeStruct((total.shape[0], FB, 2 * FB), jnp.float32)
    return simple_call(
        merge_kernel, (spectra,) * 3, total, near_even, near_odd, name="merge"
    )


def edges(grad, grad_even, grad_odd):
    side = jax.ShapeDtypeStruct((FB, 4 * FB), jnp.float32)
    return simple_call(edges_kernel, (side,) * 2, grad, grad_even, grad_odd, name="edges")


def preparation(own, other):
    tables = jnp.asarray(TABLES["imaging"])
    shape = jax.ShapeDtypeStruct((2 * own.shape[0], FB, 2 * FB), jnp.float32)
    vmem = pl.BlockSpec(memory_space=pltpu.VMEM)
    return pl.pallas_call(
        preparation_kernel,
        out_shape=(shape, shape, jax.ShapeDtypeStruct(tables.shape, tables.dtype)),
        in_specs=[vmem, vmem, pl.BlockSpec(memory_space=pl.ANY)],
        out_specs=[vmem] * 3,
        scratch_shapes=[pltpu.SemaphoreType.DMA],
        compiler_params=pltpu.CompilerParams(vmem_limit_bytes=VMEM_LIMIT),
        cost_estimate=pl.CostEstimate(flops=400000, bytes_accessed=4000000, transcendentals=0),
        name="preparation",
    )(own, other, tables)


def imaging(share, from_even, from_odd, straight, crossed, tables, target):
    tiles = share.shape[0]
    kernels = straight.shape[0]
    spectra = pl.BlockSpec((TILES_AT_ONCE, FB, 2 * FB), lambda step: (step, 0, 0))
    pixels = pl.BlockSpec((TILES_AT_ONCE * TILE, TILE), lambda step: (step, 0))
    return pl.pallas_call(
        imaging_kernel,
        grid=(tiles // TILES_AT_ONCE,),
        out_shape=(
            jax.ShapeDtypeStruct(target.shape, jnp.float32),
            jax.ShapeDtypeStruct(share.shape, jnp.float32),
        ),
        in_specs=[spectra] * 3 + [whole(straight), whole(crossed), pixels, whole(tables)],
        out_specs=[pixels, spectra],
        scratch_shapes=[
            pltpu.VMEM((TILES_AT_ONCE, kernels, COARSE, 2 * COARSE), jnp.float32),
            pltpu.VMEM((TILES_AT_ONCE, 2, kernels // 2 * COARSE, 2 * FB), jnp.float32),
        ],
        compiler_params=params(),
        name="imaging",
    )(share, from_even, from_odd, straight, crossed, target, tables)


def inner_synthesis(own, even_in, odd_in, slope):
    tables = jnp.asarray(TABLES["synthesis"])
    place = pl.BlockSpec((PAIR * TILE, TILE), lambda step: (1, 0))
    return pl.pallas_call(
        inner_kernel,
        grid=(1,),
        out_shape=jax.ShapeDtypeStruct(slope.shape, jnp.float32),
        in_specs=[whole(own)] * 3 + [place, whole(tables)],
        out_specs=place,
        compiler_params=params(),
        cost_estimate=pl.CostEstimate(
            flops=1500000000, bytes_accessed=2500000, transcendentals=0
        ),
        name="inner_synthesis",
    )(own, even_in, odd_in, slope, tables)


def outer_synthesis(own, even_in, odd_in, near_even, near_odd, slope, partial):
    tables = jnp.asarray(TABLES["synthesis"])
    place = pl.BlockSpec((PAIR * TILE, TILE), lambda step: (2 * step, 0))
    return pl.pallas_call(
        outer_kernel,
        grid=(2,),
        out_shape=jax.ShapeDtypeStruct(slope.shape, jnp.float32),
        in_specs=[whole(own)] * 3
        + [whole(near_even), whole(near_odd), place, whole(tables)]
        + [pl.BlockSpec(memory_space=pl.ANY)],
        out_specs=place,
        input_output_aliases={7: 0},
        compiler_params=params(),
        name="outer_synthesis",
    )(own, even_in, odd_in, near_even, near_odd, slope, tables, partial)


def swap_pairs(count, first):
    pairs = []
    for place in range(first, count - 1, 2):
        pairs += [(place, place + 1), (place + 1, place)]
    return pairs


def local(mask_param, target, kernels, weights):
    rows = lax.axis_size("gy")

    def swap(value, axis, first):
        return lax.ppermute(value, axis, swap_pairs(lax.axis_size(axis), first))

    total, own, edge_even, edge_odd, slope = analysis(mask_param, kernels, weights)
    halo_odd = swap(edge_odd, "gy", 1)
    halo_even = swap(edge_even, "gy", 0)
    inner = rows // 4
    pairs = []
    for place in range(rows):
        mirror = (3 - place // inner) * inner + place % inner
        pairs += [(2 * place, 2 * mirror + 1), (2 * place + 1, 2 * mirror)]
    other = lax.ppermute(own, ("gy", "ka"), pairs)
    share, to_even, to_odd = merge(total, halo_even, halo_odd)
    from_odd = swap(to_odd, "gx", 1)
    from_even = swap(to_even, "gx", 0)
    straight, crossed, tables = preparation(own, other)
    resist, grad = imaging(share, from_even, from_odd, straight, crossed, tables, target)
    grad_odd = swap(grad, "gx", 1)
    grad_even = swap(grad, "gx", 0)
    side_even, side_odd = edges(grad, grad_even, grad_odd)
    near_odd = swap(side_odd, "gy", 1)
    near_even = swap(side_even, "gy", 0)
    partial = inner_synthesis(grad, grad_even, grad_odd, slope)
    gradient = outer_synthesis(
        grad, grad_even, grad_odd, near_even, near_odd, slope, partial
    )
    return (gradient, resist)


def solution(mesh):
    placed = (P("gy", "gx"), P("gy", "gx"), P("ka", None, None), P("ka"))
    return jax.shard_map(
        local, mesh=mesh, in_specs=placed, out_specs=(P("gy", "gx"), P("gy", "gx")), check_vma=False
    )
```

```python
import math

import jax
import jax.numpy as jnp
import ml_dtypes
import numpy as np
from jax import lax
from jax.experimental import pallas as pl
from jax.experimental.pallas import tpu as pltpu
from jax.sharding import PartitionSpec as P

WIN = 512
HALO = 128
FB = 64
TILE = 256
COARSE = 128
HALF = COARSE // 2
VMEM_LIMIT = 32 * 1024 * 1024
PAIR = 2
TILES_AT_ONCE = 3
FIRST_LIMIT = 60 * 1024 * 1024

bf16 = ml_dtypes.bfloat16


def halves(table):
    high = table.astype(np.float32).astype(bf16)
    low = (table - high.astype(np.float64)).astype(np.float32).astype(bf16)
    return high, low


def as_left(table):
    high, low = halves(table)
    return np.concatenate([high, low, high], axis=1)


def as_right(table):
    high, low = halves(table)
    return np.concatenate([high, high, low], axis=0)


def angles(points):
    frequencies = np.arange(FB) - FB // 2
    windings = np.mod(frequencies[:, None] * np.asarray(points)[None, :], WIN)
    return windings * (2.0 * math.pi / WIN)


ORDER = np.concatenate([np.arange(0, FB, 2), np.arange(1, FB, 2)])


def blocks(table):
    return [table[:, i : i + 128] for i in range(0, table.shape[1], 128)]


def make_tables():
    factor = 1.0 / (WIN * FB)
    pixels = np.arange(HALO)
    columns, rows, outs, pixs = [], [], [], []
    for points in (pixels + 3 * HALO, pixels):
        cos, sin = np.cos(angles(points)), np.sin(angles(points))
        columns.append(as_right(np.concatenate([cos.T, -sin.T], axis=1)))
        pixs.append(as_right(np.concatenate([cos, -sin], axis=0)))
        cos, sin = cos[ORDER], sin[ORDER]
        rows += blocks(as_left(factor * np.concatenate([cos, sin], axis=0)))
        outs += blocks(as_left(factor * np.concatenate([cos.T, sin.T], axis=1)))
    plus = 4 * np.arange(HALF) + 2
    samples = np.concatenate([plus, -plus])
    cos, sin = np.cos(angles(samples)), np.sin(angles(samples))
    spread = as_right(
        np.concatenate(
            [np.concatenate([cos, sin], axis=1), np.concatenate([-sin, cos], axis=1)], axis=0
        )
    )
    gather = np.concatenate(
        [np.concatenate([cos.T, -sin.T], axis=1), np.concatenate([sin.T, cos.T], axis=1)], axis=0
    )
    gather = np.concatenate(halves(gather), axis=1)
    cos, sin = np.cos(angles(plus))[ORDER], np.sin(angles(plus))[ORDER]
    lift = as_left(np.concatenate([cos.T, sin.T], axis=0))
    lift = np.concatenate([lift, np.zeros((COARSE, 64), bf16)], axis=1)
    high, low = halves(np.concatenate([cos, sin], axis=1))
    fold = np.concatenate(
        [np.concatenate([high, high], axis=1), np.concatenate([low, 0 * low], axis=1)], axis=0
    )
    offset = (np.arange(TILE) + HALO)[:, None] - samples[None, :]
    orders = np.arange(1, COARSE // 2)
    turns = np.mod(offset[..., None] * orders, WIN) * (2.0 * math.pi / WIN)
    interp = (1.0 + 2.0 * np.cos(turns).sum(-1)) / COARSE
    high, low = halves(interp)
    fine_left = np.concatenate(
        [np.concatenate([high, high], axis=1), np.concatenate([low, 0 * low], axis=1)], axis=0
    )
    coarse_left = np.concatenate(halves(interp.T), axis=0)
    coarse_right = np.concatenate(halves(interp), axis=1)
    return {
        "analysis": np.concatenate(columns + rows, axis=0),
        "synthesis": np.concatenate(pixs + outs, axis=0),
        "imaging": np.concatenate(
            sum(
                map(
                    blocks,
                    (
                        spread, gather, lift, fold, as_right(interp.T), fine_left, coarse_left,
                        coarse_right,
                    ),
                ),
                [],
            ),
            axis=0,
        ),
    }


TABLES = make_tables()
SPREAD, GATHER, LIFT, FOLD, FINE_RIGHT, FINE_LEFT, COARSE_LEFT, COARSE_RIGHT = (
    (2 * a, b - a)
    for a, b in (
        (0, 384), (384, 640), (640, 768), (768, 896), (896, 1280), (1280, 1792), (1792, 2048),
        (2048, 2304),
    )
)


def split(value):
    high = value.astype(jnp.bfloat16)
    low = (value - high.astype(jnp.float32)).astype(jnp.bfloat16)
    return high, low


def dot(left, right):
    return jnp.dot(left, right, preferred_element_type=jnp.float32)


def times_table(value, table):
    high, low = split(value)
    return dot(jnp.concatenate([high, low, high], axis=1), table)


def table_times(table, value):
    high, low = split(value)
    return dot(table, jnp.concatenate([high, high, low], axis=0))


def stacked_times(table, value):
    high, low = split(value)
    found = dot(table, jnp.concatenate([high, low], axis=0))
    size = found.shape[0] // 2
    return found[:size] + found[size:]


def times_paired(value, table):
    high, low = split(value)
    width = table.shape[1] // 2
    first = dot(high, table)
    return first[:, :width] + (first[:, width:] + dot(low, table[:, :width]))


def col_table(packed, index):
    return packed[index * 384 : (index + 1) * 384, :]


def row_table(packed, index):
    start = 768 + index * 384
    return jnp.concatenate(
        [packed[start + i : start + i + 128, :] for i in (0, 128, 256)], axis=1
    )


def wide_table(packed, place):
    start, size = place
    return jnp.concatenate(
        [packed[start : start + size, :], packed[start + size : start + 2 * size, :]], axis=1
    )


def parity(shape):
    index = lax.broadcasted_iota(jnp.int32, shape, 1)
    return (1 - 2 * (index % 2)).astype(jnp.float32)


def is_odd(axis):
    return lax.axis_index(axis) % 2 == 1


def row_parity(shape):
    index = lax.broadcasted_iota(jnp.int32, shape, 0)
    return jnp.where(index < FB // 2, 1.0, -1.0)


def low_lanes(shape):
    return lax.broadcasted_iota(jnp.int32, shape, 1) < FB


def swapped(value):
    return pltpu.roll(value, FB, 1)


def factors(spectrum):
    lanes = low_lanes((FB, 2 * FB))
    turned = swapped(spectrum)
    return jnp.where(lanes, spectrum, turned), jnp.where(lanes, -turned, spectrum)


def own_kernel(own, straight, crossed):
    for index in range(own.shape[0]):
        straight[index], crossed[index] = factors(own[index])


def other_kernel(mine, partners, straight, crossed):
    odd_col = is_odd("gx")
    half = mine.shape[0]
    for index in range(half):
        first = jnp.where(odd_col, partners[index], mine[index])
        second = jnp.where(odd_col, mine[index], partners[index])
        straight[index], crossed[index] = factors(first)
        straight[half + index], crossed[half + index] = factors(second)


def pack_kernels(kernels, weights, packed, real, imag):
    lanes = low_lanes((FB // 2, 2 * FB))
    for index in range(kernels.shape[0]):
        for row in range(FB // 2):
            place = slice(row * 2 * FB, (row + 1) * 2 * FB)
            real[row : row + 1, :] = kernels[index, 0:1, place]
            imag[row : row + 1, :] = kernels[index, 1:2, place]
        root = jnp.sqrt(jnp.full((FB // 2, 2 * FB), weights[index], jnp.float32))
        re, im = root * real[...], root * imag[...]
        packed[index, : FB // 2] = jnp.where(lanes, re, swapped(im))
        packed[index, FB // 2 :] = jnp.where(lanes, swapped(re), im)


def block_spectra(transmit, tables):
    sign = jnp.where(low_lanes((FB, 2 * FB)), 1.0, -1.0)
    high, low = split(transmit)
    rows = []
    for side in (0, 1):
        lanes = slice(side * HALO, (side + 1) * HALO)
        three = jnp.concatenate([high[:, lanes], low[:, lanes], high[:, lanes]], axis=1)
        rows.append(dot(three, col_table(tables, side)))
    rows = jnp.concatenate(rows, axis=1)
    found = []
    for block in range(transmit.shape[0] // HALO):
        both = table_times(
            row_table(tables, block % 2), rows[block * HALO : (block + 1) * HALO]
        )
        sine = both[FB:]
        turned = [sign * swapped(sine[:, : 2 * FB]), sign * swapped(sine[:, 2 * FB :])]
        found.append(both[:FB] + jnp.concatenate(turned, axis=1))
    return found


def analysis_kernel(
    mask_in, kernels_in, weights, tables_in,
    total, packed, half, edge_even, edge_odd, slope,
    real, imag, sums, mask, kernels, tables, semaphores,
):
    step = pl.program_id(0)
    count = total.shape[0]

    def pixels_copy(step):
        place = pl.ds(pl.multiple_of(step * PAIR * TILE, TILE), PAIR * TILE)
        return pltpu.make_async_copy(
            mask_in.at[place, :], mask.at[place, :], semaphores.at[step]
        )

    @pl.when(step == 0)
    def _():
        table_copy = pltpu.make_async_copy(tables_in, tables, semaphores.at[count // PAIR])
        kernel_copy = pltpu.make_async_copy(
            kernels_in, kernels, semaphores.at[count // PAIR + 1]
        )
        kernel_copy.start()
        pixels_copy(0).start()
        table_copy.start()
        for later in range(1, count // PAIR):
            pixels_copy(later).start()
        sums[...] = jnp.zeros_like(sums)
        kernel_copy.wait()
        pack_kernels(kernels, weights, packed, real, imag)
        size = half.shape[0]
        for index in range(size):
            half[index] = jnp.where(is_odd("gx"), packed[size + index], packed[index])
        table_copy.wait()

    pixels_copy(step).wait()
    transmit = jnp.tanh(mask[pl.ds(pl.multiple_of(step * PAIR * TILE, TILE), PAIR * TILE), :])
    slope[...] = 1.0 - transmit * transmit
    found = block_spectra(transmit, tables)
    flip = row_parity((FB, 4 * FB))
    first = step * PAIR
    for tile in range(PAIR):
        upper, lower = found[2 * tile], found[2 * tile + 1]
        sums[first + tile] += upper
        sums[first + tile + 1] += flip * (upper + lower)
        sums[first + tile + 2] += lower

    @pl.when(step == pl.num_programs(0) - 1)
    def _():
        total[...] = sums[1 : count + 1]
        up, down = sums[0], sums[count + 1]
        odd_row = is_odd("gy")
        edge_even[...] = jnp.where(odd_row, up, down)
        edge_odd[...] = jnp.where(odd_row, down, up)


def shares_kernel(total, share, to_even, to_odd):
    odd_col = is_odd("gx")
    for index in range(share.shape[0]):
        left, right = total[index, :, : 2 * FB], total[index, :, 2 * FB :]
        share[index] = parity((FB, 2 * FB)) * (left + right)
        to_even[index] = jnp.where(odd_col, left, right)
        to_odd[index] = jnp.where(odd_col, right, left)


def merge_kernel(
    share_in, to_even_in, to_odd_in, near_even, near_odd, share, to_even, to_odd
):
    count = share.shape[0]
    odd_row, odd_col = is_odd("gy"), is_odd("gx")
    share[...] = share_in[...]
    to_even[...] = to_even_in[...]
    to_odd[...] = to_odd_in[...]
    above = jnp.where(odd_row, near_even[...], near_odd[...])
    below = jnp.where(odd_row, near_odd[...], near_even[...])
    for index, near in ((0, above), (count - 1, below)):
        left, right = near[:, : 2 * FB], near[:, 2 * FB :]
        share[index] += parity((FB, 2 * FB)) * (left + right)
        to_even[index] += jnp.where(odd_col, left, right)
        to_odd[index] += jnp.where(odd_col, right, left)


def imaging_kernel(
    share, from_even, from_odd, straight_own, crossed_own, straight_other, crossed_other,
    target, wide, resist_out, grad, fields, sides, resists, semaphores,
):
    count = straight_own.shape[0]
    straights, crosseds = (straight_own, straight_other), (crossed_own, crossed_other)
    copies = []
    sign = jnp.where(low_lanes((HALF, 2 * FB)), 1.0, -1.0)
    tiles = range(share.shape[0])
    weights = []
    intensities = [[] for tile in tiles]

    for tile in tiles:
        spectrum = share[tile] + from_even[tile] + from_odd[tile]
        turned = swapped(spectrum)
        for group in range(2):
            first = group * count
            products = [
                straights[group][i] * spectrum + crosseds[group][i] * turned
                for i in range(count)
            ]
            rows = times_table(jnp.concatenate(products, axis=0), wide_table(wide, SPREAD))
            total = jnp.zeros((COARSE, COARSE), jnp.float32)
            for i in range(count):
                both = table_times(
                    wide_table(wide, LIFT)[:, :192], rows[i * FB : (i + 1) * FB]
                )
                cosine, sine = both[:HALF], both[HALF:]
                sine_re, sine_im = sine[:, :COARSE], sine[:, COARSE:]
                cosine_re, cosine_im = cosine[:, :COARSE], cosine[:, COARSE:]
                real = jnp.concatenate([cosine_re - sine_im, cosine_re + sine_im], axis=0)
                imag = jnp.concatenate([cosine_im + sine_re, cosine_im - sine_re], axis=0)
                fields[tile, first + i, :, :COARSE] = real
                fields[tile, first + i, :, COARSE:] = imag
                total = total + (real * real + imag * imag)
            intensities[tile].append(total)

    for tile in tiles:
        intensity = intensities[tile][0] + intensities[tile][1]
        half_fine = times_table(intensity, wide_table(wide, FINE_RIGHT))
        fine = stacked_times(wide_table(wide, FINE_LEFT), half_fine)
        resist = jax.nn.sigmoid(4.0 * (fine - 1.0))
        place = slice(tile * TILE, (tile + 1) * TILE)
        resists[place, :] = resist
        start = (pl.program_id(0) * len(tiles) + tile) * TILE
        copy = pltpu.make_async_copy(
            resists.at[pl.ds(tile * TILE, TILE), :],
            resist_out.at[pl.ds(pl.multiple_of(start, TILE), TILE), :],
            semaphores.at[tile],
        )
        copy.start()
        copies.append(copy)
        misfit = resist - target[place, :].astype(jnp.float32)
        push = 16.0 * misfit * resist * (1.0 - resist)
        high, low = split(push)
        from_high = dot(wide_table(wide, COARSE_LEFT), high)
        half_coarse = from_high[:COARSE] + (
            from_high[COARSE:] + dot(wide_table(wide, COARSE_LEFT)[:COARSE], low)
        )
        weights.append(times_paired(half_coarse, wide_table(wide, COARSE_RIGHT)))

    for tile in tiles:
        scale = jnp.concatenate([weights[tile], weights[tile]], axis=1)
        adjoint = []
        for group in range(2):
            first = group * count
            scaled = jnp.concatenate(
                [fields[tile, first + i] * scale for i in range(count)], axis=0
            )
            sides[tile, group] = times_paired(scaled, wide_table(wide, GATHER))
            total = jnp.zeros((FB, 2 * FB), jnp.float32)
            for i in range(0, count, 2):
                pair = []
                for j in (i, i + 1):
                    plus = sides[tile, group, j * COARSE : j * COARSE + HALF, :]
                    minus = sides[tile, group, j * COARSE + HALF : (j + 1) * COARSE, :]
                    pair.append(
                        jnp.concatenate([plus + minus, sign * swapped(plus - minus)], axis=0)
                    )
                found = stacked_times(
                    wide_table(wide, FOLD), jnp.concatenate(pair, axis=1)
                )
                for j in (0, 1):
                    part = found[:, j * 2 * FB : (j + 1) * 2 * FB]
                    total = total + (
                        straights[group][i + j] * part - crosseds[group][i + j] * swapped(part)
                    )
            adjoint.append(total)
        grad[tile] = adjoint[0] + adjoint[1]

    for copy in copies:
        copy.wait()


def sides_of(even_in, odd_in, index):
    odd_col = is_odd("gx")
    return (
        jnp.where(odd_col, even_in[index], odd_in[index]),
        jnp.where(odd_col, odd_in[index], even_in[index]),
    )


def synthesis_rows(rows, slope, tables):
    sign = jnp.where(low_lanes((FB, 2 * FB)), -1.0, 1.0)
    flip = row_parity((FB, 4 * FB))
    outer = []
    for index in range(1, len(rows) - 1):
        base = flip * rows[index]
        for part, near in enumerate((rows[index - 1], rows[index + 1])):
            block = base + near
            turned = [sign * swapped(block[:, : 2 * FB]), sign * swapped(block[:, 2 * FB :])]
            stacked = jnp.concatenate([block, jnp.concatenate(turned, axis=1)], axis=0)
            outer.append(table_times(row_table(tables, part), stacked))
    high, low = split(jnp.concatenate(outer, axis=0))
    sides = []
    for side in (0, 1):
        lanes = slice(side * 2 * FB, (side + 1) * 2 * FB)
        three = jnp.concatenate([high[:, lanes], low[:, lanes], high[:, lanes]], axis=1)
        sides.append(dot(three, col_table(tables, side)))
    return jnp.concatenate(sides, axis=1) * slope


def mixed_row(own, even_in, odd_in, index):
    base = parity((FB, 2 * FB)) * own[index]
    from_left, from_right = sides_of(even_in, odd_in, index)
    return jnp.concatenate([base + from_left, base + from_right], axis=1)


def edges_kernel(own, even_in, odd_in, side_even, side_odd):
    first = mixed_row(own, even_in, odd_in, 0)
    last = mixed_row(own, even_in, odd_in, own.shape[0] - 1)
    odd_row = is_odd("gy")
    side_even[...] = jnp.where(odd_row, first, last)
    side_odd[...] = jnp.where(odd_row, last, first)


def inner_kernel(own, even_in, odd_in, slope, tables, result):
    rows = [mixed_row(own, even_in, odd_in, i) for i in range(PAIR - 1, 2 * PAIR + 1)]
    result[...] = synthesis_rows(rows, slope[...], tables)


def outer_kernel(own, even_in, odd_in, near_even, near_odd, slope, tables, partial, result):
    del partial
    count = own.shape[0]
    odd_row = is_odd("gy")

    @pl.when(pl.program_id(0) == 0)
    def _():
        rows = [jnp.where(odd_row, near_even[...], near_odd[...])]
        rows += [mixed_row(own, even_in, odd_in, i) for i in range(PAIR + 1)]
        result[...] = synthesis_rows(rows, slope[...], tables)

    @pl.when(pl.program_id(0) == 1)
    def _():
        rows = [mixed_row(own, even_in, odd_in, i) for i in range(count - PAIR - 1, count)]
        rows += [jnp.where(odd_row, near_odd[...], near_even[...])]
        result[...] = synthesis_rows(rows, slope[...], tables)


def whole(array):
    zeros = (0,) * len(array.shape)
    return pl.BlockSpec(array.shape, lambda step: zeros)


def tile_pair():
    return pl.BlockSpec((PAIR * TILE, TILE), lambda step: (step, 0))


def params(limit=VMEM_LIMIT):
    return pltpu.CompilerParams(dimension_semantics=("arbitrary",), vmem_limit_bytes=limit)


def analysis(mask, kernels, weights):
    tiles = mask.shape[0] // TILE
    tables = jnp.asarray(TABLES["analysis"])
    part = pltpu.VMEM((FB // 2, 2 * FB), jnp.float32)
    total = jax.ShapeDtypeStruct((tiles, FB, 4 * FB), jnp.float32)
    packed = jax.ShapeDtypeStruct((kernels.shape[0], FB, 2 * FB), jnp.float32)
    half = jax.ShapeDtypeStruct((kernels.shape[0] // 2, FB, 2 * FB), jnp.float32)
    edge = jax.ShapeDtypeStruct((FB, 4 * FB), jnp.float32)
    return pl.pallas_call(
        analysis_kernel,
        grid=(tiles // PAIR,),
        out_shape=(
            total, packed, half, edge, edge, jax.ShapeDtypeStruct(mask.shape, jnp.float32)
        ),
        in_specs=[
            pl.BlockSpec(memory_space=pltpu.HBM),
            pl.BlockSpec(memory_space=pltpu.HBM),
            pl.BlockSpec(memory_space=pltpu.SMEM),
            pl.BlockSpec(memory_space=pltpu.HBM),
        ],
        out_specs=[whole(out) for out in (total, packed, half, edge, edge)] + [tile_pair()],
        scratch_shapes=[
            part,
            part,
            pltpu.VMEM((tiles + 2, FB, 4 * FB), jnp.float32),
            pltpu.VMEM(mask.shape, mask.dtype),
            pltpu.VMEM(kernels.shape, kernels.dtype),
            pltpu.VMEM(tables.shape, tables.dtype),
            pltpu.SemaphoreType.DMA((tiles // PAIR + 2,)),
        ],
        compiler_params=params(FIRST_LIMIT),
        name="analysis",
    )(mask, kernels, weights, tables)


def simple_call(kernel, out_shape, *operands, name):
    vmem = pl.BlockSpec(memory_space=pltpu.VMEM)
    return pl.pallas_call(
        kernel,
        out_shape=out_shape,
        in_specs=[vmem] * len(operands),
        out_specs=[vmem] * len(out_shape),
        compiler_params=pltpu.CompilerParams(vmem_limit_bytes=VMEM_LIMIT),
        name=name,
    )(*operands)


def shares(total):
    spectra = jax.ShapeDtypeStruct((total.shape[0], FB, 2 * FB), jnp.float32)
    return simple_call(shares_kernel, (spectra,) * 3, total, name="shares")


def merge(share, to_even, to_odd, near_even, near_odd):
    spectra = jax.ShapeDtypeStruct(share.shape, jnp.float32)
    return simple_call(
        merge_kernel, (spectra,) * 3, share, to_even, to_odd, near_even, near_odd, name="merge"
    )


def edges(grad, grad_even, grad_odd):
    side = jax.ShapeDtypeStruct((FB, 4 * FB), jnp.float32)
    return simple_call(edges_kernel, (side,) * 2, grad, grad_even, grad_odd, name="edges")


def prepare_own(own):
    shape = jax.ShapeDtypeStruct(own.shape, jnp.float32)
    return simple_call(own_kernel, (shape, shape), own, name="prepare_own")


def prepare_other(mine, partners):
    shape = jax.ShapeDtypeStruct((2 * mine.shape[0],) + mine.shape[1:], jnp.float32)
    return simple_call(other_kernel, (shape, shape), mine, partners, name="prepare_other")


def imaging(share, from_even, from_odd, own, other, target):
    tiles = share.shape[0]
    kernels = 2 * own[0].shape[0]
    tables = jnp.asarray(TABLES["imaging"])
    spectra = pl.BlockSpec((TILES_AT_ONCE, FB, 2 * FB), lambda step: (step, 0, 0))
    pixels = pl.BlockSpec((TILES_AT_ONCE * TILE, TILE), lambda step: (step, 0))
    return pl.pallas_call(
        imaging_kernel,
        grid=(tiles // TILES_AT_ONCE,),
        out_shape=(
            jax.ShapeDtypeStruct(target.shape, jnp.float32),
            jax.ShapeDtypeStruct(share.shape, jnp.float32),
        ),
        in_specs=[spectra] * 3 + [whole(own[0])] * 4 + [pixels, whole(tables)],
        out_specs=[pl.BlockSpec(memory_space=pl.ANY), spectra],
        scratch_shapes=[
            pltpu.VMEM((TILES_AT_ONCE, kernels, COARSE, 2 * COARSE), jnp.float32),
            pltpu.VMEM((TILES_AT_ONCE, 2, kernels // 2 * COARSE, 2 * FB), jnp.float32),
            pltpu.VMEM((TILES_AT_ONCE * TILE, TILE), jnp.float32),
            pltpu.SemaphoreType.DMA((TILES_AT_ONCE,)),
        ],
        compiler_params=params(),
        name="imaging",
    )(share, from_even, from_odd, *own, *other, target, tables)


def inner_synthesis(own, even_in, odd_in, slope):
    tables = jnp.asarray(TABLES["synthesis"])
    place = pl.BlockSpec((PAIR * TILE, TILE), lambda step: (1, 0))
    return pl.pallas_call(
        inner_kernel,
        grid=(1,),
        out_shape=jax.ShapeDtypeStruct(slope.shape, jnp.float32),
        in_specs=[whole(own)] * 3 + [place, whole(tables)],
        out_specs=place,
        compiler_params=params(),
        cost_estimate=pl.CostEstimate(
            flops=1500000000, bytes_accessed=2500000, transcendentals=0
        ),
        name="inner_synthesis",
    )(own, even_in, odd_in, slope, tables)


def outer_synthesis(own, even_in, odd_in, near_even, near_odd, slope, partial):
    tables = jnp.asarray(TABLES["synthesis"])
    place = pl.BlockSpec((PAIR * TILE, TILE), lambda step: (2 * step, 0))
    return pl.pallas_call(
        outer_kernel,
        grid=(2,),
        out_shape=jax.ShapeDtypeStruct(slope.shape, jnp.float32),
        in_specs=[whole(own)] * 3
        + [whole(near_even), whole(near_odd), place, whole(tables)]
        + [pl.BlockSpec(memory_space=pl.ANY)],
        out_specs=place,
        input_output_aliases={7: 0},
        compiler_params=params(),
        name="outer_synthesis",
    )(own, even_in, odd_in, near_even, near_odd, slope, tables, partial)


def swap_pairs(count, first):
    pairs = []
    for place in range(first, count - 1, 2):
        pairs += [(place, place + 1), (place + 1, place)]
    return pairs


def local(mask_param, target, kernels, weights):
    rows = lax.axis_size("gy")

    def swap(value, axis, first):
        return lax.ppermute(value, axis, swap_pairs(lax.axis_size(axis), first))

    total, packed, half, edge_even, edge_odd, slope = analysis(mask_param, kernels, weights)
    inner = rows // 4
    pairs = []
    for place in range(rows):
        mirror = (3 - place // inner) * inner + place % inner
        pairs += [(2 * place, 2 * mirror + 1), (2 * place + 1, 2 * mirror)]
    mine = lax.ppermute(half, ("gy", "ka"), pairs)
    halo_odd = swap(edge_odd, "gy", 1)
    halo_even = swap(edge_even, "gy", 0)
    share, to_even, to_odd = merge(*shares(total), halo_even, halo_odd)
    from_odd = swap(to_odd, "gx", 1)
    from_even = swap(to_even, "gx", 0)
    own = prepare_own(packed)
    partners = swap(mine, "gx", 0)
    other = prepare_other(mine, partners)
    resist, grad = imaging(share, from_even, from_odd, own, other, target)
    grad_odd = swap(grad, "gx", 1)
    grad_even = swap(grad, "gx", 0)
    side_even, side_odd = edges(grad, grad_even, grad_odd)
    near_odd = swap(side_odd, "gy", 1)
    near_even = swap(side_even, "gy", 0)
    partial = inner_synthesis(grad, grad_even, grad_odd, slope)
    gradient = outer_synthesis(
        grad, grad_even, grad_odd, near_even, near_odd, slope, partial
    )
    return (gradient, resist)


def solution(mesh):
    placed = (P("gy", "gx"), P("gy", "gx"), P("ka", None, None), P("ka"))
    return jax.shard_map(
        local, mesh=mesh, in_specs=placed, out_specs=(P("gy", "gx"), P("gy", "gx")), check_vma=False
    )
```

```python
import math

import jax
import jax.numpy as jnp
import ml_dtypes
import numpy as np
from jax import lax
from jax.experimental import pallas as pl
from jax.experimental.pallas import tpu as pltpu
from jax.sharding import PartitionSpec as P

WIN = 512
HALO = 128
FB = 64
TILE = 256
COARSE = 128
HALF = COARSE // 2
VMEM_LIMIT = 40 * 1024 * 1024
PAIR = 2
TILES_AT_ONCE = 6
FIRST_LIMIT = 60 * 1024 * 1024

bf16 = ml_dtypes.bfloat16


def halves(table):
    high = table.astype(np.float32).astype(bf16)
    low = (table - high.astype(np.float64)).astype(np.float32).astype(bf16)
    return high, low


def as_left(table):
    high, low = halves(table)
    return np.concatenate([high, low, high], axis=1)


def as_right(table):
    high, low = halves(table)
    return np.concatenate([high, high, low], axis=0)


def angles(points):
    frequencies = np.arange(FB) - FB // 2
    windings = np.mod(frequencies[:, None] * np.asarray(points)[None, :], WIN)
    return windings * (2.0 * math.pi / WIN)


ORDER = np.concatenate([np.arange(0, FB, 2), np.arange(1, FB, 2)])


def blocks(table):
    return [table[:, i : i + 128] for i in range(0, table.shape[1], 128)]


def make_tables():
    factor = 1.0 / (WIN * FB)
    pixels = np.arange(HALO)
    columns, rows, outs, pixs = [], [], [], []
    for points in (pixels + 3 * HALO, pixels):
        cos, sin = np.cos(angles(points)), np.sin(angles(points))
        columns += halves(np.concatenate([cos.T, -sin.T], axis=1))
        pixs += halves(np.concatenate([cos, -sin], axis=0))
        cos, sin = cos[ORDER], sin[ORDER]
        rows += halves(factor * np.concatenate([cos, sin], axis=0))
        outs += halves(factor * np.concatenate([cos.T, sin.T], axis=1))
    plus = 4 * np.arange(HALF) + 2
    samples = np.concatenate([plus, -plus])
    cos, sin = np.cos(angles(samples)), np.sin(angles(samples))
    spread = as_right(
        np.concatenate(
            [np.concatenate([cos, sin], axis=1), np.concatenate([-sin, cos], axis=1)], axis=0
        )
    )
    gather = np.concatenate(
        [np.concatenate([cos.T, -sin.T], axis=1), np.concatenate([sin.T, cos.T], axis=1)], axis=0
    )
    gather = np.concatenate(halves(gather), axis=1)
    cos, sin = np.cos(angles(plus))[ORDER], np.sin(angles(plus))[ORDER]
    lift = as_left(np.concatenate([cos.T, sin.T], axis=0))
    lift = np.concatenate([lift, np.zeros((COARSE, 64), bf16)], axis=1)
    high, low = halves(np.concatenate([cos, sin], axis=1))
    fold = np.concatenate(
        [np.concatenate([high, high], axis=1), np.concatenate([low, 0 * low], axis=1)], axis=0
    )
    offset = (np.arange(TILE) + HALO)[:, None] - samples[None, :]
    orders = np.arange(1, COARSE // 2)
    turns = np.mod(offset[..., None] * orders, WIN) * (2.0 * math.pi / WIN)
    interp = (1.0 + 2.0 * np.cos(turns).sum(-1)) / COARSE
    high, low = halves(interp)
    fine_left = np.concatenate(
        [np.concatenate([high, high], axis=1), np.concatenate([low, 0 * low], axis=1)], axis=0
    )
    coarse_left = np.concatenate(halves(interp.T), axis=0)
    coarse_right = np.concatenate(halves(interp), axis=1)
    return {
        "analysis": np.concatenate(columns + rows, axis=0),
        "synthesis": np.concatenate(pixs + outs, axis=0),
        "imaging": np.concatenate(
            sum(
                map(
                    blocks,
                    (
                        spread, gather, lift, fold, as_right(interp.T), fine_left, coarse_left,
                        coarse_right,
                    ),
                ),
                [],
            ),
            axis=0,
        ),
    }


TABLES = make_tables()
SPREAD, GATHER, LIFT, FOLD, FINE_RIGHT, FINE_LEFT, COARSE_LEFT, COARSE_RIGHT = (
    (2 * a, b - a)
    for a, b in (
        (0, 384), (384, 640), (640, 768), (768, 896), (896, 1280), (1280, 1792), (1792, 2048),
        (2048, 2304),
    )
)


def split(value):
    high = value.astype(jnp.bfloat16)
    low = (value - high.astype(jnp.float32)).astype(jnp.bfloat16)
    return high, low


def dot(left, right):
    return jnp.dot(left, right, preferred_element_type=jnp.float32)


def times_table(value, table):
    high, low = split(value)
    return dot(jnp.concatenate([high, low, high], axis=1), table)


def table_times(table, value):
    high, low = split(value)
    return dot(table, jnp.concatenate([high, high, low], axis=0))


def stacked_times(table, value):
    high, low = split(value)
    found = dot(table, jnp.concatenate([high, low], axis=0))
    size = found.shape[0] // 2
    return found[:size] + found[size:]


def times_paired(value, table):
    high, low = split(value)
    width = table.shape[1] // 2
    first = dot(high, table)
    return first[:, :width] + (first[:, width:] + dot(low, table[:, :width]))


def square(packed, index):
    return packed[index * 128 : (index + 1) * 128, :]


def times_diagonal(value, packed):
    zeros = jnp.zeros((128, 128), jnp.bfloat16)
    high_table, low_table = (
        jnp.concatenate(
            [
                jnp.concatenate([square(packed, i), zeros], axis=1),
                jnp.concatenate([zeros, square(packed, i + 2)], axis=1),
            ],
            axis=0,
        )
        for i in (0, 1)
    )
    high, low = split(value)
    return dot(
        jnp.concatenate([high, low, high], axis=1),
        jnp.concatenate([high_table, high_table, low_table], axis=0),
    )


def stacked_table(packed, part):
    high, low = square(packed, 4 + 2 * part), square(packed, 5 + 2 * part)
    return jnp.concatenate(
        [
            jnp.concatenate([high, high], axis=1),
            jnp.concatenate([low, jnp.zeros_like(low)], axis=1),
        ],
        axis=0,
    )


def wide_table(packed, place):
    start, size = place
    return jnp.concatenate(
        [packed[start : start + size, :], packed[start + size : start + 2 * size, :]], axis=1
    )


def parity(shape):
    index = lax.broadcasted_iota(jnp.int32, shape, 1)
    return (1 - 2 * (index % 2)).astype(jnp.float32)


def is_odd(axis):
    return lax.axis_index(axis) % 2 == 1


def row_parity(shape):
    index = lax.broadcasted_iota(jnp.int32, shape, 0)
    return jnp.where(index < FB // 2, 1.0, -1.0)


def low_lanes(shape):
    return lax.broadcasted_iota(jnp.int32, shape, 1) < FB


def swapped(value):
    return pltpu.roll(value, FB, 1)


def factors(spectrum):
    lanes = low_lanes((FB, 2 * FB))
    turned = swapped(spectrum)
    return jnp.where(lanes, spectrum, turned), jnp.where(lanes, -turned, spectrum)


def own_kernel(own, straight, crossed):
    for index in range(own.shape[0]):
        straight[index], crossed[index] = factors(own[index])


def other_kernel(mine, partners, straight, crossed):
    odd_col = is_odd("gx")
    half = mine.shape[0]
    for index in range(half):
        first = jnp.where(odd_col, partners[index], mine[index])
        second = jnp.where(odd_col, mine[index], partners[index])
        straight[index], crossed[index] = factors(first)
        straight[half + index], crossed[half + index] = factors(second)


def pack_kernels(kernels, weights, packed, real, imag):
    lanes = low_lanes((FB // 2, 2 * FB))
    for index in range(kernels.shape[0]):
        for row in range(FB // 2):
            place = slice(row * 2 * FB, (row + 1) * 2 * FB)
            real[row : row + 1, :] = kernels[index, 0:1, place]
            imag[row : row + 1, :] = kernels[index, 1:2, place]
        root = jnp.sqrt(jnp.full((FB // 2, 2 * FB), weights[index], jnp.float32))
        re, im = root * real[...], root * imag[...]
        packed[index, : FB // 2] = jnp.where(lanes, re, swapped(im))
        packed[index, FB // 2 :] = jnp.where(lanes, swapped(re), im)


def block_spectra(transmit, tables):
    sign = jnp.where(low_lanes((FB, 2 * FB)), 1.0, -1.0)
    rows = times_diagonal(transmit, tables)
    found = []
    for block in range(transmit.shape[0] // HALO):
        both = stacked_times(
            stacked_table(tables, block % 2), rows[block * HALO : (block + 1) * HALO]
        )
        sine = both[FB:]
        turned = [sign * swapped(sine[:, : 2 * FB]), sign * swapped(sine[:, 2 * FB :])]
        found.append(both[:FB] + jnp.concatenate(turned, axis=1))
    return found


def analysis_kernel(
    mask_in, kernels_in, weights, tables_in,
    total, packed, half, edge_even, edge_odd, slope,
    real, imag, sums, mask, kernels, tables, semaphores,
):
    step = pl.program_id(0)
    count = total.shape[0]

    def pixels_copy(step):
        place = pl.ds(pl.multiple_of(step * PAIR * TILE, TILE), PAIR * TILE)
        return pltpu.make_async_copy(
            mask_in.at[place, :], mask.at[place, :], semaphores.at[step]
        )

    @pl.when(step == 0)
    def _():
        table_copy = pltpu.make_async_copy(tables_in, tables, semaphores.at[count // PAIR])
        kernel_copy = pltpu.make_async_copy(
            kernels_in, kernels, semaphores.at[count // PAIR + 1]
        )
        kernel_copy.start()
        pixels_copy(0).start()
        table_copy.start()
        for later in range(1, count // PAIR):
            pixels_copy(later).start()
        sums[...] = jnp.zeros_like(sums)
        kernel_copy.wait()
        pack_kernels(kernels, weights, packed, real, imag)
        size = half.shape[0]
        for index in range(size):
            half[index] = jnp.where(is_odd("gx"), packed[size + index], packed[index])
        table_copy.wait()

    pixels_copy(step).wait()
    transmit = jnp.tanh(mask[pl.ds(pl.multiple_of(step * PAIR * TILE, TILE), PAIR * TILE), :])
    slope[...] = 1.0 - transmit * transmit
    found = block_spectra(transmit, tables)
    flip = row_parity((FB, 4 * FB))
    first = step * PAIR
    for tile in range(PAIR):
        upper, lower = found[2 * tile], found[2 * tile + 1]
        sums[first + tile] += upper
        sums[first + tile + 1] += flip * (upper + lower)
        sums[first + tile + 2] += lower

    @pl.when(step == pl.num_programs(0) - 1)
    def _():
        total[...] = sums[1 : count + 1]
        up, down = sums[0], sums[count + 1]
        odd_row = is_odd("gy")
        edge_even[...] = jnp.where(odd_row, up, down)
        edge_odd[...] = jnp.where(odd_row, down, up)


def shares_kernel(total, share, to_even, to_odd):
    odd_col = is_odd("gx")
    for index in range(share.shape[0]):
        left, right = total[index, :, : 2 * FB], total[index, :, 2 * FB :]
        share[index] = parity((FB, 2 * FB)) * (left + right)
        to_even[index] = jnp.where(odd_col, left, right)
        to_odd[index] = jnp.where(odd_col, right, left)


def merge_kernel(
    share_in, to_even_in, to_odd_in, near_even, near_odd, share, to_even, to_odd
):
    count = share.shape[0]
    odd_row, odd_col = is_odd("gy"), is_odd("gx")
    share[...] = share_in[...]
    to_even[...] = to_even_in[...]
    to_odd[...] = to_odd_in[...]
    above = jnp.where(odd_row, near_even[...], near_odd[...])
    below = jnp.where(odd_row, near_odd[...], near_even[...])
    for index, near in ((0, above), (count - 1, below)):
        left, right = near[:, : 2 * FB], near[:, 2 * FB :]
        share[index] += parity((FB, 2 * FB)) * (left + right)
        to_even[index] += jnp.where(odd_col, left, right)
        to_odd[index] += jnp.where(odd_col, right, left)


def imaging_kernel(
    share, from_even, from_odd, straight_own, crossed_own, straight_other, crossed_other,
    target, wide, resist_out, grad, fields, sides, resists, semaphores,
):
    count = straight_own.shape[0]
    straights, crosseds = (straight_own, straight_other), (crossed_own, crossed_other)
    copies = []
    sign = jnp.where(low_lanes((HALF, 2 * FB)), 1.0, -1.0)
    tiles = range(share.shape[0])
    weights = []
    intensities = [[] for tile in tiles]

    for tile in tiles:
        spectrum = share[tile] + from_even[tile] + from_odd[tile]
        turned = swapped(spectrum)
        for group in range(2):
            first = group * count
            products = [
                straights[group][i] * spectrum + crosseds[group][i] * turned
                for i in range(count)
            ]
            rows = times_table(jnp.concatenate(products, axis=0), wide_table(wide, SPREAD))
            total = jnp.zeros((COARSE, COARSE), jnp.float32)
            for i in range(count):
                both = table_times(
                    wide_table(wide, LIFT)[:, :192], rows[i * FB : (i + 1) * FB]
                )
                cosine, sine = both[:HALF], both[HALF:]
                sine_re, sine_im = sine[:, :COARSE], sine[:, COARSE:]
                cosine_re, cosine_im = cosine[:, :COARSE], cosine[:, COARSE:]
                real = jnp.concatenate([cosine_re - sine_im, cosine_re + sine_im], axis=0)
                imag = jnp.concatenate([cosine_im + sine_re, cosine_im - sine_re], axis=0)
                fields[tile, first + i, :, :COARSE] = real
                fields[tile, first + i, :, COARSE:] = imag
                total = total + (real * real + imag * imag)
            intensities[tile].append(total)

    for tile in tiles:
        intensity = intensities[tile][0] + intensities[tile][1]
        half_fine = times_table(intensity, wide_table(wide, FINE_RIGHT))
        fine = stacked_times(wide_table(wide, FINE_LEFT), half_fine)
        resist = jax.nn.sigmoid(4.0 * (fine - 1.0))
        place = slice(tile * TILE, (tile + 1) * TILE)
        resists[place, :] = resist
        start = (pl.program_id(0) * len(tiles) + tile) * TILE
        copy = pltpu.make_async_copy(
            resists.at[pl.ds(tile * TILE, TILE), :],
            resist_out.at[pl.ds(pl.multiple_of(start, TILE), TILE), :],
            semaphores.at[tile],
        )
        copy.start()
        copies.append(copy)
        misfit = resist - target[place, :].astype(jnp.float32)
        push = 16.0 * misfit * resist * (1.0 - resist)
        high, low = split(push)
        from_high = dot(wide_table(wide, COARSE_LEFT), high)
        half_coarse = from_high[:COARSE] + (
            from_high[COARSE:] + dot(wide_table(wide, COARSE_LEFT)[:COARSE], low)
        )
        weights.append(times_paired(half_coarse, wide_table(wide, COARSE_RIGHT)))

    for tile in tiles:
        scale = jnp.concatenate([weights[tile], weights[tile]], axis=1)
        adjoint = []
        for group in range(2):
            first = group * count
            scaled = jnp.concatenate(
                [fields[tile, first + i] * scale for i in range(count)], axis=0
            )
            sides[tile, group] = times_paired(scaled, wide_table(wide, GATHER))
            total = jnp.zeros((FB, 2 * FB), jnp.float32)
            for i in range(0, count, 2):
                pair = []
                for j in (i, i + 1):
                    plus = sides[tile, group, j * COARSE : j * COARSE + HALF, :]
                    minus = sides[tile, group, j * COARSE + HALF : (j + 1) * COARSE, :]
                    pair.append(
                        jnp.concatenate([plus + minus, sign * swapped(plus - minus)], axis=0)
                    )
                found = stacked_times(
                    wide_table(wide, FOLD), jnp.concatenate(pair, axis=1)
                )
                for j in (0, 1):
                    part = found[:, j * 2 * FB : (j + 1) * 2 * FB]
                    total = total + (
                        straights[group][i + j] * part - crosseds[group][i + j] * swapped(part)
                    )
            adjoint.append(total)
        grad[tile] = adjoint[0] + adjoint[1]

    for copy in copies:
        copy.wait()


def sides_of(even_in, odd_in, index):
    odd_col = is_odd("gx")
    return (
        jnp.where(odd_col, even_in[index], odd_in[index]),
        jnp.where(odd_col, odd_in[index], even_in[index]),
    )


def synthesis_rows(rows, slope, tables):
    sign = jnp.where(low_lanes((FB, 2 * FB)), -1.0, 1.0)
    flip = row_parity((FB, 4 * FB))
    outer = []
    for index in range(1, len(rows) - 1):
        base = flip * rows[index]
        for part, near in enumerate((rows[index - 1], rows[index + 1])):
            block = base + near
            turned = [sign * swapped(block[:, : 2 * FB]), sign * swapped(block[:, 2 * FB :])]
            stacked = jnp.concatenate([block, jnp.concatenate(turned, axis=1)], axis=0)
            outer.append(stacked_times(stacked_table(tables, part), stacked))
    return times_diagonal(jnp.concatenate(outer, axis=0), tables) * slope


def mixed_row(own, even_in, odd_in, index):
    base = parity((FB, 2 * FB)) * own[index]
    from_left, from_right = sides_of(even_in, odd_in, index)
    return jnp.concatenate([base + from_left, base + from_right], axis=1)


def edges_kernel(own, even_in, odd_in, side_even, side_odd):
    first = mixed_row(own, even_in, odd_in, 0)
    last = mixed_row(own, even_in, odd_in, own.shape[0] - 1)
    odd_row = is_odd("gy")
    side_even[...] = jnp.where(odd_row, first, last)
    side_odd[...] = jnp.where(odd_row, last, first)


def write_rows(values, result, first, buffer, semaphore):
    buffer[...] = values
    copy = pltpu.make_async_copy(
        buffer, result.at[pl.ds(first, values.shape[0]), :], semaphore
    )
    copy.start()
    return copy


def inner_kernel(own, even_in, odd_in, slope, tables, result, buffer, semaphore):
    count = own.shape[0]
    rows = [mixed_row(own, even_in, odd_in, i) for i in range(count)]
    values = synthesis_rows(rows, slope[TILE : (count - 1) * TILE, :], tables)
    write_rows(values, result, TILE, buffer, semaphore).wait()


def outer_kernel(
    own, even_in, odd_in, near_even, near_odd, slope, tables, partial, result, buffers,
    semaphores,
):
    del partial
    count = own.shape[0]
    odd_row = is_odd("gy")
    above = jnp.where(odd_row, near_even[...], near_odd[...])
    below = jnp.where(odd_row, near_odd[...], near_even[...])
    rows = [mixed_row(own, even_in, odd_in, i) for i in (0, 1, count - 2, count - 1)]
    last = (count - 1) * TILE
    copies = []
    for index, first, near in ((0, 0, [above] + rows[:2]), (1, last, rows[2:] + [below])):
        values = synthesis_rows(near, slope[first : first + TILE, :], tables)
        copies.append(
            write_rows(values, result, first, buffers.at[index], semaphores.at[index])
        )
    for copy in copies:
        copy.wait()


def whole(array):
    zeros = (0,) * len(array.shape)
    return pl.BlockSpec(array.shape, lambda step: zeros)


def tile_pair():
    return pl.BlockSpec((PAIR * TILE, TILE), lambda step: (step, 0))


def params(limit=VMEM_LIMIT):
    return pltpu.CompilerParams(dimension_semantics=("arbitrary",), vmem_limit_bytes=limit)


def analysis(mask, kernels, weights):
    tiles = mask.shape[0] // TILE
    tables = jnp.asarray(TABLES["analysis"])
    part = pltpu.VMEM((FB // 2, 2 * FB), jnp.float32)
    total = jax.ShapeDtypeStruct((tiles, FB, 4 * FB), jnp.float32)
    packed = jax.ShapeDtypeStruct((kernels.shape[0], FB, 2 * FB), jnp.float32)
    half = jax.ShapeDtypeStruct((kernels.shape[0] // 2, FB, 2 * FB), jnp.float32)
    edge = jax.ShapeDtypeStruct((FB, 4 * FB), jnp.float32)
    return pl.pallas_call(
        analysis_kernel,
        grid=(tiles // PAIR,),
        out_shape=(
            total, packed, half, edge, edge, jax.ShapeDtypeStruct(mask.shape, jnp.float32)
        ),
        in_specs=[
            pl.BlockSpec(memory_space=pltpu.HBM),
            pl.BlockSpec(memory_space=pltpu.HBM),
            pl.BlockSpec(memory_space=pltpu.SMEM),
            pl.BlockSpec(memory_space=pltpu.HBM),
        ],
        out_specs=[whole(out) for out in (total, packed, half, edge, edge)] + [tile_pair()],
        scratch_shapes=[
            part,
            part,
            pltpu.VMEM((tiles + 2, FB, 4 * FB), jnp.float32),
            pltpu.VMEM(mask.shape, mask.dtype),
            pltpu.VMEM(kernels.shape, kernels.dtype),
            pltpu.VMEM(tables.shape, tables.dtype),
            pltpu.SemaphoreType.DMA((tiles // PAIR + 2,)),
        ],
        compiler_params=params(FIRST_LIMIT),
        name="analysis",
    )(mask, kernels, weights, tables)


def simple_call(kernel, out_shape, *operands, name):
    vmem = pl.BlockSpec(memory_space=pltpu.VMEM)
    return pl.pallas_call(
        kernel,
        out_shape=out_shape,
        in_specs=[vmem] * len(operands),
        out_specs=[vmem] * len(out_shape),
        compiler_params=pltpu.CompilerParams(vmem_limit_bytes=VMEM_LIMIT),
        name=name,
    )(*operands)


def shares(total):
    spectra = jax.ShapeDtypeStruct((total.shape[0], FB, 2 * FB), jnp.float32)
    return simple_call(shares_kernel, (spectra,) * 3, total, name="shares")


def merge(share, to_even, to_odd, near_even, near_odd):
    spectra = jax.ShapeDtypeStruct(share.shape, jnp.float32)
    return simple_call(
        merge_kernel, (spectra,) * 3, share, to_even, to_odd, near_even, near_odd, name="merge"
    )


def edges(grad, grad_even, grad_odd):
    side = jax.ShapeDtypeStruct((FB, 4 * FB), jnp.float32)
    return simple_call(edges_kernel, (side,) * 2, grad, grad_even, grad_odd, name="edges")


def prepare_own(own):
    shape = jax.ShapeDtypeStruct(own.shape, jnp.float32)
    return simple_call(own_kernel, (shape, shape), own, name="prepare_own")


def prepare_other(mine, partners):
    shape = jax.ShapeDtypeStruct((2 * mine.shape[0],) + mine.shape[1:], jnp.float32)
    return simple_call(other_kernel, (shape, shape), mine, partners, name="prepare_other")


def imaging(share, from_even, from_odd, own, other, target):
    tiles = share.shape[0]
    kernels = 2 * own[0].shape[0]
    tables = jnp.asarray(TABLES["imaging"])
    spectra = pl.BlockSpec((TILES_AT_ONCE, FB, 2 * FB), lambda step: (step, 0, 0))
    pixels = pl.BlockSpec((TILES_AT_ONCE * TILE, TILE), lambda step: (step, 0))
    return pl.pallas_call(
        imaging_kernel,
        grid=(tiles // TILES_AT_ONCE,),
        out_shape=(
            jax.ShapeDtypeStruct(target.shape, jnp.float32),
            jax.ShapeDtypeStruct(share.shape, jnp.float32),
        ),
        in_specs=[spectra] * 3 + [whole(own[0])] * 4 + [pixels, whole(tables)],
        out_specs=[pl.BlockSpec(memory_space=pl.ANY), spectra],
        scratch_shapes=[
            pltpu.VMEM((TILES_AT_ONCE, kernels, COARSE, 2 * COARSE), jnp.float32),
            pltpu.VMEM((TILES_AT_ONCE, 2, kernels // 2 * COARSE, 2 * FB), jnp.float32),
            pltpu.VMEM((TILES_AT_ONCE * TILE, TILE), jnp.float32),
            pltpu.SemaphoreType.DMA((TILES_AT_ONCE,)),
        ],
        compiler_params=params(),
        name="imaging",
    )(share, from_even, from_odd, *own, *other, target, tables)


def inner_synthesis(own, even_in, odd_in, slope):
    tables = jnp.asarray(TABLES["synthesis"])
    vmem = pl.BlockSpec(memory_space=pltpu.VMEM)
    return pl.pallas_call(
        inner_kernel,
        out_shape=jax.ShapeDtypeStruct(slope.shape, jnp.float32),
        in_specs=[vmem] * 5,
        out_specs=pl.BlockSpec(memory_space=pl.ANY),
        scratch_shapes=[
            pltpu.VMEM((slope.shape[0] - 2 * TILE, TILE), jnp.float32),
            pltpu.SemaphoreType.DMA,
        ],
        compiler_params=pltpu.CompilerParams(vmem_limit_bytes=VMEM_LIMIT),
        cost_estimate=pl.CostEstimate(
            flops=1500000000, bytes_accessed=2500000, transcendentals=0
        ),
        name="inner_synthesis",
    )(own, even_in, odd_in, slope, tables)


def outer_synthesis(own, even_in, odd_in, near_even, near_odd, slope, partial):
    tables = jnp.asarray(TABLES["synthesis"])
    vmem = pl.BlockSpec(memory_space=pltpu.VMEM)
    return pl.pallas_call(
        outer_kernel,
        out_shape=jax.ShapeDtypeStruct(slope.shape, jnp.float32),
        in_specs=[vmem] * 7 + [pl.BlockSpec(memory_space=pl.ANY)],
        out_specs=pl.BlockSpec(memory_space=pl.ANY),
        input_output_aliases={7: 0},
        scratch_shapes=[
            pltpu.VMEM((2, TILE, TILE), jnp.float32),
            pltpu.SemaphoreType.DMA((2,)),
        ],
        compiler_params=pltpu.CompilerParams(vmem_limit_bytes=VMEM_LIMIT),
        name="outer_synthesis",
    )(own, even_in, odd_in, near_even, near_odd, slope, tables, partial)


def swap_pairs(count, first):
    pairs = []
    for place in range(first, count - 1, 2):
        pairs += [(place, place + 1), (place + 1, place)]
    return pairs


def local(mask_param, target, kernels, weights):
    rows = lax.axis_size("gy")

    def swap(value, axis, first):
        return lax.ppermute(value, axis, swap_pairs(lax.axis_size(axis), first))

    total, packed, half, edge_even, edge_odd, slope = analysis(mask_param, kernels, weights)
    inner = rows // 4
    pairs = []
    for place in range(rows):
        mirror = (3 - place // inner) * inner + place % inner
        pairs += [(2 * place, 2 * mirror + 1), (2 * place + 1, 2 * mirror)]
    mine = lax.ppermute(half, ("gy", "ka"), pairs)
    halo_odd = swap(edge_odd, "gy", 1)
    halo_even = swap(edge_even, "gy", 0)
    share, to_even, to_odd = merge(*shares(total), halo_even, halo_odd)
    from_odd = swap(to_odd, "gx", 1)
    from_even = swap(to_even, "gx", 0)
    own = prepare_own(packed)
    partners = swap(mine, "gx", 0)
    other = prepare_other(mine, partners)
    resist, grad = imaging(share, from_even, from_odd, own, other, target)
    grad_odd = swap(grad, "gx", 1)
    grad_even = swap(grad, "gx", 0)
    side_even, side_odd = edges(grad, grad_even, grad_odd)
    near_odd = swap(side_odd, "gy", 1)
    near_even = swap(side_even, "gy", 0)
    partial = inner_synthesis(grad, grad_even, grad_odd, slope)
    gradient = outer_synthesis(
        grad, grad_even, grad_odd, near_even, near_odd, slope, partial
    )
    return (gradient, resist)


def solution(mesh):
    placed = (P("gy", "gx"), P("gy", "gx"), P("ka", None, None), P("ka"))
    return jax.shard_map(
        local, mesh=mesh, in_specs=placed, out_specs=(P("gy", "gx"), P("gy", "gx")), check_vma=False
    )
```

```python
import math

import jax
import jax.numpy as jnp
import ml_dtypes
import numpy as np
from jax import lax
from jax.experimental import pallas as pl
from jax.experimental.pallas import tpu as pltpu
from jax.sharding import PartitionSpec as P

WIN = 512
HALO = 128
FB = 64
TILE = 256
COARSE = 128
HALF = COARSE // 2
VMEM_LIMIT = 40 * 1024 * 1024
PAIR = 3
TILES_AT_ONCE = 3
FIRST_LIMIT = 60 * 1024 * 1024

bf16 = ml_dtypes.bfloat16


def halves(table):
    high = table.astype(np.float32).astype(bf16)
    low = (table - high.astype(np.float64)).astype(np.float32).astype(bf16)
    return high, low


def as_left(table):
    high, low = halves(table)
    return np.concatenate([high, low, high], axis=1)


def as_right(table):
    high, low = halves(table)
    return np.concatenate([high, high, low], axis=0)


def angles(points):
    frequencies = np.arange(FB) - FB // 2
    windings = np.mod(frequencies[:, None] * np.asarray(points)[None, :], WIN)
    return windings * (2.0 * math.pi / WIN)


ORDER = np.concatenate([np.arange(0, FB, 2), np.arange(1, FB, 2)])


def blocks(table):
    return [table[:, i : i + 128] for i in range(0, table.shape[1], 128)]


def make_tables():
    factor = 1.0 / (WIN * FB)
    pixels = np.arange(HALO)
    columns, rows, outs, pixs = [], [], [], []
    for points in (pixels + 3 * HALO, pixels):
        cos, sin = np.cos(angles(points)), np.sin(angles(points))
        columns += halves(np.concatenate([cos.T, -sin.T], axis=1))
        pixs += halves(np.concatenate([cos, -sin], axis=0))
        cos, sin = cos[ORDER], sin[ORDER]
        rows += halves(factor * np.concatenate([cos, sin], axis=0))
        outs += halves(factor * np.concatenate([cos.T, sin.T], axis=1))
    plus = 4 * np.arange(HALF) + 2
    samples = np.concatenate([plus, -plus])
    cos, sin = np.cos(angles(samples)), np.sin(angles(samples))
    spread = as_right(
        np.concatenate(
            [np.concatenate([cos, sin], axis=1), np.concatenate([-sin, cos], axis=1)], axis=0
        )
    )
    gather = np.concatenate(
        [np.concatenate([cos.T, -sin.T], axis=1), np.concatenate([sin.T, cos.T], axis=1)], axis=0
    )
    gather = np.concatenate(halves(gather), axis=1)
    cos, sin = np.cos(angles(plus))[ORDER], np.sin(angles(plus))[ORDER]
    lift = as_left(np.concatenate([cos.T, sin.T], axis=0))
    lift = np.concatenate([lift, np.zeros((COARSE, 64), bf16)], axis=1)
    high, low = halves(np.concatenate([cos, sin], axis=1))
    fold = np.concatenate(
        [np.concatenate([high, high], axis=1), np.concatenate([low, 0 * low], axis=1)], axis=0
    )
    offset = (np.arange(TILE) + HALO)[:, None] - samples[None, :]
    orders = np.arange(1, COARSE // 2)
    turns = np.mod(offset[..., None] * orders, WIN) * (2.0 * math.pi / WIN)
    interp = (1.0 + 2.0 * np.cos(turns).sum(-1)) / COARSE
    high, low = halves(interp)
    fine_left = np.concatenate(
        [np.concatenate([high, high], axis=1), np.concatenate([low, 0 * low], axis=1)], axis=0
    )
    coarse_left = np.concatenate(halves(interp.T), axis=0)
    coarse_right = np.concatenate(halves(interp), axis=1)
    return {
        "analysis": np.concatenate(columns + rows, axis=0),
        "synthesis": np.concatenate(pixs + outs, axis=0),
        "imaging": np.concatenate(
            sum(
                map(
                    blocks,
                    (
                        spread, gather, lift, fold, as_right(interp.T), fine_left, coarse_left,
                        coarse_right,
                    ),
                ),
                [],
            ),
            axis=0,
        ),
    }


TABLES = make_tables()
SPREAD, GATHER, LIFT, FOLD, FINE_RIGHT, FINE_LEFT, COARSE_LEFT, COARSE_RIGHT = (
    (2 * a, b - a)
    for a, b in (
        (0, 384), (384, 640), (640, 768), (768, 896), (896, 1280), (1280, 1792), (1792, 2048),
        (2048, 2304),
    )
)


def split(value):
    high = value.astype(jnp.bfloat16)
    low = (value - high.astype(jnp.float32)).astype(jnp.bfloat16)
    return high, low


def dot(left, right):
    return jnp.dot(left, right, preferred_element_type=jnp.float32)


def times_table(value, table):
    high, low = split(value)
    return dot(jnp.concatenate([high, low, high], axis=1), table)


def table_times(table, value):
    high, low = split(value)
    return dot(table, jnp.concatenate([high, high, low], axis=0))


def stacked_times(table, value):
    high, low = split(value)
    found = dot(table, jnp.concatenate([high, low], axis=0))
    size = found.shape[0] // 2
    return found[:size] + found[size:]


def times_paired(value, table):
    high, low = split(value)
    width = table.shape[1] // 2
    first = dot(high, table)
    return first[:, :width] + (first[:, width:] + dot(low, table[:, :width]))


def square(packed, index):
    return packed[index * 128 : (index + 1) * 128, :]


def times_sides(value, packed):
    high, low = split(value)
    found = []
    for side in (0, 1):
        lanes = slice(side * 128, (side + 1) * 128)
        first, second = square(packed, 2 * side), square(packed, 2 * side + 1)
        found.append(
            dot(
                jnp.concatenate([high[:, lanes], low[:, lanes], high[:, lanes]], axis=1),
                jnp.concatenate([first, first, second], axis=0),
            )
        )
    return jnp.concatenate(found, axis=1)


def times_diagonal(value, packed):
    zeros = jnp.zeros((128, 128), jnp.bfloat16)
    high_table, low_table = (
        jnp.concatenate(
            [
                jnp.concatenate([square(packed, i), zeros], axis=1),
                jnp.concatenate([zeros, square(packed, i + 2)], axis=1),
            ],
            axis=0,
        )
        for i in (0, 1)
    )
    high, low = split(value)
    return dot(
        jnp.concatenate([high, low, high], axis=1),
        jnp.concatenate([high_table, high_table, low_table], axis=0),
    )


def stacked_table(packed, part):
    high, low = square(packed, 4 + 2 * part), square(packed, 5 + 2 * part)
    return jnp.concatenate(
        [
            jnp.concatenate([high, high], axis=1),
            jnp.concatenate([low, jnp.zeros_like(low)], axis=1),
        ],
        axis=0,
    )


def wide_table(packed, place):
    start, size = place
    return jnp.concatenate(
        [packed[start : start + size, :], packed[start + size : start + 2 * size, :]], axis=1
    )


def parity(shape):
    index = lax.broadcasted_iota(jnp.int32, shape, 1)
    return (1 - 2 * (index % 2)).astype(jnp.float32)


def is_odd(axis):
    return lax.axis_index(axis) % 2 == 1


def row_parity(shape):
    index = lax.broadcasted_iota(jnp.int32, shape, 0)
    return jnp.where(index < FB // 2, 1.0, -1.0)


def low_lanes(shape):
    return lax.broadcasted_iota(jnp.int32, shape, 1) < FB


def swapped(value):
    return pltpu.roll(value, FB, 1)


def factors(spectrum):
    lanes = low_lanes((FB, 2 * FB))
    turned = swapped(spectrum)
    return jnp.where(lanes, spectrum, turned), jnp.where(lanes, -turned, spectrum)


def own_kernel(own, straight, crossed):
    for index in range(own.shape[0]):
        straight[index], crossed[index] = factors(own[index])


def other_kernel(mine, partners, straight, crossed):
    odd_col = is_odd("gx")
    half = mine.shape[0]
    for index in range(half):
        first = jnp.where(odd_col, partners[index], mine[index])
        second = jnp.where(odd_col, mine[index], partners[index])
        straight[index], crossed[index] = factors(first)
        straight[half + index], crossed[half + index] = factors(second)


def pack_kernels(kernels, weights, packed, real, imag):
    lanes = low_lanes((FB // 2, 2 * FB))
    for index in range(kernels.shape[0]):
        for row in range(FB // 2):
            place = slice(row * 2 * FB, (row + 1) * 2 * FB)
            real[row : row + 1, :] = kernels[index, 0:1, place]
            imag[row : row + 1, :] = kernels[index, 1:2, place]
        root = jnp.sqrt(jnp.full((FB // 2, 2 * FB), weights[index], jnp.float32))
        re, im = root * real[...], root * imag[...]
        packed[index, : FB // 2] = jnp.where(lanes, re, swapped(im))
        packed[index, FB // 2 :] = jnp.where(lanes, swapped(re), im)


def block_spectra(transmit, tables):
    sign = jnp.where(low_lanes((FB, 2 * FB)), 1.0, -1.0)
    rows = times_sides(transmit, tables)
    found = []
    for block in range(transmit.shape[0] // HALO):
        first = square(tables, 4 + 2 * (block % 2))
        second = square(tables, 5 + 2 * (block % 2))
        both = table_times(
            jnp.concatenate([first, second, first], axis=1),
            rows[block * HALO : (block + 1) * HALO],
        )
        sine = both[FB:]
        turned = [sign * swapped(sine[:, : 2 * FB]), sign * swapped(sine[:, 2 * FB :])]
        found.append(both[:FB] + jnp.concatenate(turned, axis=1))
    return found


def analysis_kernel(
    mask_in, kernels_in, weights, tables_in,
    total, packed, half, edge_even, edge_odd, slope,
    real, imag, sums, mask, kernels, tables, semaphores,
):
    step = pl.program_id(0)
    count = total.shape[0]

    def pixels_copy(step):
        place = pl.ds(pl.multiple_of(step * PAIR * TILE, TILE), PAIR * TILE)
        return pltpu.make_async_copy(
            mask_in.at[place, :], mask.at[place, :], semaphores.at[step]
        )

    @pl.when(step == 0)
    def _():
        table_copy = pltpu.make_async_copy(tables_in, tables, semaphores.at[count // PAIR])
        kernel_copy = pltpu.make_async_copy(
            kernels_in, kernels, semaphores.at[count // PAIR + 1]
        )
        kernel_copy.start()
        pixels_copy(0).start()
        table_copy.start()
        for later in range(1, count // PAIR):
            pixels_copy(later).start()
        sums[...] = jnp.zeros_like(sums)
        kernel_copy.wait()
        pack_kernels(kernels, weights, packed, real, imag)
        size = half.shape[0]
        for index in range(size):
            half[index] = jnp.where(is_odd("gx"), packed[size + index], packed[index])
        table_copy.wait()

    pixels_copy(step).wait()
    transmit = jnp.tanh(mask[pl.ds(pl.multiple_of(step * PAIR * TILE, TILE), PAIR * TILE), :])
    slope[...] = 1.0 - transmit * transmit
    found = block_spectra(transmit, tables)
    flip = row_parity((FB, 4 * FB))
    first = step * PAIR
    for tile in range(PAIR):
        upper, lower = found[2 * tile], found[2 * tile + 1]
        sums[first + tile] += upper
        sums[first + tile + 1] += flip * (upper + lower)
        sums[first + tile + 2] += lower

    @pl.when(step == pl.num_programs(0) - 1)
    def _():
        total[...] = sums[1 : count + 1]
        up, down = sums[0], sums[count + 1]
        odd_row = is_odd("gy")
        edge_even[...] = jnp.where(odd_row, up, down)
        edge_odd[...] = jnp.where(odd_row, down, up)


def shares_kernel(total, share, to_even, to_odd):
    odd_col = is_odd("gx")
    for index in range(share.shape[0]):
        left, right = total[index, :, : 2 * FB], total[index, :, 2 * FB :]
        share[index] = parity((FB, 2 * FB)) * (left + right)
        to_even[index] = jnp.where(odd_col, left, right)
        to_odd[index] = jnp.where(odd_col, right, left)


def merge_kernel(
    share_in, to_even_in, to_odd_in, near_even, near_odd, share, to_even, to_odd
):
    count = share.shape[0]
    odd_row, odd_col = is_odd("gy"), is_odd("gx")
    share[...] = share_in[...]
    to_even[...] = to_even_in[...]
    to_odd[...] = to_odd_in[...]
    above = jnp.where(odd_row, near_even[...], near_odd[...])
    below = jnp.where(odd_row, near_odd[...], near_even[...])
    for index, near in ((0, above), (count - 1, below)):
        left, right = near[:, : 2 * FB], near[:, 2 * FB :]
        share[index] += parity((FB, 2 * FB)) * (left + right)
        to_even[index] += jnp.where(odd_col, left, right)
        to_odd[index] += jnp.where(odd_col, right, left)


def imaging_kernel(
    share, from_even, from_odd, straight_own, crossed_own, straight_other, crossed_other,
    target, wide, resist_out, grad, fields, sides, resists, semaphores,
):
    count = straight_own.shape[0]
    straights, crosseds = (straight_own, straight_other), (crossed_own, crossed_other)
    copies = []
    sign = jnp.where(low_lanes((HALF, 2 * FB)), 1.0, -1.0)
    tiles = range(share.shape[0])
    intensities = [[] for tile in tiles]

    spectra = [share[tile] + from_even[tile] + from_odd[tile] for tile in tiles]
    turned = [swapped(spectrum) for spectrum in spectra]
    for group in range(2):
        products = [
            straights[group][i] * spectra[tile] + crosseds[group][i] * turned[tile]
            for tile in tiles
            for i in range(count)
        ]
        rows = times_table(jnp.concatenate(products, axis=0), wide_table(wide, SPREAD))
        for tile in tiles:
            total = jnp.zeros((COARSE, COARSE), jnp.float32)
            for i in range(count):
                place = (tile * count + i) * FB
                both = table_times(wide_table(wide, LIFT)[:, :192], rows[place : place + FB])
                cosine, sine = both[:HALF], both[HALF:]
                sine_re, sine_im = sine[:, :COARSE], sine[:, COARSE:]
                cosine_re, cosine_im = cosine[:, :COARSE], cosine[:, COARSE:]
                real = jnp.concatenate([cosine_re - sine_im, cosine_re + sine_im], axis=0)
                imag = jnp.concatenate([cosine_im + sine_re, cosine_im - sine_re], axis=0)
                fields[tile, group * count + i, :, :COARSE] = real
                fields[tile, group * count + i, :, COARSE:] = imag
                total = total + (real * real + imag * imag)
            intensities[tile].append(total)

    half_fine = times_table(
        jnp.concatenate([first + second for first, second in intensities], axis=0),
        wide_table(wide, FINE_RIGHT),
    )
    half_coarse = []
    for tile in tiles:
        fine = stacked_times(
            wide_table(wide, FINE_LEFT), half_fine[tile * COARSE : (tile + 1) * COARSE]
        )
        resist = jax.nn.sigmoid(4.0 * (fine - 1.0))
        place = slice(tile * TILE, (tile + 1) * TILE)
        resists[place, :] = resist
        start = (pl.program_id(0) * len(tiles) + tile) * TILE
        copy = pltpu.make_async_copy(
            resists.at[pl.ds(tile * TILE, TILE), :],
            resist_out.at[pl.ds(pl.multiple_of(start, TILE), TILE), :],
            semaphores.at[tile],
        )
        copy.start()
        copies.append(copy)
        misfit = resist - target[place, :].astype(jnp.float32)
        push = 16.0 * misfit * resist * (1.0 - resist)
        high, low = split(push)
        from_high = dot(wide_table(wide, COARSE_LEFT), high)
        half_coarse.append(
            from_high[:COARSE]
            + (from_high[COARSE:] + dot(wide_table(wide, COARSE_LEFT)[:COARSE], low))
        )
    weights = times_paired(jnp.concatenate(half_coarse, axis=0), wide_table(wide, COARSE_RIGHT))
    scales = [
        jnp.concatenate([weights[tile * COARSE : (tile + 1) * COARSE]] * 2, axis=1)
        for tile in tiles
    ]

    adjoint = [[] for tile in tiles]
    for group in range(2):
        scaled = [
            fields[tile, group * count + i] * scales[tile]
            for tile in tiles
            for i in range(count)
        ]
        sides[group] = times_paired(
            jnp.concatenate(scaled, axis=0), wide_table(wide, GATHER)
        )
        for tile in tiles:
            total = jnp.zeros((FB, 2 * FB), jnp.float32)
            for i in range(0, count, 2):
                pair = []
                for j in (i, i + 1):
                    place = (tile * count + j) * COARSE
                    plus = sides[group, place : place + HALF, :]
                    minus = sides[group, place + HALF : place + COARSE, :]
                    pair.append(
                        jnp.concatenate([plus + minus, sign * swapped(plus - minus)], axis=0)
                    )
                found = stacked_times(
                    wide_table(wide, FOLD), jnp.concatenate(pair, axis=1)
                )
                for j in (0, 1):
                    part = found[:, j * 2 * FB : (j + 1) * 2 * FB]
                    total = total + (
                        straights[group][i + j] * part - crosseds[group][i + j] * swapped(part)
                    )
            adjoint[tile].append(total)
    for tile in tiles:
        grad[tile] = adjoint[tile][0] + adjoint[tile][1]

    for copy in copies:
        copy.wait()


def sides_of(even_in, odd_in, index):
    odd_col = is_odd("gx")
    return (
        jnp.where(odd_col, even_in[index], odd_in[index]),
        jnp.where(odd_col, odd_in[index], even_in[index]),
    )


def synthesis_rows(rows, slope, tables):
    sign = jnp.where(low_lanes((FB, 2 * FB)), -1.0, 1.0)
    flip = row_parity((FB, 4 * FB))
    outer = []
    for index in range(1, len(rows) - 1):
        base = flip * rows[index]
        for part, near in enumerate((rows[index - 1], rows[index + 1])):
            block = base + near
            turned = [sign * swapped(block[:, : 2 * FB]), sign * swapped(block[:, 2 * FB :])]
            stacked = jnp.concatenate([block, jnp.concatenate(turned, axis=1)], axis=0)
            outer.append(stacked_times(stacked_table(tables, part), stacked))
    return times_diagonal(jnp.concatenate(outer, axis=0), tables) * slope


def mixed_row(own, even_in, odd_in, index):
    base = parity((FB, 2 * FB)) * own[index]
    from_left, from_right = sides_of(even_in, odd_in, index)
    return jnp.concatenate([base + from_left, base + from_right], axis=1)


def edges_kernel(own, even_in, odd_in, side_even, side_odd):
    first = mixed_row(own, even_in, odd_in, 0)
    last = mixed_row(own, even_in, odd_in, own.shape[0] - 1)
    odd_row = is_odd("gy")
    side_even[...] = jnp.where(odd_row, first, last)
    side_odd[...] = jnp.where(odd_row, last, first)


def write_rows(values, result, first, buffer, semaphore):
    buffer[...] = values
    copy = pltpu.make_async_copy(
        buffer, result.at[pl.ds(first, values.shape[0]), :], semaphore
    )
    copy.start()
    return copy


def inner_kernel(own, even_in, odd_in, slope, tables, result, buffer, semaphore):
    count = own.shape[0]
    rows = [mixed_row(own, even_in, odd_in, i) for i in range(count)]
    values = synthesis_rows(rows, slope[TILE : (count - 1) * TILE, :], tables)
    write_rows(values, result, TILE, buffer, semaphore).wait()


def outer_kernel(
    own, even_in, odd_in, near_even, near_odd, slope, tables, partial, result, buffers,
    semaphores,
):
    del partial
    count = own.shape[0]
    odd_row = is_odd("gy")
    above = jnp.where(odd_row, near_even[...], near_odd[...])
    below = jnp.where(odd_row, near_odd[...], near_even[...])
    rows = [mixed_row(own, even_in, odd_in, i) for i in (0, 1, count - 2, count - 1)]
    last = (count - 1) * TILE
    copies = []
    for index, first, near in ((0, 0, [above] + rows[:2]), (1, last, rows[2:] + [below])):
        values = synthesis_rows(near, slope[first : first + TILE, :], tables)
        copies.append(
            write_rows(values, result, first, buffers.at[index], semaphores.at[index])
        )
    for copy in copies:
        copy.wait()


def whole(array):
    zeros = (0,) * len(array.shape)
    return pl.BlockSpec(array.shape, lambda step: zeros)


def tile_pair():
    return pl.BlockSpec((PAIR * TILE, TILE), lambda step: (step, 0))


def params(limit=VMEM_LIMIT):
    return pltpu.CompilerParams(dimension_semantics=("arbitrary",), vmem_limit_bytes=limit)


def analysis(mask, kernels, weights):
    tiles = mask.shape[0] // TILE
    tables = jnp.asarray(TABLES["analysis"])
    part = pltpu.VMEM((FB // 2, 2 * FB), jnp.float32)
    total = jax.ShapeDtypeStruct((tiles, FB, 4 * FB), jnp.float32)
    packed = jax.ShapeDtypeStruct((kernels.shape[0], FB, 2 * FB), jnp.float32)
    half = jax.ShapeDtypeStruct((kernels.shape[0] // 2, FB, 2 * FB), jnp.float32)
    edge = jax.ShapeDtypeStruct((FB, 4 * FB), jnp.float32)
    return pl.pallas_call(
        analysis_kernel,
        grid=(tiles // PAIR,),
        out_shape=(
            total, packed, half, edge, edge, jax.ShapeDtypeStruct(mask.shape, jnp.float32)
        ),
        in_specs=[
            pl.BlockSpec(memory_space=pltpu.HBM),
            pl.BlockSpec(memory_space=pltpu.HBM),
            pl.BlockSpec(memory_space=pltpu.SMEM),
            pl.BlockSpec(memory_space=pltpu.HBM),
        ],
        out_specs=[whole(out) for out in (total, packed, half, edge, edge)] + [tile_pair()],
        scratch_shapes=[
            part,
            part,
            pltpu.VMEM((tiles + 2, FB, 4 * FB), jnp.float32),
            pltpu.VMEM(mask.shape, mask.dtype),
            pltpu.VMEM(kernels.shape, kernels.dtype),
            pltpu.VMEM(tables.shape, tables.dtype),
            pltpu.SemaphoreType.DMA((tiles // PAIR + 2,)),
        ],
        compiler_params=params(FIRST_LIMIT),
        name="analysis",
    )(mask, kernels, weights, tables)


def simple_call(kernel, out_shape, *operands, name):
    vmem = pl.BlockSpec(memory_space=pltpu.VMEM)
    return pl.pallas_call(
        kernel,
        out_shape=out_shape,
        in_specs=[vmem] * len(operands),
        out_specs=[vmem] * len(out_shape),
        compiler_params=pltpu.CompilerParams(vmem_limit_bytes=VMEM_LIMIT),
        name=name,
    )(*operands)


def shares(total):
    spectra = jax.ShapeDtypeStruct((total.shape[0], FB, 2 * FB), jnp.float32)
    return simple_call(shares_kernel, (spectra,) * 3, total, name="shares")


def merge(share, to_even, to_odd, near_even, near_odd):
    spectra = jax.ShapeDtypeStruct(share.shape, jnp.float32)
    return simple_call(
        merge_kernel, (spectra,) * 3, share, to_even, to_odd, near_even, near_odd, name="merge"
    )


def edges(grad, grad_even, grad_odd):
    side = jax.ShapeDtypeStruct((FB, 4 * FB), jnp.float32)
    return simple_call(edges_kernel, (side,) * 2, grad, grad_even, grad_odd, name="edges")


def prepare_own(own):
    shape = jax.ShapeDtypeStruct(own.shape, jnp.float32)
    return simple_call(own_kernel, (shape, shape), own, name="prepare_own")


def prepare_other(mine, partners):
    shape = jax.ShapeDtypeStruct((2 * mine.shape[0],) + mine.shape[1:], jnp.float32)
    return simple_call(other_kernel, (shape, shape), mine, partners, name="prepare_other")


def imaging(share, from_even, from_odd, own, other, target):
    tiles = share.shape[0]
    kernels = 2 * own[0].shape[0]
    tables = jnp.asarray(TABLES["imaging"])
    spectra = pl.BlockSpec((TILES_AT_ONCE, FB, 2 * FB), lambda step: (step, 0, 0))
    pixels = pl.BlockSpec((TILES_AT_ONCE * TILE, TILE), lambda step: (step, 0))
    return pl.pallas_call(
        imaging_kernel,
        grid=(tiles // TILES_AT_ONCE,),
        out_shape=(
            jax.ShapeDtypeStruct(target.shape, jnp.float32),
            jax.ShapeDtypeStruct(share.shape, jnp.float32),
        ),
        in_specs=[spectra] * 3 + [whole(own[0])] * 4 + [pixels, whole(tables)],
        out_specs=[pl.BlockSpec(memory_space=pl.ANY), spectra],
        scratch_shapes=[
            pltpu.VMEM((TILES_AT_ONCE, kernels, COARSE, 2 * COARSE), jnp.float32),
            pltpu.VMEM((2, TILES_AT_ONCE * kernels // 2 * COARSE, 2 * FB), jnp.float32),
            pltpu.VMEM((TILES_AT_ONCE * TILE, TILE), jnp.float32),
            pltpu.SemaphoreType.DMA((TILES_AT_ONCE,)),
        ],
        compiler_params=params(),
        name="imaging",
    )(share, from_even, from_odd, *own, *other, target, tables)


def inner_synthesis(own, even_in, odd_in, slope):
    tables = jnp.asarray(TABLES["synthesis"])
    vmem = pl.BlockSpec(memory_space=pltpu.VMEM)
    return pl.pallas_call(
        inner_kernel,
        out_shape=jax.ShapeDtypeStruct(slope.shape, jnp.float32),
        in_specs=[vmem] * 5,
        out_specs=pl.BlockSpec(memory_space=pl.ANY),
        scratch_shapes=[
            pltpu.VMEM((slope.shape[0] - 2 * TILE, TILE), jnp.float32),
            pltpu.SemaphoreType.DMA,
        ],
        compiler_params=pltpu.CompilerParams(vmem_limit_bytes=VMEM_LIMIT),
        cost_estimate=pl.CostEstimate(
            flops=1500000000, bytes_accessed=2500000, transcendentals=0
        ),
        name="inner_synthesis",
    )(own, even_in, odd_in, slope, tables)


def outer_synthesis(own, even_in, odd_in, near_even, near_odd, slope, partial):
    tables = jnp.asarray(TABLES["synthesis"])
    vmem = pl.BlockSpec(memory_space=pltpu.VMEM)
    return pl.pallas_call(
        outer_kernel,
        out_shape=jax.ShapeDtypeStruct(slope.shape, jnp.float32),
        in_specs=[vmem] * 7 + [pl.BlockSpec(memory_space=pl.ANY)],
        out_specs=pl.BlockSpec(memory_space=pl.ANY),
        input_output_aliases={7: 0},
        scratch_shapes=[
            pltpu.VMEM((2, TILE, TILE), jnp.float32),
            pltpu.SemaphoreType.DMA((2,)),
        ],
        compiler_params=pltpu.CompilerParams(vmem_limit_bytes=VMEM_LIMIT),
        name="outer_synthesis",
    )(own, even_in, odd_in, near_even, near_odd, slope, tables, partial)


def swap_pairs(count, first):
    pairs = []
    for place in range(first, count - 1, 2):
        pairs += [(place, place + 1), (place + 1, place)]
    return pairs


def local(mask_param, target, kernels, weights):
    rows = lax.axis_size("gy")

    def swap(value, axis, first):
        return lax.ppermute(value, axis, swap_pairs(lax.axis_size(axis), first))

    total, packed, half, edge_even, edge_odd, slope = analysis(mask_param, kernels, weights)
    inner = rows // 4
    pairs = []
    for place in range(rows):
        mirror = (3 - place // inner) * inner + place % inner
        pairs += [(2 * place, 2 * mirror + 1), (2 * place + 1, 2 * mirror)]
    mine = lax.ppermute(half, ("gy", "ka"), pairs)
    halo_odd = swap(edge_odd, "gy", 1)
    halo_even = swap(edge_even, "gy", 0)
    share, to_even, to_odd = merge(*shares(total), halo_even, halo_odd)
    from_odd = swap(to_odd, "gx", 1)
    from_even = swap(to_even, "gx", 0)
    own = prepare_own(packed)
    partners = swap(mine, "gx", 0)
    other = prepare_other(mine, partners)
    resist, grad = imaging(share, from_even, from_odd, own, other, target)
    grad_odd = swap(grad, "gx", 1)
    grad_even = swap(grad, "gx", 0)
    side_even, side_odd = edges(grad, grad_even, grad_odd)
    near_odd = swap(side_odd, "gy", 1)
    near_even = swap(side_even, "gy", 0)
    partial = inner_synthesis(grad, grad_even, grad_odd, slope)
    gradient = outer_synthesis(
        grad, grad_even, grad_odd, near_even, near_odd, slope, partial
    )
    return (gradient, resist)


def solution(mesh):
    placed = (P("gy", "gx"), P("gy", "gx"), P("ka", None, None), P("ka"))
    return jax.shard_map(
        local, mesh=mesh, in_specs=placed, out_specs=(P("gy", "gx"), P("gy", "gx")), check_vma=False
    )
```

```python
import math

import jax
import jax.numpy as jnp
import ml_dtypes
import numpy as np
from jax import lax
from jax.experimental import pallas as pl
from jax.experimental.pallas import tpu as pltpu
from jax.sharding import PartitionSpec as P

WIN = 512
HALO = 128
FB = 64
TILE = 256
COARSE = 128
HALF = COARSE // 2
VMEM_LIMIT = 40 * 1024 * 1024
PAIR = 3
TILES_AT_ONCE = 3
FIRST_LIMIT = 60 * 1024 * 1024

bf16 = ml_dtypes.bfloat16


def halves(table):
    high = table.astype(np.float32).astype(bf16)
    low = (table - high.astype(np.float64)).astype(np.float32).astype(bf16)
    return high, low


def as_left(table):
    high, low = halves(table)
    return np.concatenate([high, low, high], axis=1)


def as_right(table):
    high, low = halves(table)
    return np.concatenate([high, high, low], axis=0)


def angles(points):
    frequencies = np.arange(FB) - FB // 2
    windings = np.mod(frequencies[:, None] * np.asarray(points)[None, :], WIN)
    return windings * (2.0 * math.pi / WIN)


ORDER = np.concatenate([np.arange(0, FB, 2), np.arange(1, FB, 2)])


def blocks(table):
    return [table[:, i : i + 128] for i in range(0, table.shape[1], 128)]


def make_tables():
    factor = 1.0 / (WIN * FB)
    pixels = np.arange(HALO)
    columns, rows, outs, pixs = [], [], [], []
    for points in (pixels + 3 * HALO, pixels):
        cos, sin = np.cos(angles(points)), np.sin(angles(points))
        columns += halves(np.concatenate([cos.T, -sin.T], axis=1))
        pixs += halves(np.concatenate([cos, -sin], axis=0))
        cos, sin = cos[ORDER], sin[ORDER]
        rows += halves(factor * np.concatenate([cos, sin], axis=0))
        outs += halves(factor * np.concatenate([cos.T, sin.T], axis=1))
    plus = 4 * np.arange(HALF) + 2
    samples = np.concatenate([plus, -plus])
    cos, sin = np.cos(angles(samples)), np.sin(angles(samples))
    spread = np.concatenate(
        [np.concatenate([cos, sin], axis=1), np.concatenate([-sin, cos], axis=1)], axis=0
    )
    gather = spread.T
    order = np.concatenate([ORDER, FB + ORDER])
    offset = (np.arange(TILE) + HALO)[:, None] - samples[None, :]
    orders = np.arange(1, COARSE // 2)
    turns = np.mod(offset[..., None] * orders, WIN) * (2.0 * math.pi / WIN)
    interp = (1.0 + 2.0 * np.cos(turns).sum(-1)) / COARSE
    imaging = (
        as_right(spread),
        as_right(spread[order]),
        np.concatenate(halves(gather), axis=1),
        np.concatenate(halves(gather[:, order]), axis=1),
        as_right(interp.T),
        np.concatenate(halves(interp), axis=1),
    )
    return {
        "analysis": np.concatenate(columns + rows, axis=0),
        "synthesis": np.concatenate(pixs + outs, axis=0),
        "imaging": np.concatenate(sum(map(blocks, imaging), []), axis=0),
    }


TABLES = make_tables()
SPREAD, SPREAD_ROWS, GATHER, GATHER_ROWS, FINE, COARSEN = (
    (2 * a, b - a)
    for a, b in (
        (0, 384), (384, 768), (768, 1024), (1024, 1280), (1280, 1664), (1664, 1920),
    )
)


def split(value):
    high = value.astype(jnp.bfloat16)
    low = (value - high.astype(jnp.float32)).astype(jnp.bfloat16)
    return high, low


def dot(left, right):
    return jnp.dot(left, right, preferred_element_type=jnp.float32)


def times_table(value, table):
    high, low = split(value)
    return dot(jnp.concatenate([high, low, high], axis=1), table)


def table_times(table, value):
    high, low = split(value)
    return dot(table, jnp.concatenate([high, high, low], axis=0))


def stacked_times(table, value):
    high, low = split(value)
    found = dot(table, jnp.concatenate([high, low], axis=0))
    size = found.shape[0] // 2
    return found[:size] + found[size:]


def times_paired(value, table):
    high, low = split(value)
    width = table.shape[1] // 2
    first = dot(high, table)
    return first[:, :width] + (first[:, width:] + dot(low, table[:, :width]))


def square(packed, index):
    return packed[index * 128 : (index + 1) * 128, :]


def times_sides(value, packed):
    high, low = split(value)
    found = []
    for side in (0, 1):
        lanes = slice(side * 128, (side + 1) * 128)
        first, second = square(packed, 2 * side), square(packed, 2 * side + 1)
        found.append(
            dot(
                jnp.concatenate([high[:, lanes], low[:, lanes], high[:, lanes]], axis=1),
                jnp.concatenate([first, first, second], axis=0),
            )
        )
    return jnp.concatenate(found, axis=1)


def times_diagonal(value, packed):
    zeros = jnp.zeros((128, 128), jnp.bfloat16)
    high_table, low_table = (
        jnp.concatenate(
            [
                jnp.concatenate([square(packed, i), zeros], axis=1),
                jnp.concatenate([zeros, square(packed, i + 2)], axis=1),
            ],
            axis=0,
        )
        for i in (0, 1)
    )
    high, low = split(value)
    return dot(
        jnp.concatenate([high, low, high], axis=1),
        jnp.concatenate([high_table, high_table, low_table], axis=0),
    )


def stacked_table(packed, part):
    high, low = square(packed, 4 + 2 * part), square(packed, 5 + 2 * part)
    return jnp.concatenate(
        [
            jnp.concatenate([high, high], axis=1),
            jnp.concatenate([low, jnp.zeros_like(low)], axis=1),
        ],
        axis=0,
    )


def wide_table(packed, place):
    start, size = place
    return jnp.concatenate(
        [packed[start : start + size, :], packed[start + size : start + 2 * size, :]], axis=1
    )


def parity(shape):
    index = lax.broadcasted_iota(jnp.int32, shape, 1)
    return (1 - 2 * (index % 2)).astype(jnp.float32)


def is_odd(axis):
    return lax.axis_index(axis) % 2 == 1


def row_parity(shape):
    index = lax.broadcasted_iota(jnp.int32, shape, 0)
    return jnp.where(index < FB // 2, 1.0, -1.0)


def low_lanes(shape):
    return lax.broadcasted_iota(jnp.int32, shape, 1) < FB


def swapped(value):
    return pltpu.roll(value, FB, 1)


def factors(spectrum):
    lanes = low_lanes((FB, 2 * FB))
    turned = swapped(spectrum)
    return jnp.where(lanes, spectrum, turned), jnp.where(lanes, -turned, spectrum)


def own_kernel(own, straight, crossed):
    for index in range(own.shape[0]):
        straight[index], crossed[index] = factors(own[index])


def other_kernel(mine, partners, straight, crossed):
    odd_col = is_odd("gx")
    half = mine.shape[0]
    for index in range(half):
        first = jnp.where(odd_col, partners[index], mine[index])
        second = jnp.where(odd_col, mine[index], partners[index])
        straight[index], crossed[index] = factors(first)
        straight[half + index], crossed[half + index] = factors(second)


def pack_kernels(kernels, weights, packed, real, imag):
    lanes = low_lanes((FB // 2, 2 * FB))
    for index in range(kernels.shape[0]):
        for row in range(FB // 2):
            place = slice(row * 2 * FB, (row + 1) * 2 * FB)
            real[row : row + 1, :] = kernels[index, 0:1, place]
            imag[row : row + 1, :] = kernels[index, 1:2, place]
        root = jnp.sqrt(jnp.full((FB // 2, 2 * FB), weights[index], jnp.float32))
        re, im = root * real[...], root * imag[...]
        packed[index, : FB // 2] = jnp.where(lanes, re, swapped(im))
        packed[index, FB // 2 :] = jnp.where(lanes, swapped(re), im)


def block_spectra(transmit, tables):
    sign = jnp.where(low_lanes((FB, 2 * FB)), 1.0, -1.0)
    rows = times_sides(transmit, tables)
    found = []
    for block in range(transmit.shape[0] // HALO):
        first = square(tables, 4 + 2 * (block % 2))
        second = square(tables, 5 + 2 * (block % 2))
        both = table_times(
            jnp.concatenate([first, second, first], axis=1),
            rows[block * HALO : (block + 1) * HALO],
        )
        sine = both[FB:]
        turned = [sign * swapped(sine[:, : 2 * FB]), sign * swapped(sine[:, 2 * FB :])]
        found.append(both[:FB] + jnp.concatenate(turned, axis=1))
    return found


def analysis_kernel(
    mask_in, kernels_in, weights, tables_in,
    total, packed, half, edge_even, edge_odd, slope,
    real, imag, sums, mask, kernels, tables, semaphores,
):
    step = pl.program_id(0)
    count = total.shape[0]

    def pixels_copy(step):
        place = pl.ds(pl.multiple_of(step * PAIR * TILE, TILE), PAIR * TILE)
        return pltpu.make_async_copy(
            mask_in.at[place, :], mask.at[place, :], semaphores.at[step]
        )

    @pl.when(step == 0)
    def _():
        table_copy = pltpu.make_async_copy(tables_in, tables, semaphores.at[count // PAIR])
        kernel_copy = pltpu.make_async_copy(
            kernels_in, kernels, semaphores.at[count // PAIR + 1]
        )
        kernel_copy.start()
        pixels_copy(0).start()
        table_copy.start()
        for later in range(1, count // PAIR):
            pixels_copy(later).start()
        sums[...] = jnp.zeros_like(sums)
        kernel_copy.wait()
        pack_kernels(kernels, weights, packed, real, imag)
        size = half.shape[0]
        for index in range(size):
            half[index] = jnp.where(is_odd("gx"), packed[size + index], packed[index])
        table_copy.wait()

    pixels_copy(step).wait()
    transmit = jnp.tanh(mask[pl.ds(pl.multiple_of(step * PAIR * TILE, TILE), PAIR * TILE), :])
    slope[...] = 1.0 - transmit * transmit
    found = block_spectra(transmit, tables)
    flip = row_parity((FB, 4 * FB))
    first = step * PAIR
    for tile in range(PAIR):
        upper, lower = found[2 * tile], found[2 * tile + 1]
        sums[first + tile] += upper
        sums[first + tile + 1] += flip * (upper + lower)
        sums[first + tile + 2] += lower

    @pl.when(step == pl.num_programs(0) - 1)
    def _():
        total[...] = sums[1 : count + 1]
        up, down = sums[0], sums[count + 1]
        odd_row = is_odd("gy")
        edge_even[...] = jnp.where(odd_row, up, down)
        edge_odd[...] = jnp.where(odd_row, down, up)


def shares_kernel(total, share, to_even, to_odd):
    odd_col = is_odd("gx")
    for index in range(share.shape[0]):
        left, right = total[index, :, : 2 * FB], total[index, :, 2 * FB :]
        share[index] = parity((FB, 2 * FB)) * (left + right)
        to_even[index] = jnp.where(odd_col, left, right)
        to_odd[index] = jnp.where(odd_col, right, left)


def merge_kernel(
    share_in, to_even_in, to_odd_in, near_even, near_odd, share, to_even, to_odd
):
    count = share.shape[0]
    odd_row, odd_col = is_odd("gy"), is_odd("gx")
    share[...] = share_in[...]
    to_even[...] = to_even_in[...]
    to_odd[...] = to_odd_in[...]
    above = jnp.where(odd_row, near_even[...], near_odd[...])
    below = jnp.where(odd_row, near_odd[...], near_even[...])
    for index, near in ((0, above), (count - 1, below)):
        left, right = near[:, : 2 * FB], near[:, 2 * FB :]
        share[index] += parity((FB, 2 * FB)) * (left + right)
        to_even[index] += jnp.where(odd_col, left, right)
        to_odd[index] += jnp.where(odd_col, right, left)


def parts(value, count):
    size = value.shape[0] // count
    return [value[index * size : (index + 1) * size] for index in range(count)]


def imaging_kernel(
    share, from_even, from_odd, straight_own, crossed_own, straight_other, crossed_other,
    target, wide, resist_out, grad, fields, sides, resists, semaphores,
):
    count = straight_own.shape[0]
    straights, crosseds = (straight_own, straight_other), (crossed_own, crossed_other)
    tiles = range(share.shape[0])
    size = len(tiles) * count
    intensities = [[] for tile in tiles]

    spectra = [share[tile] + from_even[tile] + from_odd[tile] for tile in tiles]
    turned = [swapped(spectrum) for spectrum in spectra]
    for group in range(2):
        products = [
            straights[group][i] * spectra[tile] + crosseds[group][i] * turned[tile]
            for tile in tiles
            for i in range(count)
        ]
        rows = times_table(jnp.concatenate(products, axis=0), wide_table(wide, SPREAD))
        columns = [
            jnp.concatenate([part[:, :COARSE], part[:, COARSE:]], axis=0).T
            for part in parts(rows, size)
        ]
        found = times_table(jnp.concatenate(columns, axis=0), wide_table(wide, SPREAD_ROWS))
        fields[group] = found
        powers = [
            part[:, :COARSE] * part[:, :COARSE] + part[:, COARSE:] * part[:, COARSE:]
            for part in parts(found, size)
        ]
        for tile in tiles:
            intensities[tile].append(sum(powers[tile * count : (tile + 1) * count]))

    half_fine = times_table(
        jnp.concatenate([first + second for first, second in intensities], axis=0),
        wide_table(wide, FINE),
    )
    fines = times_table(
        jnp.concatenate([part.T for part in parts(half_fine, len(tiles))], axis=0),
        wide_table(wide, FINE),
    )
    pushes = []
    copies = []
    for tile, fine in enumerate(parts(fines, len(tiles))):
        resist = jax.nn.sigmoid(4.0 * (fine - 1.0))
        place = slice(tile * TILE, (tile + 1) * TILE)
        resists[place, :] = resist
        start = (pl.program_id(0) * len(tiles) + tile) * TILE
        copy = pltpu.make_async_copy(
            resists.at[pl.ds(tile * TILE, TILE), :],
            resist_out.at[pl.ds(pl.multiple_of(start, TILE), TILE), :],
            semaphores.at[tile],
        )
        copy.start()
        copies.append(copy)
        misfit = resist - target[place, :].astype(jnp.float32)
        pushes.append(16.0 * misfit * resist * (1.0 - resist))
    half_coarse = times_paired(jnp.concatenate(pushes, axis=0), wide_table(wide, COARSEN))
    weights = times_paired(
        jnp.concatenate([part.T for part in parts(half_coarse, len(tiles))], axis=0),
        wide_table(wide, COARSEN),
    )
    scales = [
        jnp.concatenate([weight, weight], axis=1) for weight in parts(weights, len(tiles))
    ]

    adjoint = [[] for tile in tiles]
    for group in range(2):
        scaled = [
            fields[group, (tile * count + i) * COARSE : (tile * count + i + 1) * COARSE, :]
            * scales[tile]
            for tile in tiles
            for i in range(count)
        ]
        sides[group] = times_paired(
            jnp.concatenate(scaled, axis=0), wide_table(wide, GATHER_ROWS)
        )
        columns = []
        for index in range(size):
            column = sides[group, index * COARSE : (index + 1) * COARSE, :].T
            columns.append(jnp.concatenate([column[:FB], column[FB:]], axis=1))
        found = times_paired(jnp.concatenate(columns, axis=0), wide_table(wide, GATHER))
        for tile in tiles:
            total = jnp.zeros((FB, 2 * FB), jnp.float32)
            for i in range(count):
                place = (tile * count + i) * FB
                part = found[place : place + FB]
                total = total + (
                    straights[group][i] * part - crosseds[group][i] * swapped(part)
                )
            adjoint[tile].append(total)
    for tile in tiles:
        grad[tile] = adjoint[tile][0] + adjoint[tile][1]

    for copy in copies:
        copy.wait()


def sides_of(even_in, odd_in, index):
    odd_col = is_odd("gx")
    return (
        jnp.where(odd_col, even_in[index], odd_in[index]),
        jnp.where(odd_col, odd_in[index], even_in[index]),
    )


def synthesis_rows(rows, slope, tables):
    sign = jnp.where(low_lanes((FB, 2 * FB)), -1.0, 1.0)
    flip = row_parity((FB, 4 * FB))
    outer = []
    for index in range(1, len(rows) - 1):
        base = flip * rows[index]
        for part, near in enumerate((rows[index - 1], rows[index + 1])):
            block = base + near
            turned = [sign * swapped(block[:, : 2 * FB]), sign * swapped(block[:, 2 * FB :])]
            stacked = jnp.concatenate([block, jnp.concatenate(turned, axis=1)], axis=0)
            outer.append(stacked_times(stacked_table(tables, part), stacked))
    return times_diagonal(jnp.concatenate(outer, axis=0), tables) * slope


def mixed_row(own, even_in, odd_in, index):
    base = parity((FB, 2 * FB)) * own[index]
    from_left, from_right = sides_of(even_in, odd_in, index)
    return jnp.concatenate([base + from_left, base + from_right], axis=1)


def edges_kernel(own, even_in, odd_in, side_even, side_odd):
    first = mixed_row(own, even_in, odd_in, 0)
    last = mixed_row(own, even_in, odd_in, own.shape[0] - 1)
    odd_row = is_odd("gy")
    side_even[...] = jnp.where(odd_row, first, last)
    side_odd[...] = jnp.where(odd_row, last, first)


def write_rows(values, result, first, buffer, semaphore):
    buffer[...] = values
    copy = pltpu.make_async_copy(
        buffer, result.at[pl.ds(first, values.shape[0]), :], semaphore
    )
    copy.start()
    return copy


def inner_kernel(own, even_in, odd_in, slope, tables, result, buffer, semaphore):
    count = own.shape[0]
    rows = [mixed_row(own, even_in, odd_in, i) for i in range(count)]
    values = synthesis_rows(rows, slope[TILE : (count - 1) * TILE, :], tables)
    write_rows(values, result, TILE, buffer, semaphore).wait()


def outer_kernel(
    own, even_in, odd_in, near_even, near_odd, slope, tables, partial, result, buffers,
    semaphores,
):
    del partial
    count = own.shape[0]
    odd_row = is_odd("gy")
    above = jnp.where(odd_row, near_even[...], near_odd[...])
    below = jnp.where(odd_row, near_odd[...], near_even[...])
    rows = [mixed_row(own, even_in, odd_in, i) for i in (0, 1, count - 2, count - 1)]
    last = (count - 1) * TILE
    copies = []
    for index, first, near in ((0, 0, [above] + rows[:2]), (1, last, rows[2:] + [below])):
        values = synthesis_rows(near, slope[first : first + TILE, :], tables)
        copies.append(
            write_rows(values, result, first, buffers.at[index], semaphores.at[index])
        )
    for copy in copies:
        copy.wait()


def whole(array):
    zeros = (0,) * len(array.shape)
    return pl.BlockSpec(array.shape, lambda step: zeros)


def tile_pair():
    return pl.BlockSpec((PAIR * TILE, TILE), lambda step: (step, 0))


def params(limit=VMEM_LIMIT):
    return pltpu.CompilerParams(dimension_semantics=("arbitrary",), vmem_limit_bytes=limit)


def analysis(mask, kernels, weights):
    tiles = mask.shape[0] // TILE
    tables = jnp.asarray(TABLES["analysis"])
    part = pltpu.VMEM((FB // 2, 2 * FB), jnp.float32)
    total = jax.ShapeDtypeStruct((tiles, FB, 4 * FB), jnp.float32)
    packed = jax.ShapeDtypeStruct((kernels.shape[0], FB, 2 * FB), jnp.float32)
    half = jax.ShapeDtypeStruct((kernels.shape[0] // 2, FB, 2 * FB), jnp.float32)
    edge = jax.ShapeDtypeStruct((FB, 4 * FB), jnp.float32)
    return pl.pallas_call(
        analysis_kernel,
        grid=(tiles // PAIR,),
        out_shape=(
            total, packed, half, edge, edge, jax.ShapeDtypeStruct(mask.shape, jnp.float32)
        ),
        in_specs=[
            pl.BlockSpec(memory_space=pltpu.HBM),
            pl.BlockSpec(memory_space=pltpu.HBM),
            pl.BlockSpec(memory_space=pltpu.SMEM),
            pl.BlockSpec(memory_space=pltpu.HBM),
        ],
        out_specs=[whole(out) for out in (total, packed, half, edge, edge)] + [tile_pair()],
        scratch_shapes=[
            part,
            part,
            pltpu.VMEM((tiles + 2, FB, 4 * FB), jnp.float32),
            pltpu.VMEM(mask.shape, mask.dtype),
            pltpu.VMEM(kernels.shape, kernels.dtype),
            pltpu.VMEM(tables.shape, tables.dtype),
            pltpu.SemaphoreType.DMA((tiles // PAIR + 2,)),
        ],
        compiler_params=params(FIRST_LIMIT),
        name="analysis",
    )(mask, kernels, weights, tables)


def simple_call(kernel, out_shape, *operands, name):
    vmem = pl.BlockSpec(memory_space=pltpu.VMEM)
    return pl.pallas_call(
        kernel,
        out_shape=out_shape,
        in_specs=[vmem] * len(operands),
        out_specs=[vmem] * len(out_shape),
        compiler_params=pltpu.CompilerParams(vmem_limit_bytes=VMEM_LIMIT),
        name=name,
    )(*operands)


def shares(total):
    spectra = jax.ShapeDtypeStruct((total.shape[0], FB, 2 * FB), jnp.float32)
    return simple_call(shares_kernel, (spectra,) * 3, total, name="shares")


def merge(share, to_even, to_odd, near_even, near_odd):
    spectra = jax.ShapeDtypeStruct(share.shape, jnp.float32)
    return simple_call(
        merge_kernel, (spectra,) * 3, share, to_even, to_odd, near_even, near_odd, name="merge"
    )


def edges(grad, grad_even, grad_odd):
    side = jax.ShapeDtypeStruct((FB, 4 * FB), jnp.float32)
    return simple_call(edges_kernel, (side,) * 2, grad, grad_even, grad_odd, name="edges")


def prepare_own(own):
    shape = jax.ShapeDtypeStruct(own.shape, jnp.float32)
    return simple_call(own_kernel, (shape, shape), own, name="prepare_own")


def prepare_other(mine, partners):
    shape = jax.ShapeDtypeStruct((2 * mine.shape[0],) + mine.shape[1:], jnp.float32)
    return simple_call(other_kernel, (shape, shape), mine, partners, name="prepare_other")


def imaging(share, from_even, from_odd, own, other, target):
    tiles = share.shape[0]
    kernels = 2 * own[0].shape[0]
    tables = jnp.asarray(TABLES["imaging"])
    spectra = pl.BlockSpec((TILES_AT_ONCE, FB, 2 * FB), lambda step: (step, 0, 0))
    pixels = pl.BlockSpec((TILES_AT_ONCE * TILE, TILE), lambda step: (step, 0))
    return pl.pallas_call(
        imaging_kernel,
        grid=(tiles // TILES_AT_ONCE,),
        out_shape=(
            jax.ShapeDtypeStruct(target.shape, jnp.float32),
            jax.ShapeDtypeStruct(share.shape, jnp.float32),
        ),
        in_specs=[spectra] * 3 + [whole(own[0])] * 4 + [pixels, whole(tables)],
        out_specs=[pl.BlockSpec(memory_space=pl.ANY), spectra],
        scratch_shapes=[
            pltpu.VMEM((2, TILES_AT_ONCE * kernels // 2 * COARSE, 2 * COARSE), jnp.float32),
            pltpu.VMEM((2, TILES_AT_ONCE * kernels // 2 * COARSE, 2 * FB), jnp.float32),
            pltpu.VMEM((TILES_AT_ONCE * TILE, TILE), jnp.float32),
            pltpu.SemaphoreType.DMA((TILES_AT_ONCE,)),
        ],
        compiler_params=params(),
        name="imaging",
    )(share, from_even, from_odd, *own, *other, target, tables)


def inner_synthesis(own, even_in, odd_in, slope):
    tables = jnp.asarray(TABLES["synthesis"])
    vmem = pl.BlockSpec(memory_space=pltpu.VMEM)
    return pl.pallas_call(
        inner_kernel,
        out_shape=jax.ShapeDtypeStruct(slope.shape, jnp.float32),
        in_specs=[vmem] * 5,
        out_specs=pl.BlockSpec(memory_space=pl.ANY),
        scratch_shapes=[
            pltpu.VMEM((slope.shape[0] - 2 * TILE, TILE), jnp.float32),
            pltpu.SemaphoreType.DMA,
        ],
        compiler_params=pltpu.CompilerParams(vmem_limit_bytes=VMEM_LIMIT),
        cost_estimate=pl.CostEstimate(
            flops=1500000000, bytes_accessed=2500000, transcendentals=0
        ),
        name="inner_synthesis",
    )(own, even_in, odd_in, slope, tables)


def outer_synthesis(own, even_in, odd_in, near_even, near_odd, slope, partial):
    tables = jnp.asarray(TABLES["synthesis"])
    vmem = pl.BlockSpec(memory_space=pltpu.VMEM)
    return pl.pallas_call(
        outer_kernel,
        out_shape=jax.ShapeDtypeStruct(slope.shape, jnp.float32),
        in_specs=[vmem] * 7 + [pl.BlockSpec(memory_space=pl.ANY)],
        out_specs=pl.BlockSpec(memory_space=pl.ANY),
        input_output_aliases={7: 0},
        scratch_shapes=[
            pltpu.VMEM((2, TILE, TILE), jnp.float32),
            pltpu.SemaphoreType.DMA((2,)),
        ],
        compiler_params=pltpu.CompilerParams(vmem_limit_bytes=VMEM_LIMIT),
        name="outer_synthesis",
    )(own, even_in, odd_in, near_even, near_odd, slope, tables, partial)


def swap_pairs(count, first):
    pairs = []
    for place in range(first, count - 1, 2):
        pairs += [(place, place + 1), (place + 1, place)]
    return pairs


def local(mask_param, target, kernels, weights):
    rows = lax.axis_size("gy")

    def swap(value, axis, first):
        return lax.ppermute(value, axis, swap_pairs(lax.axis_size(axis), first))

    total, packed, half, edge_even, edge_odd, slope = analysis(mask_param, kernels, weights)
    inner = rows // 4
    pairs = []
    for place in range(rows):
        mirror = (3 - place // inner) * inner + place % inner
        pairs += [(2 * place, 2 * mirror + 1), (2 * place + 1, 2 * mirror)]
    mine = lax.ppermute(half, ("gy", "ka"), pairs)
    halo_odd = swap(edge_odd, "gy", 1)
    halo_even = swap(edge_even, "gy", 0)
    share, to_even, to_odd = merge(*shares(total), halo_even, halo_odd)
    from_odd = swap(to_odd, "gx", 1)
    from_even = swap(to_even, "gx", 0)
    own = prepare_own(packed)
    partners = swap(mine, "gx", 0)
    other = prepare_other(mine, partners)
    resist, grad = imaging(share, from_even, from_odd, own, other, target)
    grad_odd = swap(grad, "gx", 1)
    grad_even = swap(grad, "gx", 0)
    side_even, side_odd = edges(grad, grad_even, grad_odd)
    near_odd = swap(side_odd, "gy", 1)
    near_even = swap(side_even, "gy", 0)
    partial = inner_synthesis(grad, grad_even, grad_odd, slope)
    gradient = outer_synthesis(
        grad, grad_even, grad_odd, near_even, near_odd, slope, partial
    )
    return (gradient, resist)


def solution(mesh):
    placed = (P("gy", "gx"), P("gy", "gx"), P("ka", None, None), P("ka"))
    return jax.shard_map(
        local, mesh=mesh, in_specs=placed, out_specs=(P("gy", "gx"), P("gy", "gx")), check_vma=False
    )
```

```python
import math

import jax
import jax.numpy as jnp
import ml_dtypes
import numpy as np
from jax import lax
from jax.experimental import pallas as pl
from jax.experimental.pallas import tpu as pltpu
from jax.sharding import PartitionSpec as P

WIN = 512
HALO = 128
FB = 64
TILE = 256
COARSE = 128
HALF = COARSE // 2
VMEM_LIMIT = 40 * 1024 * 1024
PAIR = 3
TILES_AT_ONCE = 3
FIRST_LIMIT = 60 * 1024 * 1024

bf16 = ml_dtypes.bfloat16


def halves(table):
    high = table.astype(np.float32).astype(bf16)
    low = (table - high.astype(np.float64)).astype(np.float32).astype(bf16)
    return high, low


def as_left(table):
    high, low = halves(table)
    return np.concatenate([high, low, high], axis=1)


def as_right(table):
    high, low = halves(table)
    return np.concatenate([high, high, low], axis=0)


def angles(points):
    frequencies = np.arange(FB) - FB // 2
    windings = np.mod(frequencies[:, None] * np.asarray(points)[None, :], WIN)
    return windings * (2.0 * math.pi / WIN)


ORDER = np.concatenate([np.arange(0, FB, 2), np.arange(1, FB, 2)])


def blocks(table):
    return [table[:, i : i + 128] for i in range(0, table.shape[1], 128)]


def make_tables():
    factor = 1.0 / (WIN * FB)
    pixels = np.arange(HALO)
    columns, rows, outs, pixs = [], [], [], []
    for points in (pixels + 3 * HALO, pixels):
        cos, sin = np.cos(angles(points)), np.sin(angles(points))
        columns += halves(np.concatenate([cos.T, -sin.T], axis=1))
        pixs += halves(np.concatenate([cos, -sin], axis=0))
        cos, sin = cos[ORDER], sin[ORDER]
        rows += halves(factor * np.concatenate([cos, sin], axis=0))
        outs += halves(factor * np.concatenate([cos.T, sin.T], axis=1))
    plus = 4 * np.arange(HALF) + 2
    samples = np.concatenate([plus, -plus])
    cos, sin = np.cos(angles(samples)), np.sin(angles(samples))
    spread = as_right(
        np.concatenate(
            [np.concatenate([cos, sin], axis=1), np.concatenate([-sin, cos], axis=1)], axis=0
        )
    )
    gather = np.concatenate(
        [np.concatenate([cos.T, -sin.T], axis=1), np.concatenate([sin.T, cos.T], axis=1)], axis=0
    )
    gather = np.concatenate(halves(gather), axis=1)
    cos, sin = np.cos(angles(plus))[ORDER], np.sin(angles(plus))[ORDER]
    lift = as_left(np.concatenate([cos.T, sin.T], axis=0))
    lift = np.concatenate([lift, np.zeros((COARSE, 64), bf16)], axis=1)
    high, low = halves(np.concatenate([cos, sin], axis=1))
    fold = np.concatenate(
        [np.concatenate([high, high], axis=1), np.concatenate([low, 0 * low], axis=1)], axis=0
    )
    offset = (np.arange(TILE) + HALO)[:, None] - samples[None, :]
    orders = np.arange(1, COARSE // 2)
    turns = np.mod(offset[..., None] * orders, WIN) * (2.0 * math.pi / WIN)
    interp = (1.0 + 2.0 * np.cos(turns).sum(-1)) / COARSE
    high, low = halves(interp)
    fine_left = np.concatenate(
        [np.concatenate([high, high], axis=1), np.concatenate([low, 0 * low], axis=1)], axis=0
    )
    coarse_left = np.concatenate(halves(interp.T), axis=0)
    coarse_right = np.concatenate(halves(interp), axis=1)
    return {
        "analysis": np.concatenate(columns + rows, axis=0),
        "synthesis": np.concatenate(pixs + outs, axis=0),
        "imaging": np.concatenate(
            sum(
                map(
                    blocks,
                    (
                        spread, gather, lift, fold, as_right(interp.T), fine_left, coarse_left,
                        coarse_right,
                    ),
                ),
                [],
            ),
            axis=0,
        ),
    }


TABLES = make_tables()
SPREAD, GATHER, LIFT, FOLD, FINE_RIGHT, FINE_LEFT, COARSE_LEFT, COARSE_RIGHT = (
    (2 * a, b - a)
    for a, b in (
        (0, 384), (384, 640), (640, 768), (768, 896), (896, 1280), (1280, 1792), (1792, 2048),
        (2048, 2304),
    )
)


def split(value):
    high = value.astype(jnp.bfloat16)
    low = (value - high.astype(jnp.float32)).astype(jnp.bfloat16)
    return high, low


def dot(left, right):
    return jnp.dot(left, right, preferred_element_type=jnp.float32)


def times_table(value, table):
    high, low = split(value)
    return dot(jnp.concatenate([high, low, high], axis=1), table)


def table_times(table, value):
    high, low = split(value)
    return dot(table, jnp.concatenate([high, high, low], axis=0))


def stacked_times(table, value):
    high, low = split(value)
    found = dot(table, jnp.concatenate([high, low], axis=0))
    size = found.shape[0] // 2
    return found[:size] + found[size:]


def times_paired(value, table):
    high, low = split(value)
    width = table.shape[1] // 2
    first = dot(high, table)
    return first[:, :width] + (first[:, width:] + dot(low, table[:, :width]))


def square(packed, index):
    return packed[index * 128 : (index + 1) * 128, :]


def times_sides(value, packed):
    high, low = split(value)
    found = []
    for side in (0, 1):
        lanes = slice(side * 128, (side + 1) * 128)
        first, second = square(packed, 2 * side), square(packed, 2 * side + 1)
        found.append(
            dot(
                jnp.concatenate([high[:, lanes], low[:, lanes], high[:, lanes]], axis=1),
                jnp.concatenate([first, first, second], axis=0),
            )
        )
    return jnp.concatenate(found, axis=1)


def times_diagonal(value, packed):
    zeros = jnp.zeros((128, 128), jnp.bfloat16)
    high_table, low_table = (
        jnp.concatenate(
            [
                jnp.concatenate([square(packed, i), zeros], axis=1),
                jnp.concatenate([zeros, square(packed, i + 2)], axis=1),
            ],
            axis=0,
        )
        for i in (0, 1)
    )
    high, low = split(value)
    return dot(
        jnp.concatenate([high, low, high], axis=1),
        jnp.concatenate([high_table, high_table, low_table], axis=0),
    )


def stacked_table(packed, part):
    high, low = square(packed, 4 + 2 * part), square(packed, 5 + 2 * part)
    return jnp.concatenate(
        [
            jnp.concatenate([high, high], axis=1),
            jnp.concatenate([low, jnp.zeros_like(low)], axis=1),
        ],
        axis=0,
    )


def wide_table(packed, place):
    start, size = place
    return jnp.concatenate(
        [packed[start : start + size, :], packed[start + size : start + 2 * size, :]], axis=1
    )


def parity(shape):
    index = lax.broadcasted_iota(jnp.int32, shape, 1)
    return (1 - 2 * (index % 2)).astype(jnp.float32)


def is_odd(axis):
    return lax.axis_index(axis) % 2 == 1


def row_parity(shape):
    index = lax.broadcasted_iota(jnp.int32, shape, 0)
    return jnp.where(index < FB // 2, 1.0, -1.0)


def low_lanes(shape):
    return lax.broadcasted_iota(jnp.int32, shape, 1) < FB


def swapped(value):
    return pltpu.roll(value, FB, 1)


def factors(spectrum):
    lanes = low_lanes((FB, 2 * FB))
    turned = swapped(spectrum)
    return jnp.where(lanes, spectrum, turned), jnp.where(lanes, -turned, spectrum)


def own_kernel(own, straight, crossed):
    for index in range(own.shape[0]):
        straight[index], crossed[index] = factors(own[index])


def other_kernel(mine, partners, straight, crossed):
    odd_col = is_odd("gx")
    half = mine.shape[0]
    for index in range(half):
        first = jnp.where(odd_col, partners[index], mine[index])
        second = jnp.where(odd_col, mine[index], partners[index])
        straight[index], crossed[index] = factors(first)
        straight[half + index], crossed[half + index] = factors(second)


def pack_kernels(kernels, weights, packed, real, imag):
    lanes = low_lanes((FB // 2, 2 * FB))
    for index in range(kernels.shape[0]):
        for row in range(FB // 2):
            place = slice(row * 2 * FB, (row + 1) * 2 * FB)
            real[row : row + 1, :] = kernels[index, 0:1, place]
            imag[row : row + 1, :] = kernels[index, 1:2, place]
        root = jnp.sqrt(jnp.full((FB // 2, 2 * FB), weights[index], jnp.float32))
        re, im = root * real[...], root * imag[...]
        packed[index, : FB // 2] = jnp.where(lanes, re, swapped(im))
        packed[index, FB // 2 :] = jnp.where(lanes, swapped(re), im)


def block_spectra(transmit, tables):
    sign = jnp.where(low_lanes((FB, 2 * FB)), 1.0, -1.0)
    rows = times_sides(transmit, tables)
    found = []
    for block in range(transmit.shape[0] // HALO):
        first = square(tables, 4 + 2 * (block % 2))
        second = square(tables, 5 + 2 * (block % 2))
        both = table_times(
            jnp.concatenate([first, second, first], axis=1),
            rows[block * HALO : (block + 1) * HALO],
        )
        sine = both[FB:]
        turned = [sign * swapped(sine[:, : 2 * FB]), sign * swapped(sine[:, 2 * FB :])]
        found.append(both[:FB] + jnp.concatenate(turned, axis=1))
    return found


def analysis_kernel(
    mask_in, kernels_in, weights, tables_in,
    total, packed, half, edge_even, edge_odd, slope,
    real, imag, sums, mask, kernels, tables, semaphores,
):
    step = pl.program_id(0)
    count = total.shape[0]

    def pixels_copy(step):
        place = pl.ds(pl.multiple_of(step * PAIR * TILE, TILE), PAIR * TILE)
        return pltpu.make_async_copy(
            mask_in.at[place, :], mask.at[place, :], semaphores.at[step]
        )

    @pl.when(step == 0)
    def _():
        table_copy = pltpu.make_async_copy(tables_in, tables, semaphores.at[count // PAIR])
        kernel_copy = pltpu.make_async_copy(
            kernels_in, kernels, semaphores.at[count // PAIR + 1]
        )
        kernel_copy.start()
        pixels_copy(0).start()
        table_copy.start()
        for later in range(1, count // PAIR):
            pixels_copy(later).start()
        sums[...] = jnp.zeros_like(sums)
        kernel_copy.wait()
        pack_kernels(kernels, weights, packed, real, imag)
        size = half.shape[0]
        for index in range(size):
            half[index] = jnp.where(is_odd("gx"), packed[size + index], packed[index])
        table_copy.wait()

    pixels_copy(step).wait()
    transmit = jnp.tanh(mask[pl.ds(pl.multiple_of(step * PAIR * TILE, TILE), PAIR * TILE), :])
    slope[...] = 1.0 - transmit * transmit
    found = block_spectra(transmit, tables)
    flip = row_parity((FB, 4 * FB))
    first = step * PAIR
    for tile in range(PAIR):
        upper, lower = found[2 * tile], found[2 * tile + 1]
        sums[first + tile] += upper
        sums[first + tile + 1] += flip * (upper + lower)
        sums[first + tile + 2] += lower

    @pl.when(step == pl.num_programs(0) - 1)
    def _():
        total[...] = sums[1 : count + 1]
        up, down = sums[0], sums[count + 1]
        odd_row = is_odd("gy")
        edge_even[...] = jnp.where(odd_row, up, down)
        edge_odd[...] = jnp.where(odd_row, down, up)


def shares_kernel(total, share, to_even, to_odd):
    odd_col = is_odd("gx")
    for index in range(share.shape[0]):
        left, right = total[index, :, : 2 * FB], total[index, :, 2 * FB :]
        share[index] = parity((FB, 2 * FB)) * (left + right)
        to_even[index] = jnp.where(odd_col, left, right)
        to_odd[index] = jnp.where(odd_col, right, left)


def merge_kernel(
    share_in, to_even_in, to_odd_in, near_even, near_odd, share, to_even, to_odd
):
    count = share.shape[0]
    odd_row, odd_col = is_odd("gy"), is_odd("gx")
    share[...] = share_in[...]
    to_even[...] = to_even_in[...]
    to_odd[...] = to_odd_in[...]
    above = jnp.where(odd_row, near_even[...], near_odd[...])
    below = jnp.where(odd_row, near_odd[...], near_even[...])
    for index, near in ((0, above), (count - 1, below)):
        left, right = near[:, : 2 * FB], near[:, 2 * FB :]
        share[index] += parity((FB, 2 * FB)) * (left + right)
        to_even[index] += jnp.where(odd_col, left, right)
        to_odd[index] += jnp.where(odd_col, right, left)


def imaging_kernel(
    share, from_even, from_odd, straight_own, crossed_own, straight_other, crossed_other,
    target, wide, resist_out, grad, fields, sides, resists, semaphores,
):
    count = straight_own.shape[0]
    straights, crosseds = (straight_own, straight_other), (crossed_own, crossed_other)
    copies = []
    sign = jnp.where(low_lanes((HALF, 2 * FB)), 1.0, -1.0)
    tiles = range(share.shape[0])
    intensities = [[] for tile in tiles]

    spectra = [share[tile] + from_even[tile] + from_odd[tile] for tile in tiles]
    turned = [swapped(spectrum) for spectrum in spectra]
    for group in range(2):
        products = [
            straights[group][i] * spectra[tile] + crosseds[group][i] * turned[tile]
            for tile in tiles
            for i in range(count)
        ]
        halves_of = []
        for i in range(0, len(products), 2):
            both = table_times(
                wide_table(wide, LIFT)[:, :192], jnp.concatenate(products[i : i + 2], axis=1)
            )
            for j in (0, 1):
                part = both[:, j * 2 * FB : (j + 1) * 2 * FB]
                cosine, sine = part[:HALF], sign * swapped(part[HALF:])
                halves_of += [cosine - sine, cosine + sine]
        found = times_table(jnp.concatenate(halves_of, axis=0), wide_table(wide, SPREAD))
        fields[group] = found
        for tile in tiles:
            total = jnp.zeros((COARSE, COARSE), jnp.float32)
            for i in range(count):
                place = (tile * count + i) * COARSE
                real = found[place : place + COARSE, :COARSE]
                imag = found[place : place + COARSE, COARSE:]
                total = total + (real * real + imag * imag)
            intensities[tile].append(total)

    half_fine = times_table(
        jnp.concatenate([first + second for first, second in intensities], axis=0),
        wide_table(wide, FINE_RIGHT),
    )
    half_coarse = []
    for tile in tiles:
        fine = stacked_times(
            wide_table(wide, FINE_LEFT), half_fine[tile * COARSE : (tile + 1) * COARSE]
        )
        resist = jax.nn.sigmoid(4.0 * (fine - 1.0))
        place = slice(tile * TILE, (tile + 1) * TILE)
        resists[place, :] = resist
        start = (pl.program_id(0) * len(tiles) + tile) * TILE
        copy = pltpu.make_async_copy(
            resists.at[pl.ds(tile * TILE, TILE), :],
            resist_out.at[pl.ds(pl.multiple_of(start, TILE), TILE), :],
            semaphores.at[tile],
        )
        copy.start()
        copies.append(copy)
        misfit = resist - target[place, :].astype(jnp.float32)
        push = 16.0 * misfit * resist * (1.0 - resist)
        high, low = split(push)
        from_high = dot(wide_table(wide, COARSE_LEFT), high)
        half_coarse.append(
            from_high[:COARSE]
            + (from_high[COARSE:] + dot(wide_table(wide, COARSE_LEFT)[:COARSE], low))
        )
    weights = times_paired(jnp.concatenate(half_coarse, axis=0), wide_table(wide, COARSE_RIGHT))
    scales = [
        jnp.concatenate([weights[tile * COARSE : (tile + 1) * COARSE]] * 2, axis=1)
        for tile in tiles
    ]

    adjoint = [[] for tile in tiles]
    for group in range(2):
        scaled = [
            fields[group, (tile * count + i) * COARSE : (tile * count + i + 1) * COARSE, :]
            * scales[tile]
            for tile in tiles
            for i in range(count)
        ]
        sides[group] = times_paired(
            jnp.concatenate(scaled, axis=0), wide_table(wide, GATHER)
        )
        for tile in tiles:
            total = jnp.zeros((FB, 2 * FB), jnp.float32)
            for i in range(0, count, 2):
                pair = []
                for j in (i, i + 1):
                    place = (tile * count + j) * COARSE
                    plus = sides[group, place : place + HALF, :]
                    minus = sides[group, place + HALF : place + COARSE, :]
                    pair.append(
                        jnp.concatenate([plus + minus, sign * swapped(plus - minus)], axis=0)
                    )
                found = stacked_times(
                    wide_table(wide, FOLD), jnp.concatenate(pair, axis=1)
                )
                for j in (0, 1):
                    part = found[:, j * 2 * FB : (j + 1) * 2 * FB]
                    total = total + (
                        straights[group][i + j] * part - crosseds[group][i + j] * swapped(part)
                    )
            adjoint[tile].append(total)
    for tile in tiles:
        grad[tile] = adjoint[tile][0] + adjoint[tile][1]

    for copy in copies:
        copy.wait()


def sides_of(even_in, odd_in, index):
    odd_col = is_odd("gx")
    return (
        jnp.where(odd_col, even_in[index], odd_in[index]),
        jnp.where(odd_col, odd_in[index], even_in[index]),
    )


def synthesis_rows(rows, slope, tables):
    sign = jnp.where(low_lanes((FB, 2 * FB)), -1.0, 1.0)
    flip = row_parity((FB, 4 * FB))
    outer = []
    for index in range(1, len(rows) - 1):
        base = flip * rows[index]
        for part, near in enumerate((rows[index - 1], rows[index + 1])):
            block = base + near
            turned = [sign * swapped(block[:, : 2 * FB]), sign * swapped(block[:, 2 * FB :])]
            stacked = jnp.concatenate([block, jnp.concatenate(turned, axis=1)], axis=0)
            outer.append(stacked_times(stacked_table(tables, part), stacked))
    return times_diagonal(jnp.concatenate(outer, axis=0), tables) * slope


def mixed_row(own, even_in, odd_in, index):
    base = parity((FB, 2 * FB)) * own[index]
    from_left, from_right = sides_of(even_in, odd_in, index)
    return jnp.concatenate([base + from_left, base + from_right], axis=1)


def edges_kernel(own, even_in, odd_in, side_even, side_odd):
    first = mixed_row(own, even_in, odd_in, 0)
    last = mixed_row(own, even_in, odd_in, own.shape[0] - 1)
    odd_row = is_odd("gy")
    side_even[...] = jnp.where(odd_row, first, last)
    side_odd[...] = jnp.where(odd_row, last, first)


def write_rows(values, result, first, buffer, semaphore):
    buffer[...] = values
    copy = pltpu.make_async_copy(
        buffer, result.at[pl.ds(first, values.shape[0]), :], semaphore
    )
    copy.start()
    return copy


def inner_kernel(own, even_in, odd_in, slope, tables, result, buffer, semaphore):
    count = own.shape[0]
    rows = [mixed_row(own, even_in, odd_in, i) for i in range(count)]
    values = synthesis_rows(rows, slope[TILE : (count - 1) * TILE, :], tables)
    write_rows(values, result, TILE, buffer, semaphore).wait()


def outer_kernel(
    own, even_in, odd_in, near_even, near_odd, slope, tables, partial, result, buffers,
    semaphores,
):
    del partial
    count = own.shape[0]
    odd_row = is_odd("gy")
    above = jnp.where(odd_row, near_even[...], near_odd[...])
    below = jnp.where(odd_row, near_odd[...], near_even[...])
    rows = [mixed_row(own, even_in, odd_in, i) for i in (0, 1, count - 2, count - 1)]
    last = (count - 1) * TILE
    copies = []
    for index, first, near in ((0, 0, [above] + rows[:2]), (1, last, rows[2:] + [below])):
        values = synthesis_rows(near, slope[first : first + TILE, :], tables)
        copies.append(
            write_rows(values, result, first, buffers.at[index], semaphores.at[index])
        )
    for copy in copies:
        copy.wait()


def whole(array):
    zeros = (0,) * len(array.shape)
    return pl.BlockSpec(array.shape, lambda step: zeros)


def tile_pair():
    return pl.BlockSpec((PAIR * TILE, TILE), lambda step: (step, 0))


def params(limit=VMEM_LIMIT):
    return pltpu.CompilerParams(dimension_semantics=("arbitrary",), vmem_limit_bytes=limit)


def analysis(mask, kernels, weights):
    tiles = mask.shape[0] // TILE
    tables = jnp.asarray(TABLES["analysis"])
    part = pltpu.VMEM((FB // 2, 2 * FB), jnp.float32)
    total = jax.ShapeDtypeStruct((tiles, FB, 4 * FB), jnp.float32)
    packed = jax.ShapeDtypeStruct((kernels.shape[0], FB, 2 * FB), jnp.float32)
    half = jax.ShapeDtypeStruct((kernels.shape[0] // 2, FB, 2 * FB), jnp.float32)
    edge = jax.ShapeDtypeStruct((FB, 4 * FB), jnp.float32)
    return pl.pallas_call(
        analysis_kernel,
        grid=(tiles // PAIR,),
        out_shape=(
            total, packed, half, edge, edge, jax.ShapeDtypeStruct(mask.shape, jnp.float32)
        ),
        in_specs=[
            pl.BlockSpec(memory_space=pltpu.HBM),
            pl.BlockSpec(memory_space=pltpu.HBM),
            pl.BlockSpec(memory_space=pltpu.SMEM),
            pl.BlockSpec(memory_space=pltpu.HBM),
        ],
        out_specs=[whole(out) for out in (total, packed, half, edge, edge)] + [tile_pair()],
        scratch_shapes=[
            part,
            part,
            pltpu.VMEM((tiles + 2, FB, 4 * FB), jnp.float32),
            pltpu.VMEM(mask.shape, mask.dtype),
            pltpu.VMEM(kernels.shape, kernels.dtype),
            pltpu.VMEM(tables.shape, tables.dtype),
            pltpu.SemaphoreType.DMA((tiles // PAIR + 2,)),
        ],
        compiler_params=params(FIRST_LIMIT),
        name="analysis",
    )(mask, kernels, weights, tables)


def simple_call(kernel, out_shape, *operands, name):
    vmem = pl.BlockSpec(memory_space=pltpu.VMEM)
    return pl.pallas_call(
        kernel,
        out_shape=out_shape,
        in_specs=[vmem] * len(operands),
        out_specs=[vmem] * len(out_shape),
        compiler_params=pltpu.CompilerParams(vmem_limit_bytes=VMEM_LIMIT),
        name=name,
    )(*operands)


def shares(total):
    spectra = jax.ShapeDtypeStruct((total.shape[0], FB, 2 * FB), jnp.float32)
    return simple_call(shares_kernel, (spectra,) * 3, total, name="shares")


def merge(share, to_even, to_odd, near_even, near_odd):
    spectra = jax.ShapeDtypeStruct(share.shape, jnp.float32)
    return simple_call(
        merge_kernel, (spectra,) * 3, share, to_even, to_odd, near_even, near_odd, name="merge"
    )


def edges(grad, grad_even, grad_odd):
    side = jax.ShapeDtypeStruct((FB, 4 * FB), jnp.float32)
    return simple_call(edges_kernel, (side,) * 2, grad, grad_even, grad_odd, name="edges")


def prepare_own(own):
    shape = jax.ShapeDtypeStruct(own.shape, jnp.float32)
    return simple_call(own_kernel, (shape, shape), own, name="prepare_own")


def prepare_other(mine, partners):
    shape = jax.ShapeDtypeStruct((2 * mine.shape[0],) + mine.shape[1:], jnp.float32)
    return simple_call(other_kernel, (shape, shape), mine, partners, name="prepare_other")


def imaging(share, from_even, from_odd, own, other, target):
    tiles = share.shape[0]
    kernels = 2 * own[0].shape[0]
    tables = jnp.asarray(TABLES["imaging"])
    spectra = pl.BlockSpec((TILES_AT_ONCE, FB, 2 * FB), lambda step: (step, 0, 0))
    pixels = pl.BlockSpec((TILES_AT_ONCE * TILE, TILE), lambda step: (step, 0))
    return pl.pallas_call(
        imaging_kernel,
        grid=(tiles // TILES_AT_ONCE,),
        out_shape=(
            jax.ShapeDtypeStruct(target.shape, jnp.float32),
            jax.ShapeDtypeStruct(share.shape, jnp.float32),
        ),
        in_specs=[spectra] * 3 + [whole(own[0])] * 4 + [pixels, whole(tables)],
        out_specs=[pl.BlockSpec(memory_space=pl.ANY), spectra],
        scratch_shapes=[
            pltpu.VMEM((2, TILES_AT_ONCE * kernels // 2 * COARSE, 2 * COARSE), jnp.float32),
            pltpu.VMEM((2, TILES_AT_ONCE * kernels // 2 * COARSE, 2 * FB), jnp.float32),
            pltpu.VMEM((TILES_AT_ONCE * TILE, TILE), jnp.float32),
            pltpu.SemaphoreType.DMA((TILES_AT_ONCE,)),
        ],
        compiler_params=params(),
        name="imaging",
    )(share, from_even, from_odd, *own, *other, target, tables)


def inner_synthesis(own, even_in, odd_in, slope):
    tables = jnp.asarray(TABLES["synthesis"])
    vmem = pl.BlockSpec(memory_space=pltpu.VMEM)
    return pl.pallas_call(
        inner_kernel,
        out_shape=jax.ShapeDtypeStruct(slope.shape, jnp.float32),
        in_specs=[vmem] * 5,
        out_specs=pl.BlockSpec(memory_space=pl.ANY),
        scratch_shapes=[
            pltpu.VMEM((slope.shape[0] - 2 * TILE, TILE), jnp.float32),
            pltpu.SemaphoreType.DMA,
        ],
        compiler_params=pltpu.CompilerParams(vmem_limit_bytes=VMEM_LIMIT),
        cost_estimate=pl.CostEstimate(
            flops=1500000000, bytes_accessed=2500000, transcendentals=0
        ),
        name="inner_synthesis",
    )(own, even_in, odd_in, slope, tables)


def outer_synthesis(own, even_in, odd_in, near_even, near_odd, slope, partial):
    tables = jnp.asarray(TABLES["synthesis"])
    vmem = pl.BlockSpec(memory_space=pltpu.VMEM)
    return pl.pallas_call(
        outer_kernel,
        out_shape=jax.ShapeDtypeStruct(slope.shape, jnp.float32),
        in_specs=[vmem] * 7 + [pl.BlockSpec(memory_space=pl.ANY)],
        out_specs=pl.BlockSpec(memory_space=pl.ANY),
        input_output_aliases={7: 0},
        scratch_shapes=[
            pltpu.VMEM((2, TILE, TILE), jnp.float32),
            pltpu.SemaphoreType.DMA((2,)),
        ],
        compiler_params=pltpu.CompilerParams(vmem_limit_bytes=VMEM_LIMIT),
        name="outer_synthesis",
    )(own, even_in, odd_in, near_even, near_odd, slope, tables, partial)


def swap_pairs(count, first):
    pairs = []
    for place in range(first, count - 1, 2):
        pairs += [(place, place + 1), (place + 1, place)]
    return pairs


def local(mask_param, target, kernels, weights):
    rows = lax.axis_size("gy")

    def swap(value, axis, first):
        return lax.ppermute(value, axis, swap_pairs(lax.axis_size(axis), first))

    total, packed, half, edge_even, edge_odd, slope = analysis(mask_param, kernels, weights)
    inner = rows // 4
    pairs = []
    for place in range(rows):
        mirror = (3 - place // inner) * inner + place % inner
        pairs += [(2 * place, 2 * mirror + 1), (2 * place + 1, 2 * mirror)]
    mine = lax.ppermute(half, ("gy", "ka"), pairs)
    halo_odd = swap(edge_odd, "gy", 1)
    halo_even = swap(edge_even, "gy", 0)
    share, to_even, to_odd = merge(*shares(total), halo_even, halo_odd)
    from_odd = swap(to_odd, "gx", 1)
    from_even = swap(to_even, "gx", 0)
    own = prepare_own(packed)
    partners = swap(mine, "gx", 0)
    other = prepare_other(mine, partners)
    resist, grad = imaging(share, from_even, from_odd, own, other, target)
    grad_odd = swap(grad, "gx", 1)
    grad_even = swap(grad, "gx", 0)
    side_even, side_odd = edges(grad, grad_even, grad_odd)
    near_odd = swap(side_odd, "gy", 1)
    near_even = swap(side_even, "gy", 0)
    partial = inner_synthesis(grad, grad_even, grad_odd, slope)
    gradient = outer_synthesis(
        grad, grad_even, grad_odd, near_even, near_odd, slope, partial
    )
    return (gradient, resist)


def solution(mesh):
    placed = (P("gy", "gx"), P("gy", "gx"), P("ka", None, None), P("ka"))
    return jax.shard_map(
        local, mesh=mesh, in_specs=placed, out_specs=(P("gy", "gx"), P("gy", "gx")), check_vma=False
    )
```

```python
import math

import jax
import jax.numpy as jnp
import ml_dtypes
import numpy as np
from jax import lax
from jax.experimental import pallas as pl
from jax.experimental.pallas import tpu as pltpu
from jax.sharding import PartitionSpec as P

WIN = 512
HALO = 128
FB = 64
TILE = 256
COARSE = 128
HALF = COARSE // 2
VMEM_LIMIT = 40 * 1024 * 1024
PAIR = 3
TILES_AT_ONCE = 3
FIRST_LIMIT = 60 * 1024 * 1024

bf16 = ml_dtypes.bfloat16


def halves(table):
    high = table.astype(np.float32).astype(bf16)
    low = (table - high.astype(np.float64)).astype(np.float32).astype(bf16)
    return high, low


def as_left(table):
    high, low = halves(table)
    return np.concatenate([high, low, high], axis=1)


def as_right(table):
    high, low = halves(table)
    return np.concatenate([high, high, low], axis=0)


def angles(points):
    frequencies = np.arange(FB) - FB // 2
    windings = np.mod(frequencies[:, None] * np.asarray(points)[None, :], WIN)
    return windings * (2.0 * math.pi / WIN)


ORDER = np.concatenate([np.arange(0, FB, 2), np.arange(1, FB, 2)])


def blocks(table):
    return [table[:, i : i + 128] for i in range(0, table.shape[1], 128)]


def make_tables():
    factor = 1.0 / (WIN * FB)
    pixels = np.arange(HALO)
    columns, rows, outs, pixs = [], [], [], []
    for points in (pixels + 3 * HALO, pixels):
        cos, sin = np.cos(angles(points)), np.sin(angles(points))
        columns += halves(np.concatenate([cos.T, -sin.T], axis=1))
        pixs += halves(np.concatenate([cos, -sin], axis=0))
        cos, sin = cos[ORDER], sin[ORDER]
        rows += halves(factor * np.concatenate([cos, sin], axis=0))
        outs += halves(factor * np.concatenate([cos.T, sin.T], axis=1))
    plus = 4 * np.arange(HALF) + 2
    samples = np.concatenate([plus, -plus])
    cos, sin = np.cos(angles(samples)), np.sin(angles(samples))
    spread = as_right(
        np.concatenate(
            [np.concatenate([cos, sin], axis=1), np.concatenate([-sin, cos], axis=1)], axis=0
        )
    )
    gather = np.concatenate(
        [np.concatenate([cos.T, -sin.T], axis=1), np.concatenate([sin.T, cos.T], axis=1)], axis=0
    )
    gather = np.concatenate(halves(gather), axis=1)
    cos, sin = np.cos(angles(plus))[ORDER], np.sin(angles(plus))[ORDER]
    lift = as_left(np.concatenate([cos.T, sin.T], axis=0))
    lift = np.concatenate([lift, np.zeros((COARSE, 64), bf16)], axis=1)
    high, low = halves(np.concatenate([cos, sin], axis=1))
    fold = np.concatenate(
        [np.concatenate([high, high], axis=1), np.concatenate([low, 0 * low], axis=1)], axis=0
    )
    offset = (np.arange(TILE) + HALO)[:, None] - samples[None, :]
    orders = np.arange(1, COARSE // 2)
    turns = np.mod(offset[..., None] * orders, WIN) * (2.0 * math.pi / WIN)
    interp = (1.0 + 2.0 * np.cos(turns).sum(-1)) / COARSE
    high, low = halves(interp)
    fine_left = np.concatenate(
        [np.concatenate([high, high], axis=1), np.concatenate([low, 0 * low], axis=1)], axis=0
    )
    coarse_left = np.concatenate(halves(interp.T), axis=0)
    coarse_right = np.concatenate(halves(interp), axis=1)
    return {
        "analysis": np.concatenate(columns + rows, axis=0),
        "synthesis": np.concatenate(pixs + outs, axis=0),
        "imaging": np.concatenate(
            sum(
                map(
                    blocks,
                    (
                        spread, gather, lift, fold, as_right(interp.T), fine_left, coarse_left,
                        coarse_right,
                    ),
                ),
                [],
            ),
            axis=0,
        ),
    }


TABLES = make_tables()
SPREAD, GATHER, LIFT, FOLD, FINE_RIGHT, FINE_LEFT, COARSE_LEFT, COARSE_RIGHT = (
    (2 * a, b - a)
    for a, b in (
        (0, 384), (384, 640), (640, 768), (768, 896), (896, 1280), (1280, 1792), (1792, 2048),
        (2048, 2304),
    )
)


def split(value):
    high = value.astype(jnp.bfloat16)
    low = (value - high.astype(jnp.float32)).astype(jnp.bfloat16)
    return high, low


def dot(left, right):
    return jnp.dot(left, right, preferred_element_type=jnp.float32)


def times_table(value, table):
    high, low = split(value)
    return dot(jnp.concatenate([high, low, high], axis=1), table)


def table_times(table, value):
    high, low = split(value)
    return dot(table, jnp.concatenate([high, high, low], axis=0))


def stacked_times(table, value):
    high, low = split(value)
    found = dot(table, jnp.concatenate([high, low], axis=0))
    size = found.shape[0] // 2
    return found[:size] + found[size:]


def times_paired(value, table):
    high, low = split(value)
    width = table.shape[1] // 2
    first = dot(high, table)
    return first[:, :width] + (first[:, width:] + dot(low, table[:, :width]))


def square(packed, index):
    return packed[index * 128 : (index + 1) * 128, :]


def times_sides(value, packed):
    high, low = split(value)
    found = []
    for side in (0, 1):
        lanes = slice(side * 128, (side + 1) * 128)
        first, second = square(packed, 2 * side), square(packed, 2 * side + 1)
        found.append(
            dot(
                jnp.concatenate([high[:, lanes], low[:, lanes], high[:, lanes]], axis=1),
                jnp.concatenate([first, first, second], axis=0),
            )
        )
    return jnp.concatenate(found, axis=1)


def times_diagonal(value, packed):
    zeros = jnp.zeros((128, 128), jnp.bfloat16)
    high_table, low_table = (
        jnp.concatenate(
            [
                jnp.concatenate([square(packed, i), zeros], axis=1),
                jnp.concatenate([zeros, square(packed, i + 2)], axis=1),
            ],
            axis=0,
        )
        for i in (0, 1)
    )
    high, low = split(value)
    return dot(
        jnp.concatenate([high, low, high], axis=1),
        jnp.concatenate([high_table, high_table, low_table], axis=0),
    )


def stacked_table(packed, part):
    high, low = square(packed, 4 + 2 * part), square(packed, 5 + 2 * part)
    return jnp.concatenate(
        [
            jnp.concatenate([high, high], axis=1),
            jnp.concatenate([low, jnp.zeros_like(low)], axis=1),
        ],
        axis=0,
    )


def wide_table(packed, place):
    start, size = place
    return jnp.concatenate(
        [packed[start : start + size, :], packed[start + size : start + 2 * size, :]], axis=1
    )


def parity(shape):
    index = lax.broadcasted_iota(jnp.int32, shape, 1)
    return (1 - 2 * (index % 2)).astype(jnp.float32)


def is_odd(axis):
    return lax.axis_index(axis) % 2 == 1


def row_parity(shape):
    index = lax.broadcasted_iota(jnp.int32, shape, 0)
    return jnp.where(index < FB // 2, 1.0, -1.0)


def low_lanes(shape):
    return lax.broadcasted_iota(jnp.int32, shape, 1) < FB


def swapped(value):
    return pltpu.roll(value, FB, 1)


def factors(spectrum):
    lanes = low_lanes((FB, 2 * FB))
    turned = swapped(spectrum)
    return jnp.where(lanes, spectrum, turned), jnp.where(lanes, -turned, spectrum)


def own_kernel(own, straight, crossed):
    for index in range(own.shape[0]):
        straight[index], crossed[index] = factors(own[index])


def other_kernel(mine, partners, straight, crossed):
    odd_col = is_odd("gx")
    half = mine.shape[0]
    for index in range(half):
        first = jnp.where(odd_col, partners[index], mine[index])
        second = jnp.where(odd_col, mine[index], partners[index])
        straight[index], crossed[index] = factors(first)
        straight[half + index], crossed[half + index] = factors(second)


def pack_kernels(kernels, weights, packed, real, imag):
    lanes = low_lanes((FB // 2, 2 * FB))
    for index in range(kernels.shape[0]):
        for row in range(FB // 2):
            place = slice(row * 2 * FB, (row + 1) * 2 * FB)
            real[row : row + 1, :] = kernels[index, 0:1, place]
            imag[row : row + 1, :] = kernels[index, 1:2, place]
        root = jnp.sqrt(jnp.full((FB // 2, 2 * FB), weights[index], jnp.float32))
        re, im = root * real[...], root * imag[...]
        packed[index, : FB // 2] = jnp.where(lanes, re, swapped(im))
        packed[index, FB // 2 :] = jnp.where(lanes, swapped(re), im)


def block_spectra(transmit, tables):
    sign = jnp.where(low_lanes((FB, 2 * FB)), 1.0, -1.0)
    rows = times_sides(transmit, tables)
    found = []
    for block in range(transmit.shape[0] // HALO):
        first = square(tables, 4 + 2 * (block % 2))
        second = square(tables, 5 + 2 * (block % 2))
        both = table_times(
            jnp.concatenate([first, second, first], axis=1),
            rows[block * HALO : (block + 1) * HALO],
        )
        sine = both[FB:]
        turned = [sign * swapped(sine[:, : 2 * FB]), sign * swapped(sine[:, 2 * FB :])]
        found.append(both[:FB] + jnp.concatenate(turned, axis=1))
    return found


def analysis_kernel(
    mask_in, kernels_in, weights, tables_in,
    total, packed, half, edge_odd, slope,
    real, imag, sums, mask, kernels, tables, semaphores,
):
    step = pl.program_id(0)
    count = total.shape[0] - 2

    def pixels_copy(step):
        place = pl.ds(pl.multiple_of(step * PAIR * TILE, TILE), PAIR * TILE)
        return pltpu.make_async_copy(
            mask_in.at[place, :], mask.at[place, :], semaphores.at[step]
        )

    @pl.when(step == 0)
    def _():
        table_copy = pltpu.make_async_copy(tables_in, tables, semaphores.at[count // PAIR])
        kernel_copy = pltpu.make_async_copy(
            kernels_in, kernels, semaphores.at[count // PAIR + 1]
        )
        kernel_copy.start()
        pixels_copy(0).start()
        table_copy.start()
        for later in range(1, count // PAIR):
            pixels_copy(later).start()
        sums[...] = jnp.zeros_like(sums)
        kernel_copy.wait()
        pack_kernels(kernels, weights, packed, real, imag)
        size = half.shape[0]
        for index in range(size):
            half[index] = jnp.where(is_odd("gx"), packed[size + index], packed[index])
        table_copy.wait()

    pixels_copy(step).wait()
    transmit = jnp.tanh(mask[pl.ds(pl.multiple_of(step * PAIR * TILE, TILE), PAIR * TILE), :])
    slope[...] = 1.0 - transmit * transmit
    found = block_spectra(transmit, tables)
    flip = row_parity((FB, 4 * FB))
    first = step * PAIR
    for tile in range(PAIR):
        upper, lower = found[2 * tile], found[2 * tile + 1]
        sums[first + tile] += upper
        sums[first + tile + 1] += flip * (upper + lower)
        sums[first + tile + 2] += lower

    @pl.when(step == pl.num_programs(0) - 1)
    def _():
        total[...] = sums[...]
        edge_odd[...] = jnp.where(is_odd("gy"), sums[count + 1], sums[0])


def shares_kernel(total, share, to_even, to_odd, edge):
    odd_col = is_odd("gx")
    edge[...] = jnp.where(is_odd("gy"), total[0], total[share.shape[0] + 1])
    for index in range(share.shape[0]):
        left, right = total[index + 1, :, : 2 * FB], total[index + 1, :, 2 * FB :]
        share[index] = parity((FB, 2 * FB)) * (left + right)
        to_even[index] = jnp.where(odd_col, left, right)
        to_odd[index] = jnp.where(odd_col, right, left)


def merge_kernel(
    share_in, to_even_in, to_odd_in, near_even, near_odd, share, to_even, to_odd
):
    count = share.shape[0]
    odd_row, odd_col = is_odd("gy"), is_odd("gx")
    share[...] = share_in[...]
    to_even[...] = to_even_in[...]
    to_odd[...] = to_odd_in[...]
    above = jnp.where(odd_row, near_even[...], near_odd[...])
    below = jnp.where(odd_row, near_odd[...], near_even[...])
    for index, near in ((0, above), (count - 1, below)):
        left, right = near[:, : 2 * FB], near[:, 2 * FB :]
        share[index] += parity((FB, 2 * FB)) * (left + right)
        to_even[index] += jnp.where(odd_col, left, right)
        to_odd[index] += jnp.where(odd_col, right, left)


def imaging_kernel(
    share, from_even, from_odd, straight_own, crossed_own, straight_other, crossed_other,
    target, wide, resist_out, grad, fields, sides, resists, semaphores,
):
    count = straight_own.shape[0]
    straights, crosseds = (straight_own, straight_other), (crossed_own, crossed_other)
    copies = []
    sign = jnp.where(low_lanes((HALF, 2 * FB)), 1.0, -1.0)
    tiles = range(share.shape[0])

    spectra = [share[tile] + from_even[tile] + from_odd[tile] for tile in tiles]
    turned = [swapped(spectrum) for spectrum in spectra]
    order = [(group, tile, i) for group in range(2) for tile in tiles for i in range(count)]
    products = [
        straights[group][i] * spectra[tile] + crosseds[group][i] * turned[tile]
        for group, tile, i in order
    ]
    halves_of = []
    for i in range(0, len(products), 2):
        both = table_times(
            wide_table(wide, LIFT)[:, :192], jnp.concatenate(products[i : i + 2], axis=1)
        )
        for j in (0, 1):
            part = both[:, j * 2 * FB : (j + 1) * 2 * FB]
            cosine, sine = part[:HALF], sign * swapped(part[HALF:])
            halves_of += [cosine - sine, cosine + sine]
    found = times_table(jnp.concatenate(halves_of, axis=0), wide_table(wide, SPREAD))
    fields[...] = found
    totals = {}
    for place, (group, tile, i) in enumerate(order):
        real = found[place * COARSE : (place + 1) * COARSE, :COARSE]
        imag = found[place * COARSE : (place + 1) * COARSE, COARSE:]
        power = real * real + imag * imag
        totals[group, tile] = power if i == 0 else totals[group, tile] + power

    half_fine = times_table(
        jnp.concatenate([totals[0, tile] + totals[1, tile] for tile in tiles], axis=0),
        wide_table(wide, FINE_RIGHT),
    )
    half_coarse = []
    for tile in tiles:
        fine = stacked_times(
            wide_table(wide, FINE_LEFT), half_fine[tile * COARSE : (tile + 1) * COARSE]
        )
        resist = jax.nn.sigmoid(4.0 * (fine - 1.0))
        place = slice(tile * TILE, (tile + 1) * TILE)
        resists[place, :] = resist
        start = (pl.program_id(0) * len(tiles) + tile) * TILE
        copy = pltpu.make_async_copy(
            resists.at[pl.ds(tile * TILE, TILE), :],
            resist_out.at[pl.ds(pl.multiple_of(start, TILE), TILE), :],
            semaphores.at[tile],
        )
        copy.start()
        copies.append(copy)
        misfit = resist - target[place, :].astype(jnp.float32)
        push = 16.0 * misfit * resist * (1.0 - resist)
        high, low = split(push)
        from_high = dot(wide_table(wide, COARSE_LEFT), high)
        half_coarse.append(
            from_high[:COARSE]
            + (from_high[COARSE:] + dot(wide_table(wide, COARSE_LEFT)[:COARSE], low))
        )
    weights = times_paired(jnp.concatenate(half_coarse, axis=0), wide_table(wide, COARSE_RIGHT))
    scales = [
        jnp.concatenate([weights[tile * COARSE : (tile + 1) * COARSE]] * 2, axis=1)
        for tile in tiles
    ]

    scaled = [
        fields[place * COARSE : (place + 1) * COARSE, :] * scales[tile]
        for place, (group, tile, i) in enumerate(order)
    ]
    sides[...] = times_paired(jnp.concatenate(scaled, axis=0), wide_table(wide, GATHER))
    adjoint = {}
    for place in range(0, len(order), 2):
        pair = []
        for j in (place, place + 1):
            plus = sides[j * COARSE : j * COARSE + HALF, :]
            minus = sides[j * COARSE + HALF : (j + 1) * COARSE, :]
            pair.append(jnp.concatenate([plus + minus, sign * swapped(plus - minus)], axis=0))
        found = stacked_times(wide_table(wide, FOLD), jnp.concatenate(pair, axis=1))
        for j in (0, 1):
            group, tile, i = order[place + j]
            part = found[:, j * 2 * FB : (j + 1) * 2 * FB]
            term = straights[group][i] * part - crosseds[group][i] * swapped(part)
            adjoint[group, tile] = term if i == 0 else adjoint[group, tile] + term
    for tile in tiles:
        grad[tile] = adjoint[0, tile] + adjoint[1, tile]

    for copy in copies:
        copy.wait()


def sides_of(even_in, odd_in, index):
    odd_col = is_odd("gx")
    return (
        jnp.where(odd_col, even_in[index], odd_in[index]),
        jnp.where(odd_col, odd_in[index], even_in[index]),
    )


def synthesis_rows(rows, slope, tables):
    sign = jnp.where(low_lanes((FB, 2 * FB)), -1.0, 1.0)
    flip = row_parity((FB, 4 * FB))
    outer = []
    for index in range(1, len(rows) - 1):
        base = flip * rows[index]
        for part, near in enumerate((rows[index - 1], rows[index + 1])):
            block = base + near
            turned = [sign * swapped(block[:, : 2 * FB]), sign * swapped(block[:, 2 * FB :])]
            stacked = jnp.concatenate([block, jnp.concatenate(turned, axis=1)], axis=0)
            outer.append(stacked_times(stacked_table(tables, part), stacked))
    return times_diagonal(jnp.concatenate(outer, axis=0), tables) * slope


def mixed_row(own, even_in, odd_in, index):
    base = parity((FB, 2 * FB)) * own[index]
    from_left, from_right = sides_of(even_in, odd_in, index)
    return jnp.concatenate([base + from_left, base + from_right], axis=1)


def odd_edge_kernel(own, even_in, odd_in, side):
    first = mixed_row(own, even_in, odd_in, 0)
    last = mixed_row(own, even_in, odd_in, own.shape[0] - 1)
    side[...] = jnp.where(is_odd("gy"), last, first)


def even_edge_kernel(own, even_in, odd_in, before, side):
    del before
    first = mixed_row(own, even_in, odd_in, 0)
    last = mixed_row(own, even_in, odd_in, own.shape[0] - 1)
    side[...] = jnp.where(is_odd("gy"), first, last)


def write_rows(values, result, first, buffer, semaphore):
    buffer[...] = values
    copy = pltpu.make_async_copy(
        buffer, result.at[pl.ds(first, values.shape[0]), :], semaphore
    )
    copy.start()
    return copy


def inner_kernel(own, even_in, odd_in, slope, tables, result, buffer, semaphore):
    count = own.shape[0]
    rows = [mixed_row(own, even_in, odd_in, i) for i in range(count)]
    values = synthesis_rows(rows, slope[TILE : (count - 1) * TILE, :], tables)
    write_rows(values, result, TILE, buffer, semaphore).wait()


def outer_kernel(
    own, even_in, odd_in, near_even, near_odd, slope, tables, partial, result, buffers,
    semaphores,
):
    del partial
    count = own.shape[0]
    odd_row = is_odd("gy")
    above = jnp.where(odd_row, near_even[...], near_odd[...])
    below = jnp.where(odd_row, near_odd[...], near_even[...])
    rows = [mixed_row(own, even_in, odd_in, i) for i in (0, 1, count - 2, count - 1)]
    last = (count - 1) * TILE
    copies = []
    for index, first, near in ((0, 0, [above] + rows[:2]), (1, last, rows[2:] + [below])):
        values = synthesis_rows(near, slope[first : first + TILE, :], tables)
        copies.append(
            write_rows(values, result, first, buffers.at[index], semaphores.at[index])
        )
    for copy in copies:
        copy.wait()


def whole(array):
    zeros = (0,) * len(array.shape)
    return pl.BlockSpec(array.shape, lambda step: zeros)


def tile_pair():
    return pl.BlockSpec((PAIR * TILE, TILE), lambda step: (step, 0))


def params(limit=VMEM_LIMIT):
    return pltpu.CompilerParams(dimension_semantics=("arbitrary",), vmem_limit_bytes=limit)


def analysis(mask, kernels, weights):
    tiles = mask.shape[0] // TILE
    tables = jnp.asarray(TABLES["analysis"])
    part = pltpu.VMEM((FB // 2, 2 * FB), jnp.float32)
    total = jax.ShapeDtypeStruct((tiles + 2, FB, 4 * FB), jnp.float32)
    packed = jax.ShapeDtypeStruct((kernels.shape[0], FB, 2 * FB), jnp.float32)
    half = jax.ShapeDtypeStruct((kernels.shape[0] // 2, FB, 2 * FB), jnp.float32)
    edge = jax.ShapeDtypeStruct((FB, 4 * FB), jnp.float32)
    return pl.pallas_call(
        analysis_kernel,
        grid=(tiles // PAIR,),
        out_shape=(
            total, packed, half, edge, jax.ShapeDtypeStruct(mask.shape, jnp.float32)
        ),
        in_specs=[
            pl.BlockSpec(memory_space=pltpu.HBM),
            pl.BlockSpec(memory_space=pltpu.HBM),
            pl.BlockSpec(memory_space=pltpu.SMEM),
            pl.BlockSpec(memory_space=pltpu.HBM),
        ],
        out_specs=[whole(out) for out in (total, packed, half, edge)] + [tile_pair()],
        scratch_shapes=[
            part,
            part,
            pltpu.VMEM((tiles + 2, FB, 4 * FB), jnp.float32),
            pltpu.VMEM(mask.shape, mask.dtype),
            pltpu.VMEM(kernels.shape, kernels.dtype),
            pltpu.VMEM(tables.shape, tables.dtype),
            pltpu.SemaphoreType.DMA((tiles // PAIR + 2,)),
        ],
        compiler_params=params(FIRST_LIMIT),
        name="analysis",
    )(mask, kernels, weights, tables)


def simple_call(kernel, out_shape, *operands, name):
    vmem = pl.BlockSpec(memory_space=pltpu.VMEM)
    return pl.pallas_call(
        kernel,
        out_shape=out_shape,
        in_specs=[vmem] * len(operands),
        out_specs=[vmem] * len(out_shape),
        compiler_params=pltpu.CompilerParams(vmem_limit_bytes=VMEM_LIMIT),
        name=name,
    )(*operands)


def shares(total):
    spectra = jax.ShapeDtypeStruct((total.shape[0] - 2, FB, 2 * FB), jnp.float32)
    side = jax.ShapeDtypeStruct((FB, 4 * FB), jnp.float32)
    return simple_call(shares_kernel, (spectra,) * 3 + (side,), total, name="shares")


def merge(share, to_even, to_odd, near_even, near_odd):
    spectra = jax.ShapeDtypeStruct(share.shape, jnp.float32)
    return simple_call(
        merge_kernel, (spectra,) * 3, share, to_even, to_odd, near_even, near_odd, name="merge"
    )


def odd_edge(grad, grad_even, grad_odd):
    side = jax.ShapeDtypeStruct((FB, 4 * FB), jnp.float32)
    return simple_call(odd_edge_kernel, (side,), grad, grad_even, grad_odd, name="odd_edge")[0]


def even_edge(grad, grad_even, grad_odd, before):
    side = jax.ShapeDtypeStruct((FB, 4 * FB), jnp.float32)
    return simple_call(
        even_edge_kernel, (side,), grad, grad_even, grad_odd, before, name="even_edge"
    )[0]


def prepare_own(own):
    shape = jax.ShapeDtypeStruct(own.shape, jnp.float32)
    return simple_call(own_kernel, (shape, shape), own, name="prepare_own")


def prepare_other(mine, partners):
    shape = jax.ShapeDtypeStruct((2 * mine.shape[0],) + mine.shape[1:], jnp.float32)
    return simple_call(other_kernel, (shape, shape), mine, partners, name="prepare_other")


def imaging(share, from_even, from_odd, own, other, target):
    tiles = share.shape[0]
    kernels = 2 * own[0].shape[0]
    tables = jnp.asarray(TABLES["imaging"])
    spectra = pl.BlockSpec((TILES_AT_ONCE, FB, 2 * FB), lambda step: (step, 0, 0))
    pixels = pl.BlockSpec((TILES_AT_ONCE * TILE, TILE), lambda step: (step, 0))
    return pl.pallas_call(
        imaging_kernel,
        grid=(tiles // TILES_AT_ONCE,),
        out_shape=(
            jax.ShapeDtypeStruct(target.shape, jnp.float32),
            jax.ShapeDtypeStruct(share.shape, jnp.float32),
        ),
        in_specs=[spectra] * 3 + [whole(own[0])] * 4 + [pixels, whole(tables)],
        out_specs=[pl.BlockSpec(memory_space=pl.ANY), spectra],
        scratch_shapes=[
            pltpu.VMEM((TILES_AT_ONCE * kernels * COARSE, 2 * COARSE), jnp.float32),
            pltpu.VMEM((TILES_AT_ONCE * kernels * COARSE, 2 * FB), jnp.float32),
            pltpu.VMEM((TILES_AT_ONCE * TILE, TILE), jnp.float32),
            pltpu.SemaphoreType.DMA((TILES_AT_ONCE,)),
        ],
        compiler_params=params(),
        name="imaging",
    )(share, from_even, from_odd, *own, *other, target, tables)


def inner_synthesis(own, even_in, odd_in, slope):
    tables = jnp.asarray(TABLES["synthesis"])
    vmem = pl.BlockSpec(memory_space=pltpu.VMEM)
    return pl.pallas_call(
        inner_kernel,
        out_shape=jax.ShapeDtypeStruct(slope.shape, jnp.float32),
        in_specs=[vmem] * 5,
        out_specs=pl.BlockSpec(memory_space=pl.ANY),
        scratch_shapes=[
            pltpu.VMEM((slope.shape[0] - 2 * TILE, TILE), jnp.float32),
            pltpu.SemaphoreType.DMA,
        ],
        compiler_params=pltpu.CompilerParams(vmem_limit_bytes=VMEM_LIMIT),
        cost_estimate=pl.CostEstimate(
            flops=1500000000, bytes_accessed=2500000, transcendentals=0
        ),
        name="inner_synthesis",
    )(own, even_in, odd_in, slope, tables)


def outer_synthesis(own, even_in, odd_in, near_even, near_odd, slope, partial):
    tables = jnp.asarray(TABLES["synthesis"])
    vmem = pl.BlockSpec(memory_space=pltpu.VMEM)
    return pl.pallas_call(
        outer_kernel,
        out_shape=jax.ShapeDtypeStruct(slope.shape, jnp.float32),
        in_specs=[vmem] * 7 + [pl.BlockSpec(memory_space=pl.ANY)],
        out_specs=pl.BlockSpec(memory_space=pl.ANY),
        input_output_aliases={7: 0},
        scratch_shapes=[
            pltpu.VMEM((2, TILE, TILE), jnp.float32),
            pltpu.SemaphoreType.DMA((2,)),
        ],
        compiler_params=pltpu.CompilerParams(vmem_limit_bytes=VMEM_LIMIT),
        name="outer_synthesis",
    )(own, even_in, odd_in, near_even, near_odd, slope, tables, partial)


def swap_pairs(count, first):
    pairs = []
    for place in range(first, count - 1, 2):
        pairs += [(place, place + 1), (place + 1, place)]
    return pairs


def local(mask_param, target, kernels, weights):
    rows = lax.axis_size("gy")

    def swap(value, axis, first):
        return lax.ppermute(value, axis, swap_pairs(lax.axis_size(axis), first))

    total, packed, half, edge_odd, slope = analysis(mask_param, kernels, weights)
    inner = rows // 4
    pairs = []
    for place in range(rows):
        mirror = (3 - place // inner) * inner + place % inner
        pairs += [(2 * place, 2 * mirror + 1), (2 * place + 1, 2 * mirror)]
    mine = lax.ppermute(half, ("gy", "ka"), pairs)
    halo_odd = swap(edge_odd, "gy", 1)
    *sums, edge_even = shares(total)
    halo_even = swap(edge_even, "gy", 0)
    share, to_even, to_odd = merge(*sums, halo_even, halo_odd)
    from_odd = swap(to_odd, "gx", 1)
    from_even = swap(to_even, "gx", 0)
    own = prepare_own(packed)
    partners = swap(mine, "gx", 0)
    other = prepare_other(mine, partners)
    resist, grad = imaging(share, from_even, from_odd, own, other, target)
    grad_odd = swap(grad, "gx", 1)
    grad_even = swap(grad, "gx", 0)
    side_odd = odd_edge(grad, grad_even, grad_odd)
    near_odd = swap(side_odd, "gy", 1)
    side_even = even_edge(grad, grad_even, grad_odd, side_odd)
    near_even = swap(side_even, "gy", 0)
    partial = inner_synthesis(grad, grad_even, grad_odd, slope)
    gradient = outer_synthesis(
        grad, grad_even, grad_odd, near_even, near_odd, slope, partial
    )
    return (gradient, resist)


def solution(mesh):
    placed = (P("gy", "gx"), P("gy", "gx"), P("ka", None, None), P("ka"))
    return jax.shard_map(
        local, mesh=mesh, in_specs=placed, out_specs=(P("gy", "gx"), P("gy", "gx")), check_vma=False
    )
```

```python
import math

import jax
import jax.numpy as jnp
import ml_dtypes
import numpy as np
from jax import lax
from jax.experimental import pallas as pl
from jax.experimental.pallas import tpu as pltpu
from jax.sharding import PartitionSpec as P

WIN = 512
HALO = 128
FB = 64
TILE = 256
COARSE = 128
HALF = COARSE // 2
VMEM_LIMIT = 40 * 1024 * 1024
PAIR = 3
TILES_AT_ONCE = 3
FIRST_LIMIT = 60 * 1024 * 1024

bf16 = ml_dtypes.bfloat16


def halves(table):
    high = table.astype(np.float32).astype(bf16)
    low = (table - high.astype(np.float64)).astype(np.float32).astype(bf16)
    return high, low


def as_left(table):
    high, low = halves(table)
    return np.concatenate([high, low, high], axis=1)


def as_right(table):
    high, low = halves(table)
    return np.concatenate([high, high, low], axis=0)


def angles(points):
    frequencies = np.arange(FB) - FB // 2
    windings = np.mod(frequencies[:, None] * np.asarray(points)[None, :], WIN)
    return windings * (2.0 * math.pi / WIN)


ORDER = np.concatenate([np.arange(0, FB, 2), np.arange(1, FB, 2)])


def blocks(table):
    return [table[:, i : i + 128] for i in range(0, table.shape[1], 128)]


def make_tables():
    factor = 1.0 / (WIN * FB)
    pixels = np.arange(HALO)
    columns, rows, outs, pixs = [], [], [], []
    for points in (pixels + 3 * HALO, pixels):
        cos, sin = np.cos(angles(points)), np.sin(angles(points))
        columns += halves(np.concatenate([cos.T, -sin.T], axis=1))
        pixs += halves(np.concatenate([cos, -sin], axis=0))
        cos, sin = cos[ORDER], sin[ORDER]
        rows += halves(factor * np.concatenate([cos, sin], axis=0))
        outs += halves(factor * np.concatenate([cos.T, sin.T], axis=1))
    plus = 4 * np.arange(HALF) + 2
    samples = np.concatenate([plus, -plus])
    cos, sin = np.cos(angles(samples)), np.sin(angles(samples))
    spread = as_right(
        np.concatenate(
            [np.concatenate([cos, sin], axis=1), np.concatenate([-sin, cos], axis=1)], axis=0
        )
    )
    gather = np.concatenate(
        [np.concatenate([cos.T, -sin.T], axis=1), np.concatenate([sin.T, cos.T], axis=1)], axis=0
    )
    gather = np.concatenate(halves(gather), axis=1)
    cos, sin = np.cos(angles(plus))[ORDER], np.sin(angles(plus))[ORDER]
    lift = as_left(np.concatenate([cos.T, sin.T], axis=0))
    lift = np.concatenate([lift, np.zeros((COARSE, 64), bf16)], axis=1)
    high, low = halves(np.concatenate([cos, sin], axis=1))
    fold = np.concatenate(
        [np.concatenate([high, high], axis=1), np.concatenate([low, 0 * low], axis=1)], axis=0
    )
    offset = (np.arange(TILE) + HALO)[:, None] - samples[None, :]
    orders = np.arange(1, COARSE // 2)
    turns = np.mod(offset[..., None] * orders, WIN) * (2.0 * math.pi / WIN)
    interp = (1.0 + 2.0 * np.cos(turns).sum(-1)) / COARSE
    high, low = halves(interp)
    fine_left = np.concatenate(
        [np.concatenate([high, high], axis=1), np.concatenate([low, 0 * low], axis=1)], axis=0
    )
    coarse_left = np.concatenate(halves(interp.T), axis=0)
    coarse_right = np.concatenate(halves(interp), axis=1)
    return {
        "analysis": np.concatenate(columns + rows, axis=0),
        "synthesis": np.concatenate(pixs + outs, axis=0),
        "imaging": np.concatenate(
            sum(
                map(
                    blocks,
                    (
                        spread, gather, lift, fold, as_right(interp.T), fine_left, coarse_left,
                        coarse_right,
                    ),
                ),
                [],
            ),
            axis=0,
        ),
    }


TABLES = make_tables()
SPREAD, GATHER, LIFT, FOLD, FINE_RIGHT, FINE_LEFT, COARSE_LEFT, COARSE_RIGHT = (
    (2 * a, b - a)
    for a, b in (
        (0, 384), (384, 640), (640, 768), (768, 896), (896, 1280), (1280, 1792), (1792, 2048),
        (2048, 2304),
    )
)


def split(value):
    high = value.astype(jnp.bfloat16)
    low = (value - high.astype(jnp.float32)).astype(jnp.bfloat16)
    return high, low


def dot(left, right):
    return jnp.dot(left, right, preferred_element_type=jnp.float32)


def times_table(value, table):
    high, low = split(value)
    return dot(jnp.concatenate([high, low, high], axis=1), table)


def table_times(table, value):
    high, low = split(value)
    return dot(table, jnp.concatenate([high, high, low], axis=0))


def stacked_times(table, value):
    high, low = split(value)
    found = dot(table, jnp.concatenate([high, low], axis=0))
    size = found.shape[0] // 2
    return found[:size] + found[size:]


def times_paired(value, table):
    high, low = split(value)
    width = table.shape[1] // 2
    first = dot(high, table)
    return first[:, :width] + (first[:, width:] + dot(low, table[:, :width]))


def square(packed, index):
    return packed[index * 128 : (index + 1) * 128, :]


def times_sides(value, packed):
    high, low = split(value)
    found = []
    for side in (0, 1):
        lanes = slice(side * 128, (side + 1) * 128)
        first, second = square(packed, 2 * side), square(packed, 2 * side + 1)
        found.append(
            dot(
                jnp.concatenate([high[:, lanes], low[:, lanes], high[:, lanes]], axis=1),
                jnp.concatenate([first, first, second], axis=0),
            )
        )
    return jnp.concatenate(found, axis=1)


def times_diagonal(value, packed):
    zeros = jnp.zeros((128, 128), jnp.bfloat16)
    high_table, low_table = (
        jnp.concatenate(
            [
                jnp.concatenate([square(packed, i), zeros], axis=1),
                jnp.concatenate([zeros, square(packed, i + 2)], axis=1),
            ],
            axis=0,
        )
        for i in (0, 1)
    )
    high, low = split(value)
    return dot(
        jnp.concatenate([high, low, high], axis=1),
        jnp.concatenate([high_table, high_table, low_table], axis=0),
    )


def stacked_table(packed, part):
    high, low = square(packed, 4 + 2 * part), square(packed, 5 + 2 * part)
    return jnp.concatenate(
        [
            jnp.concatenate([high, high], axis=1),
            jnp.concatenate([low, jnp.zeros_like(low)], axis=1),
        ],
        axis=0,
    )


def wide_table(packed, place):
    start, size = place
    return jnp.concatenate(
        [packed[start : start + size, :], packed[start + size : start + 2 * size, :]], axis=1
    )


def parity(shape):
    index = lax.broadcasted_iota(jnp.int32, shape, 1)
    return (1 - 2 * (index % 2)).astype(jnp.float32)


def is_odd(axis):
    return lax.axis_index(axis) % 2 == 1


def row_parity(shape):
    index = lax.broadcasted_iota(jnp.int32, shape, 0)
    return jnp.where(index < FB // 2, 1.0, -1.0)


def low_lanes(shape):
    return lax.broadcasted_iota(jnp.int32, shape, 1) < FB


def swapped(value):
    return pltpu.roll(value, FB, 1)


def factors(spectrum):
    lanes = low_lanes((FB, 2 * FB))
    turned = swapped(spectrum)
    return jnp.where(lanes, spectrum, turned), jnp.where(lanes, -turned, spectrum)


def own_kernel(own, straight, crossed):
    for index in range(own.shape[0]):
        straight[index], crossed[index] = factors(own[index])


def other_kernel(mine, partners, straight, crossed):
    odd_col = is_odd("gx")
    half = mine.shape[0]
    for index in range(half):
        first = jnp.where(odd_col, partners[index], mine[index])
        second = jnp.where(odd_col, mine[index], partners[index])
        straight[index], crossed[index] = factors(first)
        straight[half + index], crossed[half + index] = factors(second)


def pack_kernels(kernels, weights, packed, real, imag):
    lanes = low_lanes((FB // 2, 2 * FB))
    for index in range(kernels.shape[0]):
        for row in range(FB // 2):
            place = slice(row * 2 * FB, (row + 1) * 2 * FB)
            real[row : row + 1, :] = kernels[index, 0:1, place]
            imag[row : row + 1, :] = kernels[index, 1:2, place]
        root = jnp.sqrt(jnp.full((FB // 2, 2 * FB), weights[index], jnp.float32))
        re, im = root * real[...], root * imag[...]
        packed[index, : FB // 2] = jnp.where(lanes, re, swapped(im))
        packed[index, FB // 2 :] = jnp.where(lanes, swapped(re), im)


def block_spectra(transmit, tables):
    sign = jnp.where(low_lanes((FB, 2 * FB)), 1.0, -1.0)
    rows = times_sides(transmit, tables)
    found = []
    for block in range(transmit.shape[0] // HALO):
        first = square(tables, 4 + 2 * (block % 2))
        second = square(tables, 5 + 2 * (block % 2))
        both = table_times(
            jnp.concatenate([first, second, first], axis=1),
            rows[block * HALO : (block + 1) * HALO],
        )
        sine = both[FB:]
        turned = [sign * swapped(sine[:, : 2 * FB]), sign * swapped(sine[:, 2 * FB :])]
        found.append(both[:FB] + jnp.concatenate(turned, axis=1))
    return found


def analysis_kernel(
    mask_in, kernels_in, weights, tables_in,
    total, packed, half, edge_odd, slope,
    real, imag, sums, mask, kernels, tables, semaphores,
):
    step = pl.program_id(0)
    count = total.shape[0] - 2

    def pixels_copy(step):
        place = pl.ds(pl.multiple_of(step * PAIR * TILE, TILE), PAIR * TILE)
        return pltpu.make_async_copy(
            mask_in.at[place, :], mask.at[place, :], semaphores.at[step]
        )

    @pl.when(step == 0)
    def _():
        table_copy = pltpu.make_async_copy(tables_in, tables, semaphores.at[count // PAIR])
        kernel_copy = pltpu.make_async_copy(
            kernels_in, kernels, semaphores.at[count // PAIR + 1]
        )
        kernel_copy.start()
        pixels_copy(0).start()
        table_copy.start()
        for later in range(1, count // PAIR):
            pixels_copy(later).start()
        sums[...] = jnp.zeros_like(sums)
        kernel_copy.wait()
        pack_kernels(kernels, weights, packed, real, imag)
        size = half.shape[0]
        for index in range(size):
            half[index] = jnp.where(is_odd("gx"), packed[size + index], packed[index])
        table_copy.wait()

    pixels_copy(step).wait()
    transmit = jnp.tanh(mask[pl.ds(pl.multiple_of(step * PAIR * TILE, TILE), PAIR * TILE), :])
    slope[...] = 1.0 - transmit * transmit
    found = block_spectra(transmit, tables)
    flip = row_parity((FB, 4 * FB))
    first = step * PAIR
    for tile in range(PAIR):
        upper, lower = found[2 * tile], found[2 * tile + 1]
        sums[first + tile] += upper
        sums[first + tile + 1] += flip * (upper + lower)
        sums[first + tile + 2] += lower

    @pl.when(step == pl.num_programs(0) - 1)
    def _():
        total[...] = sums[...]
        edge_odd[...] = jnp.where(is_odd("gy"), sums[count + 1], sums[0])


def shares_kernel(total, share, to_even, to_odd, edge):
    odd_col = is_odd("gx")
    edge[...] = jnp.where(is_odd("gy"), total[0], total[share.shape[0] + 1])
    for index in range(share.shape[0]):
        left, right = total[index + 1, :, : 2 * FB], total[index + 1, :, 2 * FB :]
        share[index] = parity((FB, 2 * FB)) * (left + right)
        to_even[index] = jnp.where(odd_col, left, right)
        to_odd[index] = jnp.where(odd_col, right, left)


def merge_kernel(
    share_in, to_even_in, to_odd_in, near_even, near_odd, share, to_even, to_odd
):
    count = share.shape[0]
    odd_row, odd_col = is_odd("gy"), is_odd("gx")
    share[...] = share_in[...]
    to_even[...] = to_even_in[...]
    to_odd[...] = to_odd_in[...]
    above = jnp.where(odd_row, near_even[...], near_odd[...])
    below = jnp.where(odd_row, near_odd[...], near_even[...])
    for index, near in ((0, above), (count - 1, below)):
        left, right = near[:, : 2 * FB], near[:, 2 * FB :]
        share[index] += parity((FB, 2 * FB)) * (left + right)
        to_even[index] += jnp.where(odd_col, left, right)
        to_odd[index] += jnp.where(odd_col, right, left)


def imaging_kernel(
    share, from_even, from_odd, straight_own, crossed_own, straight_other, crossed_other,
    target, wide, resist_out, grad, fields, sides, resists, semaphores,
):
    count = straight_own.shape[0]
    straights, crosseds = (straight_own, straight_other), (crossed_own, crossed_other)
    copies = []
    sign = jnp.where(low_lanes((HALF, 2 * FB)), 1.0, -1.0)
    tiles = range(share.shape[0])
    intensities = [[] for tile in tiles]

    spectra = [share[tile] + from_even[tile] + from_odd[tile] for tile in tiles]
    turned = [swapped(spectrum) for spectrum in spectra]
    for group in range(2):
        products = [
            straights[group][i] * spectra[tile] + crosseds[group][i] * turned[tile]
            for tile in tiles
            for i in range(count)
        ]
        halves_of = []
        for i in range(0, len(products), 2):
            both = table_times(
                wide_table(wide, LIFT)[:, :192], jnp.concatenate(products[i : i + 2], axis=1)
            )
            for j in (0, 1):
                part = both[:, j * 2 * FB : (j + 1) * 2 * FB]
                cosine, sine = part[:HALF], sign * swapped(part[HALF:])
                halves_of += [cosine - sine, cosine + sine]
        powers = []
        for first in range(0, len(halves_of), len(halves_of) // 2):
            chunk = halves_of[first : first + len(halves_of) // 2]
            found = times_table(jnp.concatenate(chunk, axis=0), wide_table(wide, SPREAD))
            place = first * HALF
            fields[group, place : place + found.shape[0], :] = found
            for start in range(0, found.shape[0], COARSE):
                real = found[start : start + COARSE, :COARSE]
                imag = found[start : start + COARSE, COARSE:]
                powers.append(real * real + imag * imag)
        for tile in tiles:
            total = powers[tile * count]
            for power in powers[tile * count + 1 : (tile + 1) * count]:
                total = total + power
            intensities[tile].append(total)

    half_fine = times_table(
        jnp.concatenate([first + second for first, second in intensities], axis=0),
        wide_table(wide, FINE_RIGHT),
    )
    half_coarse = []
    for tile in tiles:
        fine = stacked_times(
            wide_table(wide, FINE_LEFT), half_fine[tile * COARSE : (tile + 1) * COARSE]
        )
        resist = jax.nn.sigmoid(4.0 * (fine - 1.0))
        place = slice(tile * TILE, (tile + 1) * TILE)
        resists[place, :] = resist
        start = (pl.program_id(0) * len(tiles) + tile) * TILE
        copy = pltpu.make_async_copy(
            resists.at[pl.ds(tile * TILE, TILE), :],
            resist_out.at[pl.ds(pl.multiple_of(start, TILE), TILE), :],
            semaphores.at[tile],
        )
        copy.start()
        copies.append(copy)
        misfit = resist - target[place, :].astype(jnp.float32)
        push = 16.0 * misfit * resist * (1.0 - resist)
        high, low = split(push)
        from_high = dot(wide_table(wide, COARSE_LEFT), high)
        half_coarse.append(
            from_high[:COARSE]
            + (from_high[COARSE:] + dot(wide_table(wide, COARSE_LEFT)[:COARSE], low))
        )
    weights = times_paired(jnp.concatenate(half_coarse, axis=0), wide_table(wide, COARSE_RIGHT))
    scales = [
        jnp.concatenate([weights[tile * COARSE : (tile + 1) * COARSE]] * 2, axis=1)
        for tile in tiles
    ]

    adjoint = [[] for tile in tiles]
    for group in range(2):
        scaled = [
            fields[group, (tile * count + i) * COARSE : (tile * count + i + 1) * COARSE, :]
            * scales[tile]
            for tile in tiles
            for i in range(count)
        ]
        sides[group] = times_paired(
            jnp.concatenate(scaled, axis=0), wide_table(wide, GATHER)
        )
        for tile in tiles:
            total = jnp.zeros((FB, 2 * FB), jnp.float32)
            for i in range(0, count, 2):
                pair = []
                for j in (i, i + 1):
                    place = (tile * count + j) * COARSE
                    plus = sides[group, place : place + HALF, :]
                    minus = sides[group, place + HALF : place + COARSE, :]
                    pair.append(
                        jnp.concatenate([plus + minus, sign * swapped(plus - minus)], axis=0)
                    )
                found = stacked_times(
                    wide_table(wide, FOLD), jnp.concatenate(pair, axis=1)
                )
                for j in (0, 1):
                    part = found[:, j * 2 * FB : (j + 1) * 2 * FB]
                    total = total + (
                        straights[group][i + j] * part - crosseds[group][i + j] * swapped(part)
                    )
            adjoint[tile].append(total)
    for tile in tiles:
        grad[tile] = adjoint[tile][0] + adjoint[tile][1]

    for copy in copies:
        copy.wait()


def sides_of(even_in, odd_in, index):
    odd_col = is_odd("gx")
    return (
        jnp.where(odd_col, even_in[index], odd_in[index]),
        jnp.where(odd_col, odd_in[index], even_in[index]),
    )


def synthesis_rows(rows, slope, tables):
    sign = jnp.where(low_lanes((FB, 2 * FB)), -1.0, 1.0)
    flip = row_parity((FB, 4 * FB))
    outer = []
    for index in range(1, len(rows) - 1):
        base = flip * rows[index]
        for part, near in enumerate((rows[index - 1], rows[index + 1])):
            block = base + near
            turned = [sign * swapped(block[:, : 2 * FB]), sign * swapped(block[:, 2 * FB :])]
            stacked = jnp.concatenate([block, jnp.concatenate(turned, axis=1)], axis=0)
            outer.append(stacked_times(stacked_table(tables, part), stacked))
    return times_diagonal(jnp.concatenate(outer, axis=0), tables) * slope


def mixed_row(own, even_in, odd_in, index):
    base = parity((FB, 2 * FB)) * own[index]
    from_left, from_right = sides_of(even_in, odd_in, index)
    return jnp.concatenate([base + from_left, base + from_right], axis=1)


def edges_kernel(own, even_in, odd_in, side_even, side_odd):
    first = mixed_row(own, even_in, odd_in, 0)
    last = mixed_row(own, even_in, odd_in, own.shape[0] - 1)
    odd_row = is_odd("gy")
    side_even[...] = jnp.where(odd_row, first, last)
    side_odd[...] = jnp.where(odd_row, last, first)


def write_rows(values, result, first, buffer, semaphore):
    buffer[...] = values
    copy = pltpu.make_async_copy(
        buffer, result.at[pl.ds(first, values.shape[0]), :], semaphore
    )
    copy.start()
    return copy


def inner_kernel(own, even_in, odd_in, slope, tables, result, buffer, semaphore):
    count = own.shape[0]
    rows = [mixed_row(own, even_in, odd_in, i) for i in range(count)]
    values = synthesis_rows(rows, slope[TILE : (count - 1) * TILE, :], tables)
    write_rows(values, result, TILE, buffer, semaphore).wait()


def outer_kernel(
    own, even_in, odd_in, near_even, near_odd, slope, tables, partial, result, buffers,
    semaphores,
):
    del partial
    count = own.shape[0]
    odd_row = is_odd("gy")
    above = jnp.where(odd_row, near_even[...], near_odd[...])
    below = jnp.where(odd_row, near_odd[...], near_even[...])
    rows = [mixed_row(own, even_in, odd_in, i) for i in (0, 1, count - 2, count - 1)]
    last = (count - 1) * TILE
    copies = []
    for index, first, near in ((0, 0, [above] + rows[:2]), (1, last, rows[2:] + [below])):
        values = synthesis_rows(near, slope[first : first + TILE, :], tables)
        copies.append(
            write_rows(values, result, first, buffers.at[index], semaphores.at[index])
        )
    for copy in copies:
        copy.wait()


def whole(array):
    zeros = (0,) * len(array.shape)
    return pl.BlockSpec(array.shape, lambda step: zeros)


def tile_pair():
    return pl.BlockSpec((PAIR * TILE, TILE), lambda step: (step, 0))


def params(limit=VMEM_LIMIT):
    return pltpu.CompilerParams(dimension_semantics=("arbitrary",), vmem_limit_bytes=limit)


def analysis(mask, kernels, weights):
    tiles = mask.shape[0] // TILE
    tables = jnp.asarray(TABLES["analysis"])
    part = pltpu.VMEM((FB // 2, 2 * FB), jnp.float32)
    total = jax.ShapeDtypeStruct((tiles + 2, FB, 4 * FB), jnp.float32)
    packed = jax.ShapeDtypeStruct((kernels.shape[0], FB, 2 * FB), jnp.float32)
    half = jax.ShapeDtypeStruct((kernels.shape[0] // 2, FB, 2 * FB), jnp.float32)
    edge = jax.ShapeDtypeStruct((FB, 4 * FB), jnp.float32)
    return pl.pallas_call(
        analysis_kernel,
        grid=(tiles // PAIR,),
        out_shape=(
            total, packed, half, edge, jax.ShapeDtypeStruct(mask.shape, jnp.float32)
        ),
        in_specs=[
            pl.BlockSpec(memory_space=pltpu.HBM),
            pl.BlockSpec(memory_space=pltpu.HBM),
            pl.BlockSpec(memory_space=pltpu.SMEM),
            pl.BlockSpec(memory_space=pltpu.HBM),
        ],
        out_specs=[whole(out) for out in (total, packed, half, edge)] + [tile_pair()],
        scratch_shapes=[
            part,
            part,
            pltpu.VMEM((tiles + 2, FB, 4 * FB), jnp.float32),
            pltpu.VMEM(mask.shape, mask.dtype),
            pltpu.VMEM(kernels.shape, kernels.dtype),
            pltpu.VMEM(tables.shape, tables.dtype),
            pltpu.SemaphoreType.DMA((tiles // PAIR + 2,)),
        ],
        compiler_params=params(FIRST_LIMIT),
        name="analysis",
    )(mask, kernels, weights, tables)


def simple_call(kernel, out_shape, *operands, name):
    vmem = pl.BlockSpec(memory_space=pltpu.VMEM)
    return pl.pallas_call(
        kernel,
        out_shape=out_shape,
        in_specs=[vmem] * len(operands),
        out_specs=[vmem] * len(out_shape),
        compiler_params=pltpu.CompilerParams(vmem_limit_bytes=VMEM_LIMIT),
        name=name,
    )(*operands)


def shares(total):
    spectra = jax.ShapeDtypeStruct((total.shape[0] - 2, FB, 2 * FB), jnp.float32)
    side = jax.ShapeDtypeStruct((FB, 4 * FB), jnp.float32)
    return simple_call(shares_kernel, (spectra,) * 3 + (side,), total, name="shares")


def merge(share, to_even, to_odd, near_even, near_odd):
    spectra = jax.ShapeDtypeStruct(share.shape, jnp.float32)
    return simple_call(
        merge_kernel, (spectra,) * 3, share, to_even, to_odd, near_even, near_odd, name="merge"
    )


def edges(grad, grad_even, grad_odd):
    side = jax.ShapeDtypeStruct((FB, 4 * FB), jnp.float32)
    return simple_call(edges_kernel, (side,) * 2, grad, grad_even, grad_odd, name="edges")


def prepare_own(own):
    shape = jax.ShapeDtypeStruct(own.shape, jnp.float32)
    return simple_call(own_kernel, (shape, shape), own, name="prepare_own")


def prepare_other(mine, partners):
    shape = jax.ShapeDtypeStruct((2 * mine.shape[0],) + mine.shape[1:], jnp.float32)
    return simple_call(other_kernel, (shape, shape), mine, partners, name="prepare_other")


def imaging(share, from_even, from_odd, own, other, target):
    tiles = share.shape[0]
    kernels = 2 * own[0].shape[0]
    tables = jnp.asarray(TABLES["imaging"])
    spectra = pl.BlockSpec((TILES_AT_ONCE, FB, 2 * FB), lambda step: (step, 0, 0))
    pixels = pl.BlockSpec((TILES_AT_ONCE * TILE, TILE), lambda step: (step, 0))
    return pl.pallas_call(
        imaging_kernel,
        grid=(tiles // TILES_AT_ONCE,),
        out_shape=(
            jax.ShapeDtypeStruct(target.shape, jnp.float32),
            jax.ShapeDtypeStruct(share.shape, jnp.float32),
        ),
        in_specs=[spectra] * 3 + [whole(own[0])] * 4 + [pixels, whole(tables)],
        out_specs=[pl.BlockSpec(memory_space=pl.ANY), spectra],
        scratch_shapes=[
            pltpu.VMEM((2, TILES_AT_ONCE * kernels // 2 * COARSE, 2 * COARSE), jnp.float32),
            pltpu.VMEM((2, TILES_AT_ONCE * kernels // 2 * COARSE, 2 * FB), jnp.float32),
            pltpu.VMEM((TILES_AT_ONCE * TILE, TILE), jnp.float32),
            pltpu.SemaphoreType.DMA((TILES_AT_ONCE,)),
        ],
        compiler_params=params(),
        name="imaging",
    )(share, from_even, from_odd, *own, *other, target, tables)


def inner_synthesis(own, even_in, odd_in, slope):
    tables = jnp.asarray(TABLES["synthesis"])
    vmem = pl.BlockSpec(memory_space=pltpu.VMEM)
    return pl.pallas_call(
        inner_kernel,
        out_shape=jax.ShapeDtypeStruct(slope.shape, jnp.float32),
        in_specs=[vmem] * 5,
        out_specs=pl.BlockSpec(memory_space=pl.ANY),
        scratch_shapes=[
            pltpu.VMEM((slope.shape[0] - 2 * TILE, TILE), jnp.float32),
            pltpu.SemaphoreType.DMA,
        ],
        compiler_params=pltpu.CompilerParams(vmem_limit_bytes=VMEM_LIMIT),
        cost_estimate=pl.CostEstimate(
            flops=1500000000, bytes_accessed=2500000, transcendentals=0
        ),
        name="inner_synthesis",
    )(own, even_in, odd_in, slope, tables)


def outer_synthesis(own, even_in, odd_in, near_even, near_odd, slope, partial):
    tables = jnp.asarray(TABLES["synthesis"])
    vmem = pl.BlockSpec(memory_space=pltpu.VMEM)
    return pl.pallas_call(
        outer_kernel,
        out_shape=jax.ShapeDtypeStruct(slope.shape, jnp.float32),
        in_specs=[vmem] * 7 + [pl.BlockSpec(memory_space=pl.ANY)],
        out_specs=pl.BlockSpec(memory_space=pl.ANY),
        input_output_aliases={7: 0},
        scratch_shapes=[
            pltpu.VMEM((2, TILE, TILE), jnp.float32),
            pltpu.SemaphoreType.DMA((2,)),
        ],
        compiler_params=pltpu.CompilerParams(vmem_limit_bytes=VMEM_LIMIT),
        name="outer_synthesis",
    )(own, even_in, odd_in, near_even, near_odd, slope, tables, partial)


def swap_pairs(count, first):
    pairs = []
    for place in range(first, count - 1, 2):
        pairs += [(place, place + 1), (place + 1, place)]
    return pairs


def local(mask_param, target, kernels, weights):
    rows = lax.axis_size("gy")

    def swap(value, axis, first):
        return lax.ppermute(value, axis, swap_pairs(lax.axis_size(axis), first))

    total, packed, half, edge_odd, slope = analysis(mask_param, kernels, weights)
    inner = rows // 4
    pairs = []
    for place in range(rows):
        mirror = (3 - place // inner) * inner + place % inner
        pairs += [(2 * place, 2 * mirror + 1), (2 * place + 1, 2 * mirror)]
    mine = lax.ppermute(half, ("gy", "ka"), pairs)
    halo_odd = swap(edge_odd, "gy", 1)
    *sums, edge_even = shares(total)
    halo_even = swap(edge_even, "gy", 0)
    share, to_even, to_odd = merge(*sums, halo_even, halo_odd)
    from_odd = swap(to_odd, "gx", 1)
    from_even = swap(to_even, "gx", 0)
    own = prepare_own(packed)
    partners = swap(mine, "gx", 0)
    other = prepare_other(mine, partners)
    resist, grad = imaging(share, from_even, from_odd, own, other, target)
    grad_odd = swap(grad, "gx", 1)
    grad_even = swap(grad, "gx", 0)
    side_even, side_odd = edges(grad, grad_even, grad_odd)
    near_odd = swap(side_odd, "gy", 1)
    near_even = swap(side_even, "gy", 0)
    partial = inner_synthesis(grad, grad_even, grad_odd, slope)
    gradient = outer_synthesis(
        grad, grad_even, grad_odd, near_even, near_odd, slope, partial
    )
    return (gradient, resist)


def solution(mesh):
    placed = (P("gy", "gx"), P("gy", "gx"), P("ka", None, None), P("ka"))
    return jax.shard_map(
        local, mesh=mesh, in_specs=placed, out_specs=(P("gy", "gx"), P("gy", "gx")), check_vma=False
    )
```
